32 devices in a mesh: fsdp: 8 (over y, x, core), seq: 4 (over z).
Axes of the slice: x: 2, y: 2, z: 4, core: 2. Of those that a mesh axis runs over, the one named last changes fastest.
Arguments:
- tokens: bfloat16 [8, 1568, 768], P('fsdp', 'seq'), may hold values from -80 to 80
- norm_gain: bfloat16 [3, 768], P(None, 'fsdp'), may hold values from 0.5 to 1.5
- norm_bias: bfloat16 [3, 768], P(None, 'fsdp'), may hold values from -3 to 3
- attn_qkv: bfloat16 [2, 768, 2304], P(None, 'fsdp'), may hold values from -0.21875 to 0.21875
- attn_qv_bias: bfloat16 [2, 1536], P(None, 'fsdp'), may hold values from -3 to 3
- attn_out: bfloat16 [2, 768, 768], P(None, 'fsdp'), may hold values from -0.875 to 0.875
- attn_out_bias: bfloat16 [2, 768], P(None, 'fsdp'), may hold values from -2 to 2
- mlp_in: bfloat16 [768, 3072], P('fsdp'), may hold values from -0.21875 to 0.21875
- mlp_in_bias: bfloat16 [3072], P('fsdp'), may hold values from -3 to 3
- mlp_out: bfloat16 [3072, 768], P('fsdp'), may hold values from -0.15625 to 0.15625
- mlp_out_bias: bfloat16 [768], P('fsdp'), may hold values from -2 to 2
- threshold: float32 [2, 12], replicated, may hold values from 0.5 to 4
- cotangent: bfloat16 [8, 1568, 768], P('fsdp', 'seq'), may hold values from -6 to 6
Outputs:
- mixed: bfloat16 [8, 1568, 768], P('fsdp', 'seq')
- grad_tokens: float32 [8, 1568, 768], P('fsdp', 'seq')
- grad_norm_gain: float32 [3, 768], P(None, 'fsdp')
- grad_norm_bias: float32 [3, 768], P(None, 'fsdp')
- grad_attn_qkv: float32 [2, 768, 2304], P(None, 'fsdp')
- grad_attn_qv_bias: float32 [2, 1536], P(None, 'fsdp')
- grad_attn_out: float32 [2, 768, 768], P(None, 'fsdp')
- grad_attn_out_bias: float32 [2, 768], P(None, 'fsdp')
- grad_mlp_in: float32 [768, 3072], P('fsdp')
- grad_mlp_in_bias: float32 [3072], P('fsdp')
- grad_mlp_out: float32 [3072, 768], P('fsdp')
- grad_mlp_out_bias: float32 [768], P('fsdp')
- logit_max: float32 [2, 12], replicated
- clipped_qk: float32 [2, 768, 1536], P(None, 'fsdp')
The draws below stay inside these ranges and needn't reach their ends.
All inputs are finite; a program needn't handle non-finite values.
Results may differ from the reference program's by a relative error of at most 0.02.
Values may be sent and summed in bfloat16 or wider, within the bound.
No kernel may reach another device: no remote copies, remote signals or barrier semaphores. Data moves between devices by JAX's collectives and lax.ppermute only.
A program may use at most 256 MiB of HBM per device.

```python
import math
import jax
import jax.numpy as jnp
from jax import lax

D = 768
H = 12
FF = 3072
FRAMES = 8
PATCHES = 196
HD = 64
CLIP_LEN = 1568
CLIPS = 8


def draw_tokens(key, part):
    key = jax.random.fold_in(key, 11)
    key_list = jax.random.split(key, 3)
    row_scale = jnp.exp(jax.random.uniform(key_list[0], (CLIPS, CLIP_LEN, 1), jnp.float32, math.log(0.4), math.log(4.0)))
    column_scale = jnp.exp(jax.random.uniform(key_list[1], (1, 1, D), jnp.float32, math.log(0.4), math.log(4.0)))
    base_draw = jax.random.truncated_normal(key_list[2], -4.0, 4.0, (CLIPS, CLIP_LEN, D), jnp.float32)
    return (base_draw * row_scale * column_scale).astype(jnp.bfloat16)


def spiked(result, stream_key, source, target, blocks, factor):
    owner, partner = [(jnp.arange(result.shape[axis_at]) // (result.shape[axis_at] // blocks)).reshape([-1 if axis == axis_at else 1 for axis in range(result.ndim)]) for axis_at in (source, target)]
    chosen = jax.random.permutation(stream_key, blocks)[partner]
    strong = (owner == chosen) | (owner == (partner + blocks // 2) % blocks)
    return jnp.where(strong, factor * result, result)


def levels(own_key, dims, cuts, smallest, largest):
    factor_of = 1.0
    for dim, parts in cuts:
        heights = jax.random.uniform(jax.random.fold_in(jax.random.fold_in(own_key, 6), dim), (parts,), jnp.float32, smallest / len(cuts), largest / len(cuts))
        factor_of = factor_of * jnp.repeat(jnp.exp(heights), dims[dim] // parts).reshape((-1,) + (1,) * (len(dims) - 1 - dim))
    return factor_of


def gaussian(own_key, dims, width, bound, cuts=(), kind=jnp.bfloat16):
    values = jax.random.normal(own_key, dims, jnp.float32) * width
    if len(cuts) > 0:
        values = levels(own_key, dims, cuts, -0.22, 0.18) * values
    return jnp.clip(values, min=-bound, max=bound).astype(kind)


def heavy_noise(own_key, extent, width, most, shards, heavy, dtype=jnp.bfloat16):
    values = width * jax.random.normal(own_key, extent, jnp.float32)
    if shards:
        values = values * levels(own_key, extent, shards, -0.22, 0.18)
    return jnp.clip(spiked(values, jax.random.fold_in(own_key, 3), *heavy), -most, most).astype(dtype)


def setup_inputs(seed: int = 0) -> dict:
    key_of = jax.random.split(jax.random.key(seed), 14)
    return {
        "tokens": draw_tokens(jax.random.fold_in(key_of[13], 71), 0),
        "norm_gain": jnp.clip(1.0 + 0.1 * jax.random.normal(key_of[1], (3, D), jnp.float32), 0.5, 1.5).astype(jnp.bfloat16),
        "norm_bias": gaussian(key_of[2], (3, D), 0.5, 3.0, ((1, 8),)),
        "attn_qkv": gaussian(key_of[3], (2, D, 3 * D), D ** -0.5, 0.21875, ((1, 8),)),
        "attn_qv_bias": gaussian(key_of[4], (2, 2 * D), 0.5, 3.0, ((1, 8),)),
        "attn_out": gaussian(key_of[5], (2, D, D), (D // 16) ** -0.5, 0.875, ((1, 8),)),
        "attn_out_bias": gaussian(key_of[6], (2, D), 0.3, 2.0, ((1, 8),)),
        "mlp_in": gaussian(key_of[7], (D, FF), D ** -0.5, 0.21875, ((0, 8),)),
        "mlp_in_bias": gaussian(key_of[8], (FF,), 0.5, 3.0, ((0, 8),)),
        "mlp_out": gaussian(key_of[9], (FF, D), (FF // 2) ** -0.5, 0.15625, ((0, 8),)),
        "mlp_out_bias": gaussian(key_of[10], (D,), 0.3, 2.0, ((0, 8),)),
        "threshold": jnp.clip(jnp.exp(jax.random.uniform(key_of[11], (2, H), jnp.float32, math.log(0.5), math.log(4.0))), 0.5, 4.0),
        "cotangent": heavy_noise(key_of[12], (CLIPS, CLIP_LEN, D), 1.0, 6.0, ((0, 8), (1, 4)), (0, 2, 8, 2.0)),
    }


EPSILON = 1e-06
NEGATIVE = -1e+30

@jax.custom_vjp
def low(v):
    return lax.optimization_barrier(v.astype(jnp.bfloat16)).astype(jnp.float32)

@jax.custom_vjp
def low_back(v):
    return v

def low_keep(v):
    return (low(v), None)

def low_pass(kept, grad):
    return (grad,)

def back_keep(v):
    return (v, None)

def back_low(kept, grad):
    return (low(grad),)
low.defvjp(low_keep, low_pass)
low_back.defvjp(back_keep, back_low)

def highest(left_side, right_side):
    return jnp.dot(left_side, right_side, precision=lax.Precision.HIGHEST)

def layer_norm(rows_in, gain_row, shift_row):
    centre = lax.optimization_barrier(jnp.mean(rows_in, axis=-1, keepdims=True))
    centred = rows_in - centre
    second = lax.optimization_barrier(jnp.mean(centred * centred, axis=-1, keepdims=True))
    return centred * lax.rsqrt(second + EPSILON) * gain_row + shift_row

def grouped(section, temporal):
    shaped = section.reshape(FRAMES, PATCHES, H, HD)
    if temporal:
        shaped = jnp.swapaxes(shaped, 0, 1)
    return shaped

def ungrouped(blocks, temporal):
    if temporal:
        blocks = jnp.swapaxes(blocks, 0, 1)
    return blocks.reshape(FRAMES * PATCHES, D)

def attention_branch(rows_in, gain_row, shift_row, qkv_weight, qv_shift, out_weight, out_shift, temporal):
    normed = low(layer_norm(rows_in, gain_row, shift_row))
    shift_full = jnp.concatenate([qv_shift[:D], jnp.zeros((D,), jnp.float32), qv_shift[D:]])
    projected = low(low_back(highest(normed, qkv_weight) + shift_full))
    queries = grouped(projected[:, :D], temporal)
    key_heads = grouped(projected[:, D:2 * D], temporal)
    value_heads = grouped(projected[:, 2 * D:], temporal)
    scores = low_back(jnp.einsum('gqhd,gkhd->ghqk', queries, key_heads, precision=lax.Precision.HIGHEST) * HD ** (-0.5))
    peak_heads = lax.optimization_barrier(jnp.max(scores, axis=(0, 2, 3)))
    weights_soft = low(jax.nn.softmax(scores, axis=-1))
    context = jnp.einsum('ghqk,gkhd->gqhd', weights_soft, value_heads, precision=lax.Precision.HIGHEST)
    context = low(low_back(ungrouped(context, temporal)))
    return (low_back(highest(context, out_weight) + out_shift), peak_heads)

def forward(rows_in, gain_rows, shift_rows, qkv_weights, qv_shifts, out_weights, out_shifts, in_weight, in_shift, back_weight, back_shift):
    spatial, peak_space = attention_branch(rows_in, gain_rows[0], shift_rows[0], qkv_weights[0], qv_shifts[0], out_weights[0], out_shifts[0], False)
    rows_one = rows_in + spatial
    temporal_out, peak_time = attention_branch(rows_one, gain_rows[1], shift_rows[1], qkv_weights[1], qv_shifts[1], out_weights[1], out_shifts[1], True)
    rows_two = rows_one + temporal_out
    normed = low(layer_norm(rows_two, gain_rows[2], shift_rows[2]))
    hidden = low_back(highest(normed, in_weight) + in_shift)
    active = low(jax.nn.gelu(hidden, approximate=False))
    rows_out = rows_two + low_back(highest(active, back_weight) + back_shift)
    return (rows_out, jnp.stack([peak_space, peak_time]))

def reference(tokens, norm_gain, norm_bias, attn_qkv, attn_qv_bias, attn_out, attn_out_bias, mlp_in, mlp_in_bias, mlp_out, mlp_out_bias, threshold, cotangent):
    params = (norm_gain.astype(jnp.float32), norm_bias.astype(jnp.float32), attn_qkv.astype(jnp.float32), attn_qv_bias.astype(jnp.float32), attn_out.astype(jnp.float32), attn_out_bias.astype(jnp.float32), mlp_in.astype(jnp.float32), mlp_in_bias.astype(jnp.float32), mlp_out.astype(jnp.float32), mlp_out_bias.astype(jnp.float32))

    def one_clip(state_pair, clip_pair):
        grad_sums, peak_run = state_pair
        clip_rows, clip_cot = clip_pair
        outcome, pullback, clip_peaks = jax.vjp(forward, clip_rows.astype(jnp.float32), *params, has_aux=True)
        pulled = pullback(clip_cot.astype(jnp.float32))
        grad_sums = tuple((running + portion for running, portion in zip(grad_sums, pulled[1:])))
        return ((grad_sums, jnp.maximum(peak_run, clip_peaks)), (outcome.astype(jnp.bfloat16), pulled[0]))
    zero_sums = tuple((jnp.zeros_like(weight_item) for weight_item in params))
    start_peak = jnp.full((2, H), NEGATIVE, jnp.float32)
    (grad_sums, logit_max), (mixed, grad_tokens) = lax.scan(one_clip, (zero_sums, start_peak), (tokens, cotangent))
    factor = threshold / jnp.maximum(logit_max, threshold)
    column_scale = jnp.repeat(jnp.sqrt(factor), HD, axis=1)
    qkv_values = params[2]
    clipped_qk = jnp.concatenate([qkv_values[:, :, :D] * column_scale[:, None, :], qkv_values[:, :, D:2 * D] * column_scale[:, None, :]], axis=2)
    return (mixed, grad_tokens, grad_sums[0], grad_sums[1], grad_sums[2], grad_sums[3], grad_sums[4], grad_sums[5], grad_sums[6], grad_sums[7], grad_sums[8], grad_sums[9], logit_max, clipped_qk)
```

```python
import functools

import jax
import jax.numpy as jnp
from jax import lax
from jax.experimental import pallas as pl
from jax.experimental.pallas import tpu as pltpu
from jax.sharding import PartitionSpec as P

H = 12
PATCHES = 196
HD = 64
D = 768
PAIRS = H // 2
CHUNK = 208
BLOCKS = 2
ROWS = BLOCKS * CHUNK
FF_BLOCK = 768
EPSILON = 1e-06
NEGATIVE = -1e30
SCALE = HD ** (-0.5)
VMEM_LIMIT = 58 * 1024 * 1024
BF = jnp.bfloat16
F32 = jnp.float32


def mm(a, b):
    return lax.dot_general(a, b, (((1,), (0,)), ((), ())), preferred_element_type=F32)


def mm_nt(a, b):
    return lax.dot_general(a, b, (((1,), (1,)), ((), ())), preferred_element_type=F32)


def mm_tn(a, b):
    return lax.dot_general(a, b, (((0,), (0,)), ((), ())), preferred_element_type=F32)


def row_stats(rows):
    centre = jnp.mean(rows, axis=-1, keepdims=True)
    centred = rows - centre
    second = jnp.mean(centred * centred, axis=-1, keepdims=True)
    inverse = lax.rsqrt(second + EPSILON)
    return centred * inverse, inverse


def norm_backward(grad, unit, inverse, gain):
    weighted = grad * gain
    first = jnp.mean(weighted, axis=-1, keepdims=True)
    second = jnp.mean(weighted * unit, axis=-1, keepdims=True)
    return (weighted - first - unit * second) * inverse


def column_sum(values):
    return jnp.sum(values.astype(F32), axis=0, keepdims=True)


def masks(temporal, block, frames):
    row = lax.broadcasted_iota(jnp.int32, (2 * CHUNK, CHUNK), 0)
    col = lax.broadcasted_iota(jnp.int32, (2 * CHUNK, CHUNK), 1)
    if temporal:
        row = jnp.where(row >= CHUNK, row - CHUNK, row)
        allowed = (row // frames) == (col // frames)
    else:
        allowed = col < PATCHES
    return allowed


def lower_lanes(rows):
    return lax.broadcasted_iota(jnp.int32, (rows, 2 * HD), 1) < HD


def split_heads(pair, scale=None):
    low_half = lower_lanes(pair.shape[0])
    if scale is not None:
        pair = pair * jnp.asarray(scale, pair.dtype)
    zero = jnp.zeros_like(pair)
    return jnp.where(low_half, pair, zero), jnp.where(low_half, zero, pair)


def attend_forward(proj_ref, ctx_ref, soft_ref, peak_ref, temporal, frames, valid):
    lane = lax.broadcasted_iota(jnp.int32, (8, 128), 1)
    peaks = jnp.full((8, 128), NEGATIVE, F32)
    for block in range(BLOCKS):
        allowed = masks(temporal, block, frames)
        rows = slice(block * CHUNK, (block + 1) * CHUNK)
        row_id = lax.broadcasted_iota(jnp.int32, (CHUNK, 1), 0)
        for pair in range(PAIRS):
            cols = slice(pair * 128, pair * 128 + 128)
            q_a, q_b = split_heads(proj_ref[rows, cols], SCALE)
            keys = proj_ref[rows, D + pair * 128 : D + pair * 128 + 128]
            v_a, v_b = split_heads(proj_ref[rows, 2 * D + pair * 128 : 2 * D + pair * 128 + 128])
            scores = mm_nt(jnp.concatenate([q_a, q_b], axis=0), keys)
            scores = jnp.where(allowed, scores, NEGATIVE)
            top = jnp.max(scores, axis=1, keepdims=True)
            expo = jnp.exp(scores - top)
            total = jnp.sum(expo, axis=1, keepdims=True)
            soft = (expo / total).astype(BF)
            soft_ref[block * PAIRS + pair] = soft
            ctx_ref[rows, cols] = (mm(soft[:CHUNK], v_a) + mm(soft[CHUNK:], v_b)).astype(BF)
            for side in range(2):
                seen = jnp.where(row_id < valid[block], top[side * CHUNK : (side + 1) * CHUNK], NEGATIVE)
                best = jnp.max(seen, axis=0, keepdims=True)
                peaks = jnp.where(lane == 2 * pair + side, jnp.maximum(peaks, best), peaks)
    peak_ref[...] = peaks


def attend_backward(proj_ref, soft_ref, gctx_ref, gproj_ref):
    for block in range(BLOCKS):
        rows = slice(block * CHUNK, (block + 1) * CHUNK)
        for pair in range(PAIRS):
            cols = slice(pair * 128, pair * 128 + 128)
            kcols = slice(D + pair * 128, D + pair * 128 + 128)
            vcols = slice(2 * D + pair * 128, 2 * D + pair * 128 + 128)
            q_pair = jnp.concatenate(split_heads(proj_ref[rows, cols], SCALE), axis=0)
            k_a, k_b = split_heads(proj_ref[rows, kcols], SCALE)
            values = proj_ref[rows, vcols]
            g_pair = jnp.concatenate(split_heads(gctx_ref[rows, cols]), axis=0)
            soft_low = soft_ref[block * PAIRS + pair]
            soft = soft_low.astype(F32)
            grad_soft = mm_nt(g_pair, values)
            inner = jnp.sum(soft * grad_soft, axis=1, keepdims=True)
            grad_scores = (soft * (grad_soft - inner)).astype(BF)
            gproj_ref[rows, cols] = (mm(grad_scores[:CHUNK], k_a) + mm(grad_scores[CHUNK:], k_b)).astype(BF)
            gproj_ref[rows, kcols] = mm_tn(grad_scores, q_pair).astype(BF)
            gproj_ref[rows, vcols] = mm_tn(soft_low, g_pair).astype(BF)


def project(na_ref, qkv_ref, qv_ref, proj_ref):
    for part in range(3):
        cols = slice(part * D, (part + 1) * D)
        value = mm(na_ref[...], qkv_ref[:, cols])
        if part != 1:
            at = 0 if part == 0 else D
            value = value + qv_ref[:, at : at + D]
        proj_ref[:, cols] = value.astype(BF)


def space_forward_kernel(
    tok_ref, gain_ref, shift_ref, qkv_ref, qv_ref, out_ref, outb_ref,
    x1_ref, na_ref, proj_ref, soft_ref, ctx_ref, peak_ref, rows_ref,
):
    count = tok_ref.shape[0]
    flat = tok_ref[...].astype(F32)
    rows_ref[0:count, :] = flat
    rows_ref[CHUNK : CHUNK + PATCHES, :] = flat[PATCHES:, :]
    rows_ref[PATCHES:CHUNK, :] = jnp.zeros((CHUNK - PATCHES, D), F32)
    rows_ref[CHUNK + PATCHES :, :] = jnp.zeros((CHUNK - PATCHES, D), F32)
    unit, _ = row_stats(rows_ref[...])
    na_ref[...] = (unit * gain_ref[...] + shift_ref[...]).astype(BF)
    project(na_ref, qkv_ref, qv_ref, proj_ref)
    attend_forward(proj_ref, ctx_ref, soft_ref, peak_ref, False, 0, (PATCHES, PATCHES))
    rows_ref[...] = rows_ref[...] + mm(ctx_ref[...], out_ref[...]) + outb_ref[...]
    shares, frames, width = x1_ref.shape[0], x1_ref.shape[1], x1_ref.shape[2]
    for share in range(shares):
        for frame in range(frames):
            start = frame * CHUNK + share * width
            x1_ref[share, frame] = rows_ref[start : start + width, :].astype(BF)


def interleave(parts_ref, stripes_ref, rows_ref):
    shares, frames, width = parts_ref.shape[0], parts_ref.shape[1], parts_ref.shape[2]
    total = shares * frames
    for stripe in range(D // 128):
        cols = slice(stripe * 128, stripe * 128 + 128)
        for share in range(shares):
            for frame in range(frames):
                stripes_ref[stripe, pl.ds(share * frames + frame, width, stride=total), :] = parts_ref[
                    share, frame, :, cols
                ].astype(F32)
        stripes_ref[stripe, total * width :, :] = jnp.zeros((ROWS - total * width, 128), F32)
        rows_ref[:, cols] = stripes_ref[stripe].astype(rows_ref.dtype)


def separate(rows, stripes_ref, parts_ref):
    shares, frames, width = parts_ref.shape[0], parts_ref.shape[1], parts_ref.shape[2]
    total = shares * frames
    for stripe in range(D // 128):
        cols = slice(stripe * 128, stripe * 128 + 128)
        stripes_ref[stripe] = rows[:, cols]
        for share in range(shares):
            for frame in range(frames):
                parts_ref[share, frame, :, cols] = stripes_ref[
                    stripe, pl.ds(share * frames + frame, width, stride=total), :
                ].astype(parts_ref.dtype)


def time_forward_kernel(
    parts_ref, gain_ref, shift_ref, qkv_ref, qv_ref, out_ref, outb_ref,
    x1_ref, x2_ref, na_ref, proj_ref, soft_ref, ctx_ref, peak_ref, stripes_ref,
):
    frames = parts_ref.shape[0] * parts_ref.shape[1]
    count = frames * parts_ref.shape[2]
    interleave(parts_ref, stripes_ref, x1_ref)
    unit, _ = row_stats(x1_ref[...])
    na_ref[...] = (unit * gain_ref[...] + shift_ref[...]).astype(BF)
    project(na_ref, qkv_ref, qv_ref, proj_ref)
    attend_forward(proj_ref, ctx_ref, soft_ref, peak_ref, True, frames, (CHUNK, count - CHUNK))
    x2_ref[...] = x1_ref[...] + mm(ctx_ref[...], out_ref[...]) + outb_ref[...]


def mlp_kernel(
    x2_ref, gy_ref, gain_ref, shift_ref, in_ref, inb_ref, out_ref, outb_ref,
    mixed_ref, g2_ref, gin_ref, gout_ref, ggain_ref, gshift_ref, ginb_ref, goutb_ref,
    n2_ref, gyl_ref, rows_ref, back_ref, stripes_ref,
):
    step = pl.program_id(0)

    @pl.when(step == 0)
    def _():
        unit, _ = row_stats(x2_ref[...])
        n2_ref[...] = (unit * gain_ref[...] + shift_ref[...]).astype(BF)
        interleave(gy_ref, stripes_ref, gyl_ref)
        goutb_ref[...] = column_sum(gyl_ref[...])
        rows_ref[...] = jnp.zeros_like(rows_ref)
        back_ref[...] = jnp.zeros_like(back_ref)

    hidden = mm(n2_ref[...], in_ref[...]) + inb_ref[...]
    cumulative = 0.5 * (1.0 + lax.erf(hidden * (2.0 ** -0.5)))
    act = (hidden * cumulative).astype(BF)
    slope = cumulative + hidden * jnp.exp(-0.5 * hidden * hidden) * 0.3989422804014327
    rows_ref[...] += mm(act, out_ref[...])
    gout_ref[...] = mm_tn(act, gyl_ref[...]).astype(BF)
    ghid = (mm_nt(gyl_ref[...], out_ref[...]) * slope).astype(BF)
    ginb_ref[...] = column_sum(ghid)
    gin_ref[...] = mm_tn(n2_ref[...], ghid).astype(BF)
    back_ref[...] += mm_nt(ghid, in_ref[...])

    @pl.when(step == pl.num_programs(0) - 1)
    def _():
        separate(x2_ref[...] + rows_ref[...] + outb_ref[...], stripes_ref, mixed_ref)
        unit, inverse = row_stats(x2_ref[...])
        grad = back_ref[...]
        ggain_ref[...] = column_sum(grad * unit)
        gshift_ref[...] = column_sum(grad)
        g2_ref[...] = gyl_ref[...].astype(F32) + norm_backward(grad, unit, inverse, gain_ref[...])


def branch_backward(g_ref, ctx_ref, proj_ref, soft_ref, out_ref, gout_ref, goutb_ref, gproj_ref, gqv_ref, gbr_ref, gctx_ref):
    gbr_ref[...] = g_ref[...].astype(BF)
    goutb_ref[...] = column_sum(gbr_ref[...])
    gctx_ref[...] = mm_nt(gbr_ref[...], out_ref[...]).astype(BF)
    gout_ref[...] = mm_tn(ctx_ref[...], gbr_ref[...]).astype(BF)
    attend_backward(proj_ref, soft_ref, gctx_ref, gproj_ref)
    gqv_ref[:, 0:D] = column_sum(gproj_ref[:, 0:D])
    gqv_ref[:, D:] = column_sum(gproj_ref[:, 2 * D :])


def projection_backward(gproj_ref, qkv_ref):
    total = mm_nt(gproj_ref[:, 0:D], qkv_ref[:, 0:D])
    for part in range(1, 3):
        cols = slice(part * D, (part + 1) * D)
        total = total + mm_nt(gproj_ref[:, cols], qkv_ref[:, cols])
    return total


def time_backward_kernel(
    g_ref, x1_ref, gain_ref, ctx_ref, proj_ref, soft_ref, qkv_ref, out_ref,
    parts_ref, gproj_ref, gout_ref, goutb_ref, gqv_ref, ggain_ref, gshift_ref,
    gbr_ref, gctx_ref, stripes_ref,
):
    branch_backward(g_ref, ctx_ref, proj_ref, soft_ref, out_ref, gout_ref, goutb_ref, gproj_ref, gqv_ref, gbr_ref, gctx_ref)
    grad = projection_backward(gproj_ref, qkv_ref)
    unit, inverse = row_stats(x1_ref[...])
    ggain_ref[...] = column_sum(grad * unit)
    gshift_ref[...] = column_sum(grad)
    separate(g_ref[...] + norm_backward(grad, unit, inverse, gain_ref[...]), stripes_ref, parts_ref)


def weight_grad_kernel(na_ref, gproj_ref, gqkv_ref):
    for part in range(3):
        cols = slice(part * D, (part + 1) * D)
        gqkv_ref[:, cols] = mm_tn(na_ref[...], gproj_ref[:, cols]).astype(BF)


def space_backward_kernel(
    parts_ref, na_ref, ctx_ref, proj_ref, soft_ref, out_ref,
    g_ref, gproj_ref, gout_ref, goutb_ref, gqv_ref, gqkv_ref,
    gbr_ref, gctx_ref,
):
    shares, frames, width = parts_ref.shape[0], parts_ref.shape[1], parts_ref.shape[2]
    for frame in range(frames):
        for share in range(shares):
            start = frame * CHUNK + share * width
            g_ref[start : start + width, :] = parts_ref[share, frame].astype(F32)
        g_ref[frame * CHUNK + PATCHES : (frame + 1) * CHUNK, :] = jnp.zeros((CHUNK - PATCHES, D), F32)
    branch_backward(g_ref, ctx_ref, proj_ref, soft_ref, out_ref, gout_ref, goutb_ref, gproj_ref, gqv_ref, gbr_ref, gctx_ref)
    weight_grad_kernel(na_ref, gproj_ref, gqkv_ref)


def space_input_kernel(tok_ref, g_ref, gain_ref, gproj_ref, qkv_ref, gtok_ref, ggain_ref, gshift_ref, rows_ref):
    count = tok_ref.shape[0]
    flat = tok_ref[...].astype(F32)
    rows_ref[0:count, :] = flat
    rows_ref[CHUNK : CHUNK + PATCHES, :] = flat[PATCHES:, :]
    rows_ref[PATCHES:CHUNK, :] = jnp.zeros((CHUNK - PATCHES, D), F32)
    rows_ref[CHUNK + PATCHES :, :] = jnp.zeros((CHUNK - PATCHES, D), F32)
    unit, inverse = row_stats(rows_ref[...])
    grad = projection_backward(gproj_ref, qkv_ref)
    ggain_ref[...] = column_sum(grad * unit)
    gshift_ref[...] = column_sum(grad)
    rows_ref[...] = g_ref[...] + norm_backward(grad, unit, inverse, gain_ref[...])
    gtok_ref[0:PATCHES, :] = rows_ref[0:PATCHES, :]
    gtok_ref[PATCHES:, :] = rows_ref[CHUNK : CHUNK + PATCHES, :]


def call(kernel, outs, scratch, flops, *operands, name):
    return pl.pallas_call(
        kernel,
        out_shape=[jax.ShapeDtypeStruct(shape, dtype) for shape, dtype in outs],
        scratch_shapes=[pltpu.VMEM(shape, dtype) for shape, dtype in scratch],
        compiler_params=pltpu.CompilerParams(vmem_limit_bytes=VMEM_LIMIT),
        cost_estimate=pl.CostEstimate(flops=flops, bytes_accessed=8 * 2**20, transcendentals=0),
        name=name,
    )(*operands)


def exchange(parts):
    return lax.all_to_all(parts, "seq", split_axis=0, concat_axis=0, tiled=True)


def on_device(
    tokens, norm_gain, norm_bias, attn_qkv, attn_qv_bias, attn_out, attn_out_bias,
    mlp_in, mlp_in_bias, mlp_out, mlp_out_bias, threshold, cotangent,
):
    clip_count, local_len, _ = tokens.shape
    seq = lax.axis_size("seq")
    frames = local_len // PATCHES
    width = PATCHES // seq
    ff = mlp_in.shape[1]
    split_shape = (seq, frames, width, D)
    tok = tokens.reshape(local_len, D)
    cot = jnp.swapaxes(cotangent.reshape(frames, seq, width, D), 0, 1)

    def gather(value, axis):
        return lax.all_gather(value, "fsdp", axis=axis, tiled=True)

    gain = gather(norm_gain, 1).astype(F32)
    shift = gather(norm_bias, 1).astype(F32)
    qv = gather(attn_qv_bias, 1).astype(F32)
    outb = gather(attn_out_bias, 1).astype(F32)
    inb = gather(mlp_in_bias, 0).astype(F32).reshape(1, ff)
    moutb = gather(mlp_out_bias, 0).astype(F32).reshape(1, D)
    qkv = [gather(attn_qkv[a], 0) for a in range(2)]
    out = [gather(attn_out[a], 0) for a in range(2)]
    w_in = gather(mlp_in, 0)
    w_out = gather(mlp_out, 0)

    def row(matrix, index):
        return matrix[index : index + 1]

    state = lambda: [
        ((ROWS, D), BF), ((ROWS, 3 * D), BF), ((BLOCKS * PAIRS, 2 * CHUNK, CHUNK), BF), ((ROWS, D), BF), ((8, 128), F32),
    ]
    attn_flops = 2 * ROWS * D * 4 * D + 4 * BLOCKS * H * CHUNK * CHUNK * HD
    parts, na0, proj0, soft0, ctx0, peak0 = call(
        space_forward_kernel, [(split_shape, BF)] + state(), [((ROWS, D), F32)], attn_flops,
        tok, row(gain, 0), row(shift, 0), qkv[0], row(qv, 0), out[0], row(outb, 0), name="space_forward",
    )
    parts = exchange(parts)
    x1, x2, na1, proj1, soft1, ctx1, peak1 = call(
        time_forward_kernel, [((ROWS, D), F32), ((ROWS, D), F32)] + state(), [((D // 128, ROWS, 128), F32)], attn_flops,
        parts, row(gain, 1), row(shift, 1), qkv[1], row(qv, 1), out[1], row(outb, 1), name="time_forward",
    )
    gy = exchange(cot)
    fixed = lambda *shape: pl.BlockSpec(shape, lambda i: (0,) * len(shape))
    mixed, g2, g_in, g_mout, ggain2, gshift2, g_inb, g_moutb = pl.pallas_call(
        mlp_kernel,
        grid=(ff // FF_BLOCK,),
        in_specs=[
            fixed(ROWS, D), fixed(*split_shape), fixed(1, D), fixed(1, D),
            pl.BlockSpec((D, FF_BLOCK), lambda i: (0, i)), pl.BlockSpec((1, FF_BLOCK), lambda i: (0, i)),
            pl.BlockSpec((FF_BLOCK, D), lambda i: (i, 0)), fixed(1, D),
        ],
        out_specs=[
            fixed(*split_shape), fixed(ROWS, D),
            pl.BlockSpec((D, FF_BLOCK), lambda i: (0, i)), pl.BlockSpec((FF_BLOCK, D), lambda i: (i, 0)),
            fixed(1, D), fixed(1, D), pl.BlockSpec((1, FF_BLOCK), lambda i: (0, i)), fixed(1, D),
        ],
        out_shape=[
            jax.ShapeDtypeStruct(split_shape, BF), jax.ShapeDtypeStruct((ROWS, D), F32),
            jax.ShapeDtypeStruct((D, ff), BF), jax.ShapeDtypeStruct((ff, D), BF),
            jax.ShapeDtypeStruct((1, D), F32), jax.ShapeDtypeStruct((1, D), F32),
            jax.ShapeDtypeStruct((1, ff), F32), jax.ShapeDtypeStruct((1, D), F32),
        ],
        scratch_shapes=[
            pltpu.VMEM((ROWS, D), BF), pltpu.VMEM((ROWS, D), BF), pltpu.VMEM((ROWS, D), F32), pltpu.VMEM((ROWS, D), F32),
            pltpu.VMEM((D // 128, ROWS, 128), F32),
        ],
        compiler_params=pltpu.CompilerParams(vmem_limit_bytes=VMEM_LIMIT),
        cost_estimate=pl.CostEstimate(flops=10 * ROWS * D * ff, bytes_accessed=20 * 2**20, transcendentals=0),
        name="mlp",
    )(x2, gy, row(gain, 2), row(shift, 2), w_in, inb, w_out, moutb)
    mixed = exchange(mixed)
    small = [((1, D), F32), ((1, 2 * D), F32)]
    gparts, gproj1, g_out1, g_outb1, g_qv1, ggain1, gshift1 = call(
        time_backward_kernel,
        [(split_shape, BF), ((ROWS, 3 * D), BF), ((D, D), BF)] + small + [((1, D), F32)] * 2,
        [((ROWS, D), BF), ((ROWS, D), BF), ((D // 128, ROWS, 128), F32)], 2 * attn_flops,
        g2, x1, row(gain, 1), ctx1, proj1, soft1, qkv[1], out[1], name="time_backward",
    )
    gparts = exchange(gparts)
    (g_qkv1,) = call(weight_grad_kernel, [((D, 3 * D), BF)], [], attn_flops, na1, gproj1, name="time_weight_grad")
    g1, gproj0, g_out0, g_outb0, g_qv0, g_qkv0 = call(
        space_backward_kernel,
        [((ROWS, D), F32), ((ROWS, 3 * D), BF), ((D, D), BF)] + small + [((D, 3 * D), BF)],
        [((ROWS, D), BF), ((ROWS, D), BF)], 2 * attn_flops,
        gparts, na0, ctx0, proj0, soft0, out[0], name="space_backward",
    )
    g_tok, ggain0, gshift0 = call(
        space_input_kernel, [((local_len, D), F32), ((1, D), F32), ((1, D), F32)], [((ROWS, D), F32)], attn_flops,
        tok, g1, row(gain, 0), gproj0, qkv[0], name="space_input",
    )

    def scatter(value, axis):
        return lax.psum_scatter(value, "fsdp", scatter_dimension=axis, tiled=True)

    def total(value, axis):
        return lax.psum(scatter(value, axis).astype(BF), "seq").astype(F32)

    grad_qkv = jnp.stack([total(g_qkv0, 0), total(g_qkv1, 0)])
    grad_out = jnp.stack([total(g_out0, 0), total(g_out1, 0)])
    grad_in = total(g_in, 0)
    grad_mout = total(g_mout, 0)
    grad_gain = lax.psum(scatter(jnp.concatenate([ggain0, ggain1, ggain2]), 1), "seq")
    grad_shift = lax.psum(scatter(jnp.concatenate([gshift0, gshift1, gshift2]), 1), "seq")
    grad_qv = lax.psum(scatter(jnp.concatenate([g_qv0, g_qv1]), 1), "seq")
    grad_outb = lax.psum(scatter(jnp.concatenate([g_outb0, g_outb1]), 1), "seq")
    grad_inb = lax.psum(scatter(g_inb[0], 0), "seq")
    grad_moutb = lax.psum(scatter(g_moutb[0], 0), "seq")

    peak_pair = jnp.stack([peak0[0, :H], peak1[0, :H]])
    logit_max = lax.pmax(peak_pair, ("fsdp", "seq"))
    factor = threshold / jnp.maximum(logit_max, threshold)
    column_scale = jnp.repeat(jnp.sqrt(factor), HD, axis=1)
    clipped = attn_qkv[:, :, : 2 * D].astype(F32) * jnp.concatenate([column_scale, column_scale], axis=1)[:, None, :]
    mixed = jnp.swapaxes(mixed, 0, 1).reshape(tokens.shape)
    return (
        mixed, g_tok.reshape(tokens.shape), grad_gain, grad_shift, grad_qkv, grad_qv, grad_out, grad_outb,
        grad_in, grad_inb, grad_mout, grad_moutb, logit_max, clipped,
    )


def solution(mesh):
    placed = (
        P("fsdp", "seq", None), P(None, "fsdp"), P(None, "fsdp"), P(None, "fsdp", None), P(None, "fsdp"),
        P(None, "fsdp", None), P(None, "fsdp"), P("fsdp", None), P("fsdp"), P("fsdp", None), P("fsdp"), P(),
        P("fsdp", "seq", None),
    )
    return jax.shard_map(
        on_device,
        mesh=mesh,
        in_specs=placed,
        out_specs=(
            P("fsdp", "seq", None), P("fsdp", "seq", None), P(None, "fsdp"), P(None, "fsdp"), P(None, "fsdp", None),
            P(None, "fsdp"), P(None, "fsdp", None), P(None, "fsdp"), P("fsdp", None), P("fsdp"), P("fsdp", None),
            P("fsdp"), P(), P(None, "fsdp", None),
        ),
        check_vma=False,
    )
```

```python
import functools
import itertools

import jax
import jax.numpy as jnp
from jax import lax
from jax.experimental import pallas as pl
from jax.experimental.pallas import tpu as pltpu
from jax.sharding import PartitionSpec as P

H = 12
PATCHES = 196
HD = 64
D = 768
PAIRS = H // 2
CHUNK = 208
BLOCKS = 2
ROWS = BLOCKS * CHUNK
FF_BLOCK = 768
EPSILON = 1e-06
NEGATIVE = -1e30
SCALE = HD ** (-0.5)
COST = 1000
VMEM_LIMIT = 58 * 1024 * 1024
BF = jnp.bfloat16
F32 = jnp.float32


def mm(a, b):
    return lax.dot_general(a, b, (((1,), (0,)), ((), ())), preferred_element_type=F32)


def mm_nt(a, b):
    return lax.dot_general(a, b, (((1,), (1,)), ((), ())), preferred_element_type=F32)


def mm_tn(a, b):
    return lax.dot_general(a, b, (((0,), (0,)), ((), ())), preferred_element_type=F32)


def row_stats(rows):
    centre = jnp.mean(rows, axis=-1, keepdims=True)
    centred = rows - centre
    second = jnp.mean(centred * centred, axis=-1, keepdims=True)
    inverse = lax.rsqrt(second + EPSILON)
    return centred * inverse, inverse


def norm_backward(grad, unit, inverse, gain):
    weighted = grad * gain
    first = jnp.mean(weighted, axis=-1, keepdims=True)
    second = jnp.mean(weighted * unit, axis=-1, keepdims=True)
    return (weighted - first - unit * second) * inverse


def column_sum(values):
    return jnp.sum(values.astype(F32), axis=0, keepdims=True)


def masks(temporal, block, frames):
    row = lax.broadcasted_iota(jnp.int32, (2 * CHUNK, CHUNK), 0)
    col = lax.broadcasted_iota(jnp.int32, (2 * CHUNK, CHUNK), 1)
    if temporal:
        row = jnp.where(row >= CHUNK, row - CHUNK, row)
        allowed = (row // frames) == (col // frames)
    else:
        allowed = col < PATCHES
    return allowed


def lower_lanes(rows):
    return lax.broadcasted_iota(jnp.int32, (rows, 2 * HD), 1) < HD


def split_heads(pair, scale=None):
    low_half = lower_lanes(pair.shape[0])
    if scale is not None:
        pair = pair * jnp.asarray(scale, pair.dtype)
    zero = jnp.zeros_like(pair)
    return jnp.where(low_half, pair, zero), jnp.where(low_half, zero, pair)


def attend_forward(proj_ref, ctx_ref, soft_ref, peak_ref, temporal, frames, valid):
    lane = lax.broadcasted_iota(jnp.int32, (8, 128), 1)
    peaks = jnp.full((8, 128), NEGATIVE, F32)
    for block in range(BLOCKS):
        allowed = masks(temporal, block, frames)
        rows = slice(block * CHUNK, (block + 1) * CHUNK)
        row_id = lax.broadcasted_iota(jnp.int32, (CHUNK, 1), 0)
        for pair in range(PAIRS):
            cols = slice(pair * 128, pair * 128 + 128)
            q_a, q_b = split_heads(proj_ref[rows, cols], SCALE)
            keys = proj_ref[rows, D + pair * 128 : D + pair * 128 + 128]
            v_a, v_b = split_heads(proj_ref[rows, 2 * D + pair * 128 : 2 * D + pair * 128 + 128])
            scores = mm_nt(jnp.concatenate([q_a, q_b], axis=0), keys)
            scores = jnp.where(allowed, scores, NEGATIVE)
            top = jnp.max(scores, axis=1, keepdims=True)
            expo = jnp.exp(scores - top)
            total = jnp.sum(expo, axis=1, keepdims=True)
            soft = (expo / total).astype(BF)
            soft_ref[block * PAIRS + pair] = soft
            ctx_ref[rows, cols] = (mm(soft[:CHUNK], v_a) + mm(soft[CHUNK:], v_b)).astype(BF)
            for side in range(2):
                seen = jnp.where(row_id < valid[block], top[side * CHUNK : (side + 1) * CHUNK], NEGATIVE)
                best = jnp.max(seen, axis=0, keepdims=True)
                peaks = jnp.where(lane == 2 * pair + side, jnp.maximum(peaks, best), peaks)
    peak_ref[...] = peaks


def attend_backward(proj_ref, soft_ref, gctx_ref, gproj_ref):
    for block in range(BLOCKS):
        rows = slice(block * CHUNK, (block + 1) * CHUNK)
        for pair in range(PAIRS):
            cols = slice(pair * 128, pair * 128 + 128)
            kcols = slice(D + pair * 128, D + pair * 128 + 128)
            vcols = slice(2 * D + pair * 128, 2 * D + pair * 128 + 128)
            q_pair = jnp.concatenate(split_heads(proj_ref[rows, cols], SCALE), axis=0)
            k_a, k_b = split_heads(proj_ref[rows, kcols], SCALE)
            values = proj_ref[rows, vcols]
            g_pair = jnp.concatenate(split_heads(gctx_ref[rows, cols]), axis=0)
            soft_low = soft_ref[block * PAIRS + pair]
            soft = soft_low.astype(F32)
            grad_soft = mm_nt(g_pair, values)
            inner = jnp.sum(soft * grad_soft, axis=1, keepdims=True)
            grad_scores = (soft * (grad_soft - inner)).astype(BF)
            gproj_ref[rows, cols] = (mm(grad_scores[:CHUNK], k_a) + mm(grad_scores[CHUNK:], k_b)).astype(BF)
            gproj_ref[rows, kcols] = mm_tn(grad_scores, q_pair).astype(BF)
            gproj_ref[rows, vcols] = mm_tn(soft_low, g_pair).astype(BF)


def blocks_between(slot_ref, arrays, plan, weight_ref):
    for array, index, row, column, height, width, place, scale, first, at in plan:
        start = pl.multiple_of(slot_ref[place] * scale + first, 16)
        yield (
            arrays[array].at[index, row : row + height, column : column + width],
            weight_ref.at[pl.ds(start, height), at : at + width],
        )


def fetch(slot_ref, pieces, plan, weight_ref, sems):
    copies = []
    for number, (piece, part) in enumerate(blocks_between(slot_ref, pieces, plan, weight_ref)):
        copies.append(pltpu.make_async_copy(piece, part, sems.at[number]))
        copies[-1].start()
    return copies


def deliver(slot_ref, weight_ref, targets, plan, sems):
    copies = []
    for number, (piece, part) in enumerate(blocks_between(slot_ref, targets, plan, weight_ref)):
        copies.append(pltpu.make_async_copy(part, piece, sems.at[number]))
        copies[-1].start()
    return copies


def take(refs, plan):
    count = 1 + max(entry[0] for entry in plan)
    return refs[:count], refs[count:]


def finish(copies):
    for copy in copies:
        copy.wait()


def project(na_ref, qkv_ref, qv, proj_ref):
    for part in range(3):
        cols = slice(part * D, (part + 1) * D)
        value = mm(na_ref[...], qkv_ref[:, cols])
        if part != 1:
            at = 0 if part == 0 else D
            value = value + qv[:, at : at + D]
        proj_ref[:, cols] = value.astype(BF)


def pad_frames(tok_ref, rows_ref):
    count = tok_ref.shape[0]
    flat = tok_ref[...].astype(F32)
    rows_ref[0:count, :] = flat
    rows_ref[CHUNK : CHUNK + PATCHES, :] = flat[PATCHES:, :]
    rows_ref[PATCHES:CHUNK, :] = jnp.zeros((CHUNK - PATCHES, D), F32)
    rows_ref[CHUNK + PATCHES :, :] = jnp.zeros((CHUNK - PATCHES, D), F32)


def space_forward_kernel(plan, seq, slot_ref, tok_ref, vec_ref, qv_ref, *refs):
    pieces, refs = take(refs, plan)
    part_refs, refs = refs[:seq], refs[seq:]
    na_ref, proj_ref, soft_ref, ctx_ref, peak_ref, rows_ref, weight_ref, sems = refs
    copies = fetch(slot_ref, pieces, plan, weight_ref, sems)
    pad_frames(tok_ref, rows_ref)
    unit, _ = row_stats(rows_ref[...])
    na_ref[...] = (unit * vec_ref[0:1] + vec_ref[3:4]).astype(BF)
    finish(copies)
    project(na_ref, weight_ref, qv_ref[0:1], proj_ref)
    attend_forward(proj_ref, ctx_ref, soft_ref, peak_ref, False, 0, (PATCHES, PATCHES))
    rows_ref[...] = rows_ref[...] + mm(ctx_ref[...], weight_ref[:, 3 * D :]) + vec_ref[6:7]
    frames, width = part_refs[0].shape[0], part_refs[0].shape[1]

    def body(place):
        for distance in range(seq):
            for frame in range(frames):
                start = frame * CHUNK + (place ^ distance) * width
                part_refs[distance][frame] = rows_ref[start : start + width, :].astype(BF)

    for_place(slot_ref, seq, body)


def for_place(slot_ref, count, body):
    for place in range(count):
        pl.when(slot_ref[slot_ref.shape[0] - 1] == place)(functools.partial(body, place))


def interleave(slot_ref, part_refs, stripes_ref, rows_ref):
    shares, frames, width = len(part_refs), part_refs[0].shape[0], part_refs[0].shape[1]
    total = shares * frames
    place = slot_ref[slot_ref.shape[0] - 1]
    for stripe in range(D // 128):
        cols = slice(stripe * 128, stripe * 128 + 128)
        for distance in range(shares):
            for frame in range(frames):
                first = (place ^ distance) * frames + frame
                stripes_ref[stripe, pl.ds(first, width, stride=total), :] = part_refs[distance][frame, :, cols].astype(F32)
        stripes_ref[stripe, total * width :, :] = jnp.zeros((ROWS - total * width, 128), F32)
        rows_ref[:, cols] = stripes_ref[stripe].astype(rows_ref.dtype)


def separate(slot_ref, rows, stripes_ref, part_refs):
    shares, frames, width = len(part_refs), part_refs[0].shape[0], part_refs[0].shape[1]
    total = shares * frames
    place = slot_ref[slot_ref.shape[0] - 1]
    for stripe in range(D // 128):
        cols = slice(stripe * 128, stripe * 128 + 128)
        stripes_ref[stripe] = rows[:, cols]
        for distance in range(shares):
            for frame in range(frames):
                first = (place ^ distance) * frames + frame
                part_refs[distance][frame, :, cols] = stripes_ref[stripe, pl.ds(first, width, stride=total), :].astype(
                    part_refs[distance].dtype
                )


def time_forward_kernel(plan, seq, slot_ref, vec_ref, qv_ref, *refs):
    part_refs, refs = refs[:seq], refs[seq:]
    pieces, refs = take(refs, plan)
    x1_ref, x2_ref, na_ref, proj_ref, soft_ref, ctx_ref, peak_ref, stripes_ref, weight_ref, sems = refs
    copies = fetch(slot_ref, pieces, plan, weight_ref, sems)
    frames = seq * part_refs[0].shape[0]
    count = frames * part_refs[0].shape[1]
    interleave(slot_ref, part_refs, stripes_ref, x1_ref)
    unit, _ = row_stats(x1_ref[...])
    na_ref[...] = (unit * vec_ref[1:2] + vec_ref[4:5]).astype(BF)
    finish(copies)
    project(na_ref, weight_ref, qv_ref[1:2], proj_ref)
    attend_forward(proj_ref, ctx_ref, soft_ref, peak_ref, True, frames, (CHUNK, count - CHUNK))
    x2_ref[...] = x1_ref[...] + mm(ctx_ref[...], weight_ref[:, 3 * D :]) + vec_ref[7:8]


def mlp_kernel(seq, in_plan, out_plan, in_targets, out_targets, slot_ref, x2_ref, vec_ref, inb_ref, *refs):
    gy_refs, refs = refs[:seq], refs[seq:]
    in_pieces, refs = take(refs, in_plan)
    out_pieces, refs = take(refs, out_plan)
    ginb_ref, goutb_ref, *refs = refs
    mixed_refs, refs = refs[:seq], refs[seq:]
    g2_ref, ggain_ref, gshift_ref, *refs = refs
    gin_arrays, refs = take(refs, in_targets)
    gout_arrays, refs = take(refs, out_targets)
    (
        n2_ref, gyl_ref, rows_ref, back_ref, stripes_ref, in_ref, out_ref, gin_ref, gout_ref,
        in_sems, out_sems, gin_sems, gout_sems,
    ) = refs
    blocks = in_ref.shape[1] // FF_BLOCK
    out_height = out_plan[0][4]
    rows_each = FF_BLOCK // out_height

    def span_of(step):
        return pl.ds(pl.multiple_of(step * FF_BLOCK, FF_BLOCK), FF_BLOCK)

    def in_copies(step):
        return [
            pltpu.make_async_copy(piece.at[:, span_of(step)], part.at[:, span_of(step)], in_sems.at[step, number])
            for number, (piece, part) in enumerate(blocks_between(slot_ref, in_pieces, in_plan, in_ref))
        ]

    def gin_copies(step):
        return [
            pltpu.make_async_copy(part.at[:, span_of(step)], piece.at[:, span_of(step)], gin_sems.at[step, number])
            for number, (piece, part) in enumerate(blocks_between(slot_ref, gin_arrays, in_targets, gin_ref))
        ]

    def first_row(entry):
        return slot_ref[entry[6]] * entry[7] + entry[8]

    for step in range(blocks):
        for copy in in_copies(step):
            copy.start()
        if step == 0:
            for entry, (piece, part) in zip(out_plan, blocks_between(slot_ref, out_pieces, out_plan, out_ref)):
                pltpu.make_async_copy(piece, part, out_sems.at[first_row(entry) // out_height]).start()
    unit, _ = row_stats(x2_ref[...])
    n2_ref[...] = (unit * vec_ref[2:3] + vec_ref[5:6]).astype(BF)
    interleave(slot_ref, gy_refs, stripes_ref, gyl_ref)
    goutb_ref[...] = column_sum(gyl_ref[...])
    rows_ref[...] = jnp.zeros_like(rows_ref)
    back_ref[...] = jnp.zeros_like(back_ref)
    gout_copies = [
        pltpu.make_async_copy(part, piece, gout_sems.at[number])
        for number, (piece, part) in enumerate(blocks_between(slot_ref, gout_arrays, out_targets, gout_ref))
    ]

    @pl.loop(0, blocks)
    def _(step):
        span = span_of(step)
        for copy in in_copies(step):
            copy.wait()
        for number in range(rows_each):
            part = out_ref.at[0:out_height, :]
            pltpu.make_async_copy(part, part, out_sems.at[step * rows_each + number]).wait()
        hidden = mm(n2_ref[...], in_ref[:, span]) + inb_ref[:, span]
        cumulative = 0.5 * (1.0 + lax.erf(hidden * (2.0 ** -0.5)))
        act = (hidden * cumulative).astype(BF)
        slope = cumulative + hidden * jnp.exp(-0.5 * hidden * hidden) * 0.3989422804014327
        rows_ref[...] += mm(act, out_ref[span, :])
        gout_ref[span, :] = mm_tn(act, gyl_ref[...]).astype(BF)
        for copy, entry in zip(gout_copies, out_targets):
            pl.when(first_row(entry) // FF_BLOCK == step)(copy.start)
        ghid = (mm_nt(gyl_ref[...], out_ref[span, :]) * slope).astype(BF)
        ginb_ref[:, span] = column_sum(ghid)
        gin_ref[:, span] = mm_tn(n2_ref[...], ghid).astype(BF)
        for copy in gin_copies(step):
            copy.start()
        back_ref[...] += mm_nt(ghid, in_ref[:, span])

    separate(slot_ref, x2_ref[...] + rows_ref[...] + vec_ref[8:9], stripes_ref, mixed_refs)
    unit, inverse = row_stats(x2_ref[...])
    grad = back_ref[...]
    ggain_ref[...] = column_sum(grad * unit)
    gshift_ref[...] = column_sum(grad)
    g2_ref[...] = gyl_ref[...].astype(F32) + norm_backward(grad, unit, inverse, vec_ref[2:3])
    for step in range(blocks):
        finish(gin_copies(step))
    finish(gout_copies)


def branch_backward(g_ref, proj_ref, soft_ref, weight_ref, goutb_ref, gproj_ref, gqv_ref, gbr_ref, gctx_ref):
    gbr_ref[...] = g_ref[...].astype(BF)
    goutb_ref[...] = column_sum(gbr_ref[...])
    gctx_ref[...] = mm_nt(gbr_ref[...], weight_ref[:, 3 * D :]).astype(BF)
    attend_backward(proj_ref, soft_ref, gctx_ref, gproj_ref)
    gqv_ref[:, 0:D] = column_sum(gproj_ref[:, 0:D])
    gqv_ref[:, D:] = column_sum(gproj_ref[:, 2 * D :])


def projection_backward(gproj_ref, weight_ref):
    total = mm_nt(gproj_ref[:, 0:D], weight_ref[:, 0:D])
    for part in range(1, 3):
        cols = slice(part * D, (part + 1) * D)
        total = total + mm_nt(gproj_ref[:, cols], weight_ref[:, cols])
    return total


def weight_grads(na_ref, gproj_ref, ctx_ref, gbr_ref, grad_ref):
    grad_ref[:, 3 * D :] = mm_tn(ctx_ref[...], gbr_ref[...]).astype(BF)
    for part in range(3):
        cols = slice(part * D, (part + 1) * D)
        grad_ref[:, cols] = mm_tn(na_ref[...], gproj_ref[:, cols]).astype(BF)


def time_backward_kernel(plan, seq, slot_ref, g_ref, x1_ref, vec_ref, proj_ref, soft_ref, *refs):
    pieces, refs = take(refs, plan)
    part_refs, refs = refs[:seq], refs[seq:]
    gproj_ref, gbr_ref, goutb_ref, gqv_ref, ggain_ref, gshift_ref, gctx_ref, stripes_ref, weight_ref, sems = refs
    finish(fetch(slot_ref, pieces, plan, weight_ref, sems))
    branch_backward(g_ref, proj_ref, soft_ref, weight_ref, goutb_ref, gproj_ref, gqv_ref, gbr_ref, gctx_ref)
    grad = projection_backward(gproj_ref, weight_ref)
    unit, inverse = row_stats(x1_ref[...])
    ggain_ref[...] = column_sum(grad * unit)
    gshift_ref[...] = column_sum(grad)
    separate(slot_ref, g_ref[...] + norm_backward(grad, unit, inverse, vec_ref[1:2]), stripes_ref, part_refs)


def weight_grad_kernel(targets, slot_ref, na_ref, gproj_ref, ctx_ref, gbr_ref, *refs):
    outs, (grad_ref, sems) = take(refs, targets)
    weight_grads(na_ref, gproj_ref, ctx_ref, gbr_ref, grad_ref)
    finish(deliver(slot_ref, grad_ref, outs, targets, sems))


def space_backward_kernel(plan, targets, seq, slot_ref, na_ref, ctx_ref, proj_ref, soft_ref, *refs):
    part_refs, refs = refs[:seq], refs[seq:]
    pieces, refs = take(refs, plan)
    g_ref, gproj_ref, goutb_ref, gqv_ref = refs[:4]
    outs, refs = take(refs[4:], targets)
    gbr_ref, gctx_ref, weight_ref, grad_ref, sems, grad_sems = refs
    copies = fetch(slot_ref, pieces, plan, weight_ref, sems)
    frames, width = part_refs[0].shape[0], part_refs[0].shape[1]

    def body(place):
        for frame in range(frames):
            for distance in range(seq):
                start = frame * CHUNK + (place ^ distance) * width
                g_ref[start : start + width, :] = part_refs[distance][frame].astype(F32)

    for_place(slot_ref, seq, body)
    for frame in range(frames):
        g_ref[frame * CHUNK + PATCHES : (frame + 1) * CHUNK, :] = jnp.zeros((CHUNK - PATCHES, D), F32)
    finish(copies)
    branch_backward(g_ref, proj_ref, soft_ref, weight_ref, goutb_ref, gproj_ref, gqv_ref, gbr_ref, gctx_ref)
    weight_grads(na_ref, gproj_ref, ctx_ref, gbr_ref, grad_ref)
    finish(deliver(slot_ref, grad_ref, outs, targets, grad_sems))


def space_input_kernel(plan, slot_ref, tok_ref, g_ref, vec_ref, gproj_ref, *refs):
    pieces, refs = take(refs, plan)
    gtok_ref, ggain_ref, gshift_ref, rows_ref, weight_ref, sems = refs
    copies = fetch(slot_ref, pieces, plan, weight_ref, sems)
    pad_frames(tok_ref, rows_ref)
    unit, inverse = row_stats(rows_ref[...])
    finish(copies)
    grad = projection_backward(gproj_ref, weight_ref)
    ggain_ref[...] = column_sum(grad * unit)
    gshift_ref[...] = column_sum(grad)
    rows_ref[...] = g_ref[...] + norm_backward(grad, unit, inverse, vec_ref[0:1])
    gtok_ref[0:PATCHES, :] = rows_ref[0:PATCHES, :]
    gtok_ref[PATCHES:, :] = rows_ref[CHUNK : CHUNK + PATCHES, :]


def call(kernel, outs, scratch, flops, slot, operands, pieces=(), targets=(), sems=(), *, name):
    whole = pl.BlockSpec(memory_space=pltpu.VMEM)
    far = pl.BlockSpec(memory_space=pl.ANY)
    return pl.pallas_call(
        kernel,
        in_specs=[pl.BlockSpec(memory_space=pltpu.SMEM)] + [whole] * len(operands) + [far] * len(pieces),
        out_specs=[whole] * len(outs) + [far] * len(targets),
        out_shape=[jax.ShapeDtypeStruct(shape, dtype) for shape, dtype in list(outs) + list(targets)],
        scratch_shapes=[pltpu.VMEM(shape, dtype) for shape, dtype in scratch]
        + [pltpu.SemaphoreType.DMA(count if isinstance(count, tuple) else (count,)) for count in sems],
        compiler_params=pltpu.CompilerParams(vmem_limit_bytes=VMEM_LIMIT),
        cost_estimate=pl.CostEstimate(flops=COST, bytes_accessed=COST, transcendentals=0),
        name=name,
    )(slot, *operands, *pieces)


def hop(value, axis, bit):
    return lax.ppermute(value, axis, [(index, index ^ bit) for index in range(lax.axis_size(axis))])


CORE, CHIP_X, CHIP_Y = 1, 2, 4
X_ORDER = (0, CHIP_Y, CHIP_X, CHIP_X | CHIP_Y)
Y_ORDER = (0, CHIP_X, CHIP_Y, CHIP_X | CHIP_Y)


def pack_rows(value):
    return jnp.concatenate(jnp.split(value, 4, axis=0), axis=1)


def unpack_rows(value):
    return jnp.concatenate(jnp.split(value, 4, axis=1), axis=0)


def targets_of(height, width, order):
    return [
        (side, chip, 0, 0, height, width, order[chip] ^ shift, height, 0, 0)
        for side, shift in enumerate((0, CORE)) for chip in range(4)
    ]


def gather_plain(own):
    full = lax.all_gather(own[None], "fsdp", axis=1, tiled=True)
    return [full], plain_plan(full.shape[1], full.shape[2])


def plain_plan(rows, columns):
    return [(0, 0, 0, 0, rows, columns, 0, 0, 0, 0)]


tie = lax.optimization_barrier


def sums_of(keep, got):
    return lambda part: keep[part].astype(F32) + got[part].astype(F32)


def pair_of(keep, got, first):
    return sums_of(keep, got)(slice(first + 2, first + 4)).astype(BF)


def rest_of(keep, got, first, came):
    return (sums_of(keep, got)(first + 1) + came[1].astype(F32)).astype(BF)


def own_of(keep, got, first, came, last):
    return sums_of(keep, got)(first) + came[0].astype(F32) + last.astype(F32)


def over_x(value):
    return hop(value, "fsdp", CHIP_X)


def over_y(value):
    return hop(value, "fsdp", CHIP_Y)


def over_core(value):
    return hop(value, "fsdp", CORE)


def reduce_plain(grad):
    return lax.psum_scatter(grad[0], "fsdp", scatter_dimension=0, tiled=True).astype(F32)


def seq_first(value):
    odd = (lax.axis_index("seq") & 1) == 1
    half = value.shape[0] // 2
    low, high = value[:half], value[half:]
    return (jnp.where(odd, high, low) + hop(jnp.where(odd, low, high).astype(BF), "seq", 1).astype(F32)).astype(BF)


def seq_second(part):
    return (part.astype(F32) + hop(part, "seq", 2).astype(F32)).astype(BF)


def seq_third(part):
    odd = (lax.axis_index("seq") & 1) == 1
    other = hop(part, "seq", 1)
    return jnp.where(odd, jnp.concatenate([other, part]), jnp.concatenate([part, other])).astype(F32)


def seq_total(value):
    if lax.axis_size("seq") != 4:
        return lax.psum(value.astype(BF), "seq").astype(F32)
    return seq_third(seq_second(seq_first(value)))


def by_distance(parts, place):
    shape = parts.shape
    bit = 1
    while bit < shape[0]:
        paired = parts.reshape((shape[0] // (2 * bit), 2, bit) + shape[1:])
        parts = jnp.where((place & bit) != 0, paired[:, ::-1], paired).reshape(shape)
        bit *= 2
    return parts


def swap(parts):
    return [parts[0]] + [hop(parts[distance], "seq", distance) for distance in range(1, len(parts))]


def on_device(
    tokens, norm_gain, norm_bias, attn_qkv, attn_qv_bias, attn_out, attn_out_bias,
    mlp_in, mlp_in_bias, mlp_out, mlp_out_bias, threshold, cotangent,
):
    clip_count, local_len, _ = tokens.shape
    seq, shards = lax.axis_size("seq"), lax.axis_size("fsdp")
    me = lax.axis_index("fsdp")
    frames = local_len // PATCHES
    width = PATCHES // seq
    own_rows = D // shards
    ff = mlp_in.shape[1]
    split_shape = (seq, frames, width, D)
    tok = tokens.reshape(local_len, D)
    cot = jnp.swapaxes(cotangent.reshape(frames, seq, width, D), 0, 1)
    by_chip = shards == 8

    attn_own = [jnp.concatenate([attn_qkv[a], attn_out[a]], axis=1) for a in range(2)]
    small = jnp.concatenate([
        norm_gain, norm_bias, attn_out_bias, mlp_out_bias.reshape(1, own_rows), attn_qv_bias.reshape(-1, own_rows),
        mlp_in_bias.reshape(-1, own_rows),
    ])
    place = lax.axis_index("seq")
    half = own_rows // 2
    ff_rows = ff // D
    if by_chip:
        slot = me ^ jnp.arange(shards, dtype=jnp.int32)
        low, high = attn_own[0][:half], attn_own[0][half:]
        near_x, near_y = jnp.stack([low, over_x(low)]), jnp.stack([high, over_y(high)])
        core_x, core_y = over_core(near_x), over_core(near_y)
        core_x, core_y, small = tie((core_x, core_y, small))
        small = jnp.stack([small, over_x(small), over_y(small), hop(small, "fsdp", CHIP_X | CHIP_Y)])
        far_x, far_y = over_y(near_x), over_x(near_y)
        small = jnp.stack([small, over_core(small)], axis=1).reshape((shards,) + small.shape[1:])
        small = by_distance(small, me)
        low, high = attn_own[1][:half], attn_own[1][half:]
        first_x, first_y, first_out = jnp.concatenate([low, mlp_in]), high, mlp_out
        far_x, far_y, core_x, core_y, first_x, first_y, first_out = tie(
            (far_x, far_y, core_x, core_y, first_x, first_y, first_out)
        )
        first_x, first_y, first_out = over_x(first_x), over_y(first_y), over_y(first_out)
        space_w = [near_x, far_x, near_y, far_y, core_x, over_core(far_x), core_y, over_core(far_y)]
        places = ((0, CHIP_X), (CHIP_Y, CHIP_X | CHIP_Y), (0, CHIP_Y), (CHIP_X, CHIP_X | CHIP_Y))
        attn_plan, in_plan, out_plan, out_rows = [], [], [], mlp_out.shape[0]
        for array in range(8):
            shift, lower = (0 if array < 4 else CORE), array % 4 < 2
            for index, owner in enumerate(places[array % 4]):
                owner = owner ^ shift
                attn_plan.append((array, index, 0, 0, half, 4 * D, owner, own_rows, 0 if lower else half, 0))
                array_of = array % 2 + (0 if array < 4 else 2)
                if lower:
                    in_plan.append((array_of, index, 0, 0, own_rows, ff, owner, own_rows, 0, 0))
                else:
                    out_plan.append((array_of, index, 0, 0, out_rows, D, owner, out_rows, 0, 0))
        in_targets, out_targets = targets_of(own_rows, ff, X_ORDER), targets_of(out_rows, D, Y_ORDER)
        in_shapes, out_shapes = [((4, own_rows, ff), BF)] * 2, [((4, out_rows, D), BF)] * 2
        attn_targets = [
            (side, 4 * lower + chip, 0, 0, half, 4 * D, (X_ORDER, Y_ORDER)[lower][chip] ^ shift, own_rows, lower * half, 0)
            for side, shift in enumerate((0, CORE)) for lower in range(2) for chip in range(4)
        ]
        attn_shapes = [((8, half, 4 * D), BF)] * 2
    else:
        slot = jnp.zeros((1,), jnp.int32)
        small = lax.all_gather(small, "fsdp", axis=0)
        space_w, attn_plan = gather_plain(attn_own[0])
        time_w, _ = gather_plain(attn_own[1])
        in_w, in_plan = gather_plain(mlp_in)
        out_w, _ = gather_plain(mlp_out)
        out_plan = [(0, 0, row, 0, FF_BLOCK, D, 0, 0, row, 0) for row in range(0, ff, FF_BLOCK)]
        in_targets, out_targets = plain_plan(D, ff), out_plan
        in_shapes, out_shapes = [((1, D, ff), BF)], [((1, ff, D), BF)]
        attn_targets, attn_shapes = plain_plan(D, 4 * D), [((1, D, 4 * D), BF)]
    slot = jnp.concatenate([slot, place[None]])
    small = small.astype(F32)
    turned = by_distance(cot, place)
    gy = [turned[distance] for distance in range(seq)]

    def spread(first, count, inner):
        rows = small[:, first : first + count * inner].reshape(shards, count, inner, own_rows)
        return jnp.swapaxes(rows, 0, 1).reshape(count, shards * inner * own_rows)

    vectors = spread(0, 9, 1)
    qv, inb = spread(9, 2, 2), spread(13, 1, ff_rows)

    state = [
        ((ROWS, D), BF), ((ROWS, 3 * D), BF), ((BLOCKS * PAIRS, 2 * CHUNK, CHUNK), BF), ((ROWS, D), BF), ((8, 128), F32),
    ]
    shares = [(split_shape[1:], BF)] * seq
    weight = ((D, 4 * D), BF)
    stripes = ((D // 128, ROWS, 128), F32)
    attn_flops = 2 * ROWS * D * 4 * D + 4 * BLOCKS * H * CHUNK * CHUNK * HD
    line = lambda cols: ((1, cols), F32)

    *parts, na0, proj0, soft0, ctx0, peak0 = call(
        functools.partial(space_forward_kernel, attn_plan, seq), shares + state, [((ROWS, D), F32), weight],
        attn_flops, slot, (tok, vectors, qv), space_w, sems=(len(attn_plan),), name="space_forward",
    )
    parts = swap(parts)
    if by_chip:
        na0, first_x, first_y, first_out = tie((na0, first_x, first_y, first_out))
        near_x, near_y = jnp.stack([low, first_x[:half]]), jnp.stack([high, first_y])
        far_x, far_y = over_y(near_x), over_x(near_y)
        in_near, out_near = jnp.stack([mlp_in, first_x[half:]]), jnp.stack([mlp_out, first_out])
        parts, near_x, near_y, far_x, far_y, in_near, out_near = tie((parts, near_x, near_y, far_x, far_y, in_near, out_near))
        time_w = [near_x, far_x, near_y, far_y] + [over_core(piece) for piece in (near_x, far_x, near_y, far_y)]
        in_far, out_far = over_y(in_near), over_x(out_near)
        parts, gy = tie((parts, gy))
    gy = swap(gy)
    x1, x2, na1, proj1, soft1, ctx1, peak1 = call(
        functools.partial(time_forward_kernel, attn_plan, seq), [((ROWS, D), F32), ((ROWS, D), F32)] + state,
        [stripes, weight], attn_flops, slot, [vectors, qv] + parts, time_w, sems=(len(attn_plan),), name="time_forward",
    )
    if by_chip:
        in_core, out_core = over_core(in_near), over_core(out_near)
        x2, gy, in_core, out_core = tie((x2, gy, in_core, out_core))
        in_w = [in_near, in_far, in_core, over_core(in_far)]
        out_w = [out_near, out_far, out_core, over_core(out_far)]

    ginb, g_moutb, *results = call(
        functools.partial(mlp_kernel, seq, in_plan, out_plan, in_targets, out_targets),
        [line(ff), line(D)] + shares + [((ROWS, D), F32), line(D), line(D)],
        [((ROWS, D), BF)] * 2 + [((ROWS, D), F32)] * 2 + [stripes] + [((D, ff), BF), ((ff, D), BF)] * 2,
        10 * ROWS * D * ff, slot, [x2, vectors, inb] + gy, in_w + out_w, in_shapes + out_shapes,
        ((ff // FF_BLOCK, len(in_plan)), len(out_plan), (ff // FF_BLOCK, len(in_targets)), len(out_targets)), name="mlp",
    )
    mixed, (g2, ggain2, gshift2, *mlp_grads) = results[:seq], results[seq:]
    in_grads, out_grads = mlp_grads[: len(in_shapes)], mlp_grads[len(in_shapes) :]

    if by_chip:
        (in_keep, in_send), (out_keep, out_send) = in_grads, out_grads
        in_got, out_got = over_core(in_send), over_core(out_send)
        in_pair, out_pair = pair_of(in_keep, in_got, 0), pair_of(out_keep, out_got, 0)
        g2, in_pair, out_pair, mixed = tie((g2, in_pair, out_pair, mixed))
        in_came, out_came = over_x(in_pair), over_y(out_pair)
    mixed = swap(mixed)
    *parts, gproj1, gbr1, g_outb1, g_qv1, ggain1, gshift1 = call(
        functools.partial(time_backward_kernel, attn_plan, seq),
        shares + [((ROWS, 3 * D), BF), ((ROWS, D), BF), line(D), line(2 * D), line(D), line(D)],
        [((ROWS, D), BF), stripes, weight], 2 * attn_flops,
        slot, (g2, x1, vectors, proj1, soft1), time_w, sems=(len(attn_plan),), name="time_backward",
    )
    if by_chip:
        parts, mixed = tie((parts, mixed))
    parts = swap(parts)
    time_grads = call(
        functools.partial(weight_grad_kernel, attn_targets), [], [weight], attn_flops,
        slot, (na1, gproj1, ctx1, gbr1), (), attn_shapes, (len(attn_targets),), name="time_weight_grad",
    )
    if by_chip:
        time_keep, time_send = time_grads
        in_rest, out_rest = rest_of(in_keep, in_got, 0, in_came), rest_of(out_keep, out_got, 0, out_came)
        parts, time_send, in_rest, out_rest = tie((parts, time_send, in_rest, out_rest))
        time_got = over_core(time_send)
        in_last, out_last = over_y(in_rest), over_x(out_rest)
        time_pairs = pair_of(time_keep, time_got, 0), pair_of(time_keep, time_got, 4)
        soft0, time_pairs = tie((soft0, time_pairs))
        time_came = over_x(time_pairs[0]), over_y(time_pairs[1])
    g1, gproj0, g_outb0, g_qv0, *space_grads = call(
        functools.partial(space_backward_kernel, attn_plan, attn_targets, seq),
        [((ROWS, D), F32), ((ROWS, 3 * D), BF), line(D), line(2 * D)],
        [((ROWS, D), BF), ((ROWS, D), BF), weight, weight], 2 * attn_flops,
        slot, [na0, ctx0, proj0, soft0] + parts, space_w, attn_shapes, (len(attn_plan), len(attn_targets)),
        name="space_backward",
    )
    if by_chip:
        space_keep, space_send = space_grads
        space_send, time_came, in_last, out_last = tie((space_send, time_came, in_last, out_last))
        space_got = over_core(space_send)
        mlp_total = jnp.concatenate([
            own_of(in_keep, in_got, 0, in_came, in_last), pack_rows(own_of(out_keep, out_got, 0, out_came, out_last)),
        ])
        time_rests = rest_of(time_keep, time_got, 0, time_came[0]), rest_of(time_keep, time_got, 4, time_came[1])
        space_pairs = pair_of(space_keep, space_got, 0), pair_of(space_keep, space_got, 4)
        g1, mlp_total, time_rests, space_pairs = tie((g1, mlp_total, time_rests, space_pairs))
        mlp_part = seq_first(mlp_total)
        time_lasts = over_y(time_rests[0]), over_x(time_rests[1])
        space_came = over_x(space_pairs[0]), over_y(space_pairs[1])
    g_tok, ggain0, gshift0 = call(
        functools.partial(space_input_kernel, attn_plan), [((local_len, D), F32), line(D), line(D)],
        [((ROWS, D), F32), weight], attn_flops,
        slot, (tok, g1, vectors, gproj0), space_w, sems=(len(attn_plan),), name="space_input",
    )

    def gathered(value, inner):
        count = value.shape[0]
        return jnp.swapaxes(value.reshape(count, shards, inner, own_rows), 0, 1).reshape(shards, count * inner, own_rows)

    if by_chip:
        (ggain0, ggain1, ggain2, gshift0, gshift1, gshift2, g_outb0, g_outb1, g_moutb, g_qv0, g_qv1, ginb, mlp_part) = tie(
            (ggain0, ggain1, ggain2, gshift0, gshift1, gshift2, g_outb0, g_outb1, g_moutb, g_qv0, g_qv1, ginb, mlp_part)
        )
        mlp_part = seq_second(mlp_part)
        ggain0, time_lasts, space_came = tie((ggain0, time_lasts, space_came))
    small_grads = jnp.concatenate([
        gathered(jnp.concatenate([ggain0, ggain1, ggain2, gshift0, gshift1, gshift2, g_outb0, g_outb1, g_moutb]), 1),
        gathered(jnp.concatenate([g_qv0, g_qv1]), 2), gathered(ginb, ff_rows),
    ], axis=1)
    peaks = jnp.concatenate([peak0[0:1], peak1[0:1]], axis=1)
    mine = (jnp.arange(shards * seq) == me * seq + place)[:, None]
    peaks = jnp.where(mine, peaks, 0.0).reshape(-1, 128)
    small_grads = jnp.concatenate([small_grads.reshape(-1, 128), peaks])
    if by_chip:
        space_rests = rest_of(space_keep, space_got, 0, space_came[0]), rest_of(space_keep, space_got, 4, space_came[1])
        space_lasts = over_y(space_rests[0]), over_x(space_rests[1])
        time_total = jnp.concatenate([
            own_of(time_keep, time_got, 0, time_came[0], time_lasts[0]), own_of(time_keep, time_got, 4, time_came[1], time_lasts[1]),
        ])
        time_part = seq_first(time_total)
        small_grads = small_grads + over_core(small_grads)
        space_lasts, time_part, mlp_part, small_grads = tie((space_lasts, time_part, mlp_part, small_grads))
        space_total = jnp.concatenate([
            own_of(space_keep, space_got, 0, space_came[0], space_lasts[0]),
            own_of(space_keep, space_got, 4, space_came[1], space_lasts[1]),
        ])
        space_part = seq_first(space_total)
        small_grads = small_grads + over_x(small_grads)
        small_grads = small_grads + over_y(small_grads)
        time_part = seq_second(time_part)
        space_part, small_grads, mlp_part = tie((space_part, small_grads, mlp_part))
        space_part = seq_second(space_part)
        small_grads = small_grads + hop(small_grads, "seq", 1)
        mlp_total = seq_third(mlp_part)
        space_part, time_part, small_grads = tie((space_part, time_part, small_grads))
        small_grads = small_grads + hop(small_grads, "seq", 2)
        grad_in, grad_mout = mlp_total[:own_rows], unpack_rows(mlp_total[own_rows:])
        attn_totals = [seq_third(space_part), seq_third(time_part)]
    else:
        small_grads = lax.psum(small_grads, ("fsdp", "seq"))
        (in_grads,), (out_grads,) = in_grads, out_grads
        in_total, out_total, time_total, space_total = (
            reduce_plain(value) for value in (in_grads, out_grads, time_grads[0], space_grads[0])
        )
        grad_in, grad_mout = seq_total(in_total), seq_total(out_total)
        attn_totals = [seq_total(space_total), seq_total(time_total)]
    grad_qkv = jnp.stack([value[:, : 3 * D] for value in attn_totals])
    grad_out = jnp.stack([value[:, 3 * D :] for value in attn_totals])

    peaks = small_grads[-peaks.shape[0] :].reshape(shards * seq, 2, 128)
    logit_max = jnp.max(peaks, axis=0)[:, :H]
    small_grads = small_grads[: -2 * shards * seq].reshape(shards, -1, own_rows)
    small_grads = lax.dynamic_index_in_dim(small_grads, me, 0, keepdims=False)
    grad_gain, grad_shift, grad_outb, grad_moutb = small_grads[0:3], small_grads[3:6], small_grads[6:8], small_grads[8]
    grad_qv = small_grads[9:13].reshape(2, 2 * own_rows)
    grad_inb = small_grads[13:].reshape(ff_rows * own_rows)

    factor = threshold / jnp.maximum(logit_max, threshold)
    column_scale = jnp.repeat(jnp.sqrt(factor), HD, axis=1)
    clipped = attn_qkv[:, :, : 2 * D].astype(F32) * jnp.concatenate([column_scale, column_scale], axis=1)[:, None, :]
    mixed = jnp.swapaxes(by_distance(jnp.stack(mixed), place), 0, 1).reshape(tokens.shape)
    return (
        mixed, g_tok.reshape(tokens.shape), grad_gain, grad_shift, grad_qkv, grad_qv, grad_out, grad_outb,
        grad_in, grad_inb, grad_mout, grad_moutb, logit_max, clipped,
    )


def solution(mesh):
    placed = (
        P("fsdp", "seq", None), P(None, "fsdp"), P(None, "fsdp"), P(None, "fsdp", None), P(None, "fsdp"),
        P(None, "fsdp", None), P(None, "fsdp"), P("fsdp", None), P("fsdp"), P("fsdp", None), P("fsdp"), P(),
        P("fsdp", "seq", None),
    )
    return jax.shard_map(
        on_device,
        mesh=mesh,
        in_specs=placed,
        out_specs=(
            P("fsdp", "seq", None), P("fsdp", "seq", None), P(None, "fsdp"), P(None, "fsdp"), P(None, "fsdp", None),
            P(None, "fsdp"), P(None, "fsdp", None), P(None, "fsdp"), P("fsdp", None), P("fsdp"), P("fsdp", None),
            P("fsdp"), P(), P(None, "fsdp", None),
        ),
        check_vma=False,
    )
```

```python
import functools
import itertools

import jax
import jax.numpy as jnp
from jax import lax
from jax.experimental import pallas as pl
from jax.experimental.pallas import tpu as pltpu
from jax.sharding import PartitionSpec as P

H = 12
PATCHES = 196
HD = 64
D = 768
PAIRS = H // 2
CHUNK = 208
BLOCKS = 2
ROWS = BLOCKS * CHUNK
FF_BLOCK = 768
EPSILON = 1e-06
NEGATIVE = -1e30
SCALE = HD ** (-0.5)
COST, COVER = 1000, 40 * 2**20
VMEM_LIMIT = 58 * 1024 * 1024
BF = jnp.bfloat16
F32 = jnp.float32


def mm(a, b):
    return lax.dot_general(a, b, (((1,), (0,)), ((), ())), preferred_element_type=F32)


def mm_nt(a, b):
    return lax.dot_general(a, b, (((1,), (1,)), ((), ())), preferred_element_type=F32)


def mm_tn(a, b):
    return lax.dot_general(a, b, (((0,), (0,)), ((), ())), preferred_element_type=F32)


def row_stats(rows):
    centre = jnp.mean(rows, axis=-1, keepdims=True)
    centred = rows - centre
    second = jnp.mean(centred * centred, axis=-1, keepdims=True)
    inverse = lax.rsqrt(second + EPSILON)
    return centred * inverse, inverse


def norm_backward(grad, unit, inverse, gain):
    weighted = grad * gain
    first = jnp.mean(weighted, axis=-1, keepdims=True)
    second = jnp.mean(weighted * unit, axis=-1, keepdims=True)
    return (weighted - first - unit * second) * inverse


def column_sum(values):
    return jnp.sum(values.astype(F32), axis=0, keepdims=True)


def masks(temporal, block, frames):
    row = lax.broadcasted_iota(jnp.int32, (2 * CHUNK, CHUNK), 0)
    col = lax.broadcasted_iota(jnp.int32, (2 * CHUNK, CHUNK), 1)
    if temporal:
        row = jnp.where(row >= CHUNK, row - CHUNK, row)
        allowed = (row // frames) == (col // frames)
    else:
        allowed = col < PATCHES
    return allowed


def lower_lanes(rows):
    return lax.broadcasted_iota(jnp.int32, (rows, 2 * HD), 1) < HD


def split_heads(pair, scale=None):
    low_half = lower_lanes(pair.shape[0])
    if scale is not None:
        pair = pair * jnp.asarray(scale, pair.dtype)
    zero = jnp.zeros_like(pair)
    return jnp.where(low_half, pair, zero), jnp.where(low_half, zero, pair)


def attend_forward(proj_ref, ctx_ref, soft_ref, peak_ref, temporal, frames, valid):
    lane = lax.broadcasted_iota(jnp.int32, (8, 128), 1)
    peaks = jnp.full((8, 128), NEGATIVE, F32)
    for block in range(BLOCKS):
        allowed = masks(temporal, block, frames)
        rows = slice(block * CHUNK, (block + 1) * CHUNK)
        row_id = lax.broadcasted_iota(jnp.int32, (CHUNK, 1), 0)
        for pair in range(PAIRS):
            cols = slice(pair * 128, pair * 128 + 128)
            q_a, q_b = split_heads(proj_ref[rows, cols], SCALE)
            keys = proj_ref[rows, D + pair * 128 : D + pair * 128 + 128]
            v_a, v_b = split_heads(proj_ref[rows, 2 * D + pair * 128 : 2 * D + pair * 128 + 128])
            scores = mm_nt(jnp.concatenate([q_a, q_b], axis=0), keys)
            scores = jnp.where(allowed, scores, NEGATIVE)
            top = jnp.max(scores, axis=1, keepdims=True)
            expo = jnp.exp(scores - top)
            total = jnp.sum(expo, axis=1, keepdims=True)
            soft = (expo / total).astype(BF)
            soft_ref[block * PAIRS + pair] = soft
            ctx_ref[rows, cols] = (mm(soft[:CHUNK], v_a) + mm(soft[CHUNK:], v_b)).astype(BF)
            for side in range(2):
                seen = jnp.where(row_id < valid[block], top[side * CHUNK : (side + 1) * CHUNK], NEGATIVE)
                best = jnp.max(seen, axis=0, keepdims=True)
                peaks = jnp.where(lane == 2 * pair + side, jnp.maximum(peaks, best), peaks)
    peak_ref[...] = peaks


def attend_backward(proj_ref, soft_ref, gctx_ref, gproj_ref):
    for block in range(BLOCKS):
        rows = slice(block * CHUNK, (block + 1) * CHUNK)
        for pair in range(PAIRS):
            cols = slice(pair * 128, pair * 128 + 128)
            kcols = slice(D + pair * 128, D + pair * 128 + 128)
            vcols = slice(2 * D + pair * 128, 2 * D + pair * 128 + 128)
            q_pair = jnp.concatenate(split_heads(proj_ref[rows, cols], SCALE), axis=0)
            k_a, k_b = split_heads(proj_ref[rows, kcols], SCALE)
            values = proj_ref[rows, vcols]
            g_pair = jnp.concatenate(split_heads(gctx_ref[rows, cols]), axis=0)
            soft_low = soft_ref[block * PAIRS + pair]
            soft = soft_low.astype(F32)
            grad_soft = mm_nt(g_pair, values)
            inner = jnp.sum(soft * grad_soft, axis=1, keepdims=True)
            grad_scores = (soft * (grad_soft - inner)).astype(BF)
            gproj_ref[rows, cols] = (mm(grad_scores[:CHUNK], k_a) + mm(grad_scores[CHUNK:], k_b)).astype(BF)
            gproj_ref[rows, kcols] = mm_tn(grad_scores, q_pair).astype(BF)
            gproj_ref[rows, vcols] = mm_tn(soft_low, g_pair).astype(BF)


def blocks_between(slot_ref, arrays, plan, weight_ref):
    for array, index, row, column, height, width, place, scale, first, at in plan:
        start = pl.multiple_of(slot_ref[place] * scale + first, 16)
        yield (
            arrays[array].at[index, row : row + height, column : column + width],
            weight_ref.at[pl.ds(start, height), at : at + width],
        )


def fetch(slot_ref, pieces, plan, weight_ref, sems):
    copies = []
    for number, (piece, part) in enumerate(blocks_between(slot_ref, pieces, plan, weight_ref)):
        copies.append(pltpu.make_async_copy(piece, part, sems.at[number]))
        copies[-1].start()
    return copies


def deliver(slot_ref, weight_ref, targets, plan, sems):
    copies = []
    for number, (piece, part) in enumerate(blocks_between(slot_ref, targets, plan, weight_ref)):
        copies.append(pltpu.make_async_copy(part, piece, sems.at[number]))
        copies[-1].start()
    return copies


def take(refs, plan):
    count = 1 + max(entry[0] for entry in plan)
    return refs[:count], refs[count:]


def finish(copies):
    for copy in copies:
        copy.wait()


def project(na_ref, qkv_ref, qv, proj_ref):
    for part in range(3):
        cols = slice(part * D, (part + 1) * D)
        value = mm(na_ref[...], qkv_ref[:, cols])
        if part != 1:
            at = 0 if part == 0 else D
            value = value + qv[:, at : at + D]
        proj_ref[:, cols] = value.astype(BF)


def pad_frames(tok_ref, rows_ref):
    count = tok_ref.shape[0]
    flat = tok_ref[...].astype(F32)
    rows_ref[0:count, :] = flat
    rows_ref[CHUNK : CHUNK + PATCHES, :] = flat[PATCHES:, :]
    rows_ref[PATCHES:CHUNK, :] = jnp.zeros((CHUNK - PATCHES, D), F32)
    rows_ref[CHUNK + PATCHES :, :] = jnp.zeros((CHUNK - PATCHES, D), F32)


def space_forward_kernel(plan, seq, slot_ref, tok_ref, vec_ref, qv_ref, *refs):
    pieces, refs = take(refs, plan)
    part_refs, refs = refs[:seq], refs[seq:]
    na_ref, proj_ref, soft_ref, ctx_ref, peak_ref, rows_ref, weight_ref, sems = refs
    copies = fetch(slot_ref, pieces, plan, weight_ref, sems)
    pad_frames(tok_ref, rows_ref)
    unit, _ = row_stats(rows_ref[...])
    na_ref[...] = (unit * vec_ref[0:1] + vec_ref[3:4]).astype(BF)
    finish(copies)
    project(na_ref, weight_ref, qv_ref[0:1], proj_ref)
    attend_forward(proj_ref, ctx_ref, soft_ref, peak_ref, False, 0, (PATCHES, PATCHES))
    rows_ref[...] = rows_ref[...] + mm(ctx_ref[...], weight_ref[:, 3 * D :]) + vec_ref[6:7]
    frames, width = part_refs[0].shape[0], part_refs[0].shape[1]

    def body(place):
        for distance in range(seq):
            for frame in range(frames):
                start = frame * CHUNK + (place ^ distance) * width
                part_refs[distance][frame] = rows_ref[start : start + width, :].astype(BF)

    for_place(slot_ref, seq, body)


def for_place(slot_ref, count, body):
    for place in range(count):
        pl.when(slot_ref[slot_ref.shape[0] - 1] == place)(functools.partial(body, place))


def interleave(slot_ref, part_refs, stripes_ref, rows_ref):
    shares, frames, width = len(part_refs), part_refs[0].shape[0], part_refs[0].shape[1]
    total = shares * frames
    place = 0 if slot_ref is None else slot_ref[slot_ref.shape[0] - 1]
    for stripe in range(D // 128):
        cols = slice(stripe * 128, stripe * 128 + 128)
        for distance in range(shares):
            for frame in range(frames):
                first = (place ^ distance) * frames + frame
                stripes_ref[stripe, pl.ds(first, width, stride=total), :] = part_refs[distance][frame, :, cols].astype(F32)
        stripes_ref[stripe, total * width :, :] = jnp.zeros((ROWS - total * width, 128), F32)
        rows_ref[:, cols] = stripes_ref[stripe].astype(rows_ref.dtype)


def separate(slot_ref, rows, stripes_ref, part_refs):
    shares, frames, width = len(part_refs), part_refs[0].shape[0], part_refs[0].shape[1]
    total = shares * frames
    place = slot_ref[slot_ref.shape[0] - 1]
    for stripe in range(D // 128):
        cols = slice(stripe * 128, stripe * 128 + 128)
        stripes_ref[stripe] = rows[:, cols]
        for distance in range(shares):
            for frame in range(frames):
                first = (place ^ distance) * frames + frame
                part_refs[distance][frame, :, cols] = stripes_ref[stripe, pl.ds(first, width, stride=total), :].astype(
                    part_refs[distance].dtype
                )


def time_forward_kernel(plan, seq, slot_ref, vec_ref, qv_ref, *refs):
    part_refs, refs = refs[:seq], refs[seq:]
    pieces, refs = take(refs, plan)
    x1_ref, x2_ref, na_ref, proj_ref, soft_ref, ctx_ref, peak_ref, stripes_ref, weight_ref, sems = refs
    copies = fetch(slot_ref, pieces, plan, weight_ref, sems)
    frames = seq * part_refs[0].shape[0]
    count = frames * part_refs[0].shape[1]
    interleave(slot_ref, part_refs, stripes_ref, x1_ref)
    unit, _ = row_stats(x1_ref[...])
    na_ref[...] = (unit * vec_ref[1:2] + vec_ref[4:5]).astype(BF)
    finish(copies)
    project(na_ref, weight_ref, qv_ref[1:2], proj_ref)
    attend_forward(proj_ref, ctx_ref, soft_ref, peak_ref, True, frames, (CHUNK, count - CHUNK))
    x2_ref[...] = x1_ref[...] + mm(ctx_ref[...], weight_ref[:, 3 * D :]) + vec_ref[7:8]


def mlp_kernel(seq, in_plan, out_plan, in_targets, out_targets, slot_ref, x2_ref, vec_ref, inb_ref, gy_ref, *refs):
    in_pieces, refs = take(refs, in_plan)
    out_pieces, refs = take(refs, out_plan)
    sums_ref, *refs = refs
    mixed_refs, refs = refs[:seq], refs[seq:]
    g2_ref, *refs = refs
    gin_arrays, refs = take(refs, in_targets)
    gout_arrays, refs = take(refs, out_targets)
    (
        n2_ref, gyl_ref, rows_ref, back_ref, stripes_ref, in_ref, out_ref, gin_ref, gout_ref,
        in_sems, out_sems, gin_sems, gout_sems,
    ) = refs
    blocks = in_ref.shape[1] // FF_BLOCK
    out_height = out_plan[0][4]
    rows_each = FF_BLOCK // out_height

    def span_of(step):
        return pl.ds(pl.multiple_of(step * FF_BLOCK, FF_BLOCK), FF_BLOCK)

    def in_copies(step):
        return [
            pltpu.make_async_copy(piece.at[:, span_of(step)], part.at[:, span_of(step)], in_sems.at[step, number])
            for number, (piece, part) in enumerate(blocks_between(slot_ref, in_pieces, in_plan, in_ref))
        ]

    def gin_copies(step):
        return [
            pltpu.make_async_copy(part.at[:, span_of(step)], piece.at[:, span_of(step)], gin_sems.at[step, number])
            for number, (piece, part) in enumerate(blocks_between(slot_ref, gin_arrays, in_targets, gin_ref))
        ]

    def first_row(entry):
        return slot_ref[entry[6]] * entry[7] + entry[8]

    for step in range(blocks):
        for copy in in_copies(step):
            copy.start()
        if step == 0:
            for entry, (piece, part) in zip(out_plan, blocks_between(slot_ref, out_pieces, out_plan, out_ref)):
                pltpu.make_async_copy(piece, part, out_sems.at[first_row(entry) // out_height]).start()
    unit, _ = row_stats(x2_ref[...])
    n2_ref[...] = (unit * vec_ref[2:3] + vec_ref[5:6]).astype(BF)
    interleave(None, [gy_ref.at[share] for share in range(seq)], stripes_ref, gyl_ref)
    sums_ref[2:3] = column_sum(gyl_ref[...])
    rows_ref[...] = jnp.zeros_like(rows_ref)
    back_ref[...] = jnp.zeros_like(back_ref)
    gout_copies = [
        pltpu.make_async_copy(part, piece, gout_sems.at[number])
        for number, (piece, part) in enumerate(blocks_between(slot_ref, gout_arrays, out_targets, gout_ref))
    ]

    @pl.loop(0, blocks)
    def _(step):
        span = span_of(step)
        for copy in in_copies(step):
            copy.wait()
        for number in range(rows_each):
            part = out_ref.at[0:out_height, :]
            pltpu.make_async_copy(part, part, out_sems.at[step * rows_each + number]).wait()
        hidden = mm(n2_ref[...], in_ref[:, span]) + inb_ref[:, span]
        cumulative = 0.5 * (1.0 + lax.erf(hidden * (2.0 ** -0.5)))
        act = (hidden * cumulative).astype(BF)
        slope = cumulative + hidden * jnp.exp(-0.5 * hidden * hidden) * 0.3989422804014327
        rows_ref[...] += mm(act, out_ref[span, :])
        gout_ref[span, :] = mm_tn(act, gyl_ref[...]).astype(BF)
        for copy, entry in zip(gout_copies, out_targets):
            pl.when(first_row(entry) // FF_BLOCK == step)(copy.start)
        ghid = (mm_nt(gyl_ref[...], out_ref[span, :]) * slope).astype(BF)
        sums_ref[pl.ds(3 + step, 1), :] = column_sum(ghid)
        gin_ref[:, span] = mm_tn(n2_ref[...], ghid).astype(BF)
        for copy in gin_copies(step):
            copy.start()
        back_ref[...] += mm_nt(ghid, in_ref[:, span])

    separate(slot_ref, x2_ref[...] + rows_ref[...] + vec_ref[8:9], stripes_ref, mixed_refs)
    unit, inverse = row_stats(x2_ref[...])
    grad = back_ref[...]
    sums_ref[0:1] = column_sum(grad * unit)
    sums_ref[1:2] = column_sum(grad)
    sums_ref[7:8] = jnp.zeros((1, D), F32)
    g2_ref[...] = gyl_ref[...].astype(F32) + norm_backward(grad, unit, inverse, vec_ref[2:3])
    for step in range(blocks):
        finish(gin_copies(step))
    finish(gout_copies)


def branch_backward(g_ref, proj_ref, soft_ref, weight_ref, sums_ref, gproj_ref, gbr_ref, gctx_ref):
    gbr_ref[...] = g_ref[...].astype(BF)
    sums_ref[2:3] = column_sum(gbr_ref[...])
    gctx_ref[...] = mm_nt(gbr_ref[...], weight_ref[:, 3 * D :]).astype(BF)
    attend_backward(proj_ref, soft_ref, gctx_ref, gproj_ref)
    sums_ref[3:4] = column_sum(gproj_ref[:, 0:D])
    sums_ref[4:5] = column_sum(gproj_ref[:, 2 * D :])
    sums_ref[5:8] = jnp.zeros((3, D), F32)


def projection_backward(gproj_ref, weight_ref):
    total = mm_nt(gproj_ref[:, 0:D], weight_ref[:, 0:D])
    for part in range(1, 3):
        cols = slice(part * D, (part + 1) * D)
        total = total + mm_nt(gproj_ref[:, cols], weight_ref[:, cols])
    return total


def weight_grads(na_ref, gproj_ref, ctx_ref, gbr_ref, grad_ref):
    grad_ref[:, 3 * D :] = mm_tn(ctx_ref[...], gbr_ref[...]).astype(BF)
    for part in range(3):
        cols = slice(part * D, (part + 1) * D)
        grad_ref[:, cols] = mm_tn(na_ref[...], gproj_ref[:, cols]).astype(BF)


def time_backward_kernel(plan, seq, slot_ref, g_ref, x1_ref, vec_ref, proj_ref, soft_ref, *refs):
    pieces, refs = take(refs, plan)
    part_refs, refs = refs[:seq], refs[seq:]
    gproj_ref, gbr_ref, sums_ref, gctx_ref, stripes_ref, weight_ref, sems = refs
    finish(fetch(slot_ref, pieces, plan, weight_ref, sems))
    branch_backward(g_ref, proj_ref, soft_ref, weight_ref, sums_ref, gproj_ref, gbr_ref, gctx_ref)
    grad = projection_backward(gproj_ref, weight_ref)
    unit, inverse = row_stats(x1_ref[...])
    sums_ref[0:1] = column_sum(grad * unit)
    sums_ref[1:2] = column_sum(grad)
    separate(slot_ref, g_ref[...] + norm_backward(grad, unit, inverse, vec_ref[1:2]), stripes_ref, part_refs)


def weight_grad_kernel(targets, slot_ref, na_ref, gproj_ref, ctx_ref, gbr_ref, *refs):
    outs, (grad_ref, sems) = take(refs, targets)
    weight_grads(na_ref, gproj_ref, ctx_ref, gbr_ref, grad_ref)
    finish(deliver(slot_ref, grad_ref, outs, targets, sems))


def space_backward_kernel(
    plan, targets, seq, slot_ref, tok_ref, vec_ref, mlp_sums_ref, time_sums_ref, peaks_ref, na_ref, ctx_ref, proj_ref, soft_ref, *refs
):
    part_refs, refs = refs[:seq], refs[seq:]
    pieces, refs = take(refs, plan)
    gtok_ref, all_sums_ref, *refs = refs
    sums_ref = all_sums_ref.at[16:24]
    outs, refs = take(refs, targets)
    g_ref, gproj_ref, gbr_ref, gctx_ref, weight_ref, grad_ref, sems, grad_sems = refs
    copies = fetch(slot_ref, pieces, plan, weight_ref, sems)
    frames, width = part_refs[0].shape[0], part_refs[0].shape[1]

    def body(place):
        for frame in range(frames):
            for distance in range(seq):
                start = frame * CHUNK + (place ^ distance) * width
                g_ref[start : start + width, :] = part_refs[distance][frame].astype(F32)

    for_place(slot_ref, seq, body)
    all_sums_ref[0:8] = mlp_sums_ref[...]
    all_sums_ref[8:16] = time_sums_ref[...]
    all_sums_ref[24:] = peaks_ref[...]
    for frame in range(frames):
        g_ref[frame * CHUNK + PATCHES : (frame + 1) * CHUNK, :] = jnp.zeros((CHUNK - PATCHES, D), F32)
    finish(copies)
    branch_backward(g_ref, proj_ref, soft_ref, weight_ref, sums_ref, gproj_ref, gbr_ref, gctx_ref)
    weight_grads(na_ref, gproj_ref, ctx_ref, gbr_ref, grad_ref)
    copies = deliver(slot_ref, grad_ref, outs, targets, grad_sems)
    grad = projection_backward(gproj_ref, weight_ref)
    total = g_ref[...]
    pad_frames(tok_ref, g_ref)
    unit, inverse = row_stats(g_ref[...])
    sums_ref[0:1] = column_sum(grad * unit)
    sums_ref[1:2] = column_sum(grad)
    g_ref[...] = total + norm_backward(grad, unit, inverse, vec_ref[0:1])
    gtok_ref[0:PATCHES, :] = g_ref[0:PATCHES, :]
    gtok_ref[PATCHES:, :] = g_ref[CHUNK : CHUNK + PATCHES, :]
    finish(copies)


def call(kernel, outs, scratch, flops, slot, operands, pieces=(), targets=(), sems=(), *, name, cost=COST):
    whole = pl.BlockSpec(memory_space=pltpu.VMEM)
    far = pl.BlockSpec(memory_space=pl.ANY)
    return pl.pallas_call(
        kernel,
        in_specs=[pl.BlockSpec(memory_space=pltpu.SMEM)] + [whole] * len(operands) + [far] * len(pieces),
        out_specs=[whole] * len(outs) + [far] * len(targets),
        out_shape=[jax.ShapeDtypeStruct(shape, dtype) for shape, dtype in list(outs) + list(targets)],
        scratch_shapes=[pltpu.VMEM(shape, dtype) for shape, dtype in scratch]
        + [pltpu.SemaphoreType.DMA(count if isinstance(count, tuple) else (count,)) for count in sems],
        compiler_params=pltpu.CompilerParams(vmem_limit_bytes=VMEM_LIMIT),
        cost_estimate=pl.CostEstimate(flops=1000, bytes_accessed=cost, transcendentals=0),
        name=name,
    )(slot, *operands, *pieces)


def hop(value, axis, bit):
    return lax.ppermute(value, axis, [(index, index ^ bit) for index in range(lax.axis_size(axis))])


CORE, CHIP_X, CHIP_Y = 1, 2, 4
X_ORDER = (0, CHIP_Y, CHIP_X, CHIP_X | CHIP_Y)
Y_ORDER = (0, CHIP_X, CHIP_Y, CHIP_X | CHIP_Y)


def pack_rows(value):
    return jnp.concatenate(jnp.split(value, 4, axis=0), axis=1)


def unpack_rows(value):
    return jnp.concatenate(jnp.split(value, 4, axis=1), axis=0)


def targets_of(height, width, order):
    return [
        (side, chip, 0, 0, height, width, order[chip] ^ shift, height, 0, 0)
        for side, shift in enumerate((0, CORE)) for chip in range(4)
    ]


def gather_plain(own):
    full = lax.all_gather(own[None], "fsdp", axis=1, tiled=True)
    return [full], plain_plan(full.shape[1], full.shape[2])


def plain_plan(rows, columns):
    return [(0, 0, 0, 0, rows, columns, 0, 0, 0, 0)]


tie = lax.optimization_barrier


def sums_of(keep, got):
    return lambda part: keep[part].astype(F32) + got[part].astype(F32)


def pair_of(keep, got, first):
    return sums_of(keep, got)(slice(first + 2, first + 4)).astype(BF)


def rest_of(keep, got, first, came):
    return (sums_of(keep, got)(first + 1) + came[1].astype(F32)).astype(BF)


def own_of(keep, got, first, came, last):
    return sums_of(keep, got)(first) + came[0].astype(F32) + last.astype(F32)


def over_x(value):
    return hop(value, "fsdp", CHIP_X)


def over_y(value):
    return hop(value, "fsdp", CHIP_Y)


def over_core(value):
    return hop(value, "fsdp", CORE)


def reduce_plain(grad):
    return lax.psum_scatter(grad[0], "fsdp", scatter_dimension=0, tiled=True).astype(F32)


def seq_halves(value):
    odd = (lax.axis_index("seq") & 1) == 1
    half = value.shape[0] // 2
    low, high = value[:half], value[half:]
    return jnp.where(odd, high, low), jnp.where(odd, low, high).astype(BF)


def seq_first(value):
    mine, other = seq_halves(value)
    return (mine + hop(other, "seq", 1).astype(F32)).astype(BF)


def seq_second(part):
    return (part.astype(F32) + hop(part, "seq", 2).astype(F32)).astype(BF)


def seq_join(part, other):
    odd = (lax.axis_index("seq") & 1) == 1
    return jnp.where(odd, jnp.concatenate([other, part]), jnp.concatenate([part, other])).astype(F32)


def seq_total(value):
    if lax.axis_size("seq") != 4:
        return lax.psum(value.astype(BF), "seq").astype(F32)
    part = seq_second(seq_first(value))
    return seq_join(part, hop(part, "seq", 1))


def by_distance(parts, place):
    shape = parts.shape
    bit = 1
    while bit < shape[0]:
        paired = parts.reshape((shape[0] // (2 * bit), 2, bit) + shape[1:])
        parts = jnp.where((place & bit) != 0, paired[:, ::-1], paired).reshape(shape)
        bit *= 2
    return parts


def swap(parts):
    return [parts[0]] + [hop(parts[distance], "seq", distance) for distance in range(1, len(parts))]


def on_device(
    tokens, norm_gain, norm_bias, attn_qkv, attn_qv_bias, attn_out, attn_out_bias,
    mlp_in, mlp_in_bias, mlp_out, mlp_out_bias, threshold, cotangent,
):
    clip_count, local_len, _ = tokens.shape
    seq, shards = lax.axis_size("seq"), lax.axis_size("fsdp")
    me = lax.axis_index("fsdp")
    frames = local_len // PATCHES
    width = PATCHES // seq
    own_rows = D // shards
    ff = mlp_in.shape[1]
    split_shape = (seq, frames, width, D)
    tok = tokens.reshape(local_len, D)
    cot = jnp.swapaxes(cotangent.reshape(frames, seq, width, D), 0, 1)
    by_chip = shards == 8

    attn_own = [jnp.concatenate([attn_qkv[a], attn_out[a]], axis=1) for a in range(2)]
    small = jnp.concatenate([
        norm_gain, norm_bias, attn_out_bias, mlp_out_bias.reshape(1, own_rows), attn_qv_bias.reshape(-1, own_rows),
        mlp_in_bias.reshape(-1, own_rows),
    ])
    place = lax.axis_index("seq")
    half = own_rows // 2
    ff_rows = ff // D
    if by_chip:
        slot = me ^ jnp.arange(shards, dtype=jnp.int32)
        low, high = attn_own[0][:half], attn_own[0][half:]
        near_x, near_y = jnp.stack([low, over_x(low)]), jnp.stack([high, over_y(high)])
        core_x, core_y = over_core(near_x), over_core(near_y)
        core_x, core_y, small = tie((core_x, core_y, small))
        small = jnp.stack([small, over_x(small), over_y(small), hop(small, "fsdp", CHIP_X | CHIP_Y)])
        far_x, far_y = over_y(near_x), over_x(near_y)
        small = jnp.stack([small, over_core(small)], axis=1).reshape((shards,) + small.shape[1:])
        small = by_distance(small, me)
        low, high = attn_own[1][:half], attn_own[1][half:]
        first_x, first_y, first_out = jnp.concatenate([low, mlp_in]), high, mlp_out
        far_x, far_y, core_x, core_y, first_x, first_y, first_out = tie(
            (far_x, far_y, core_x, core_y, first_x, first_y, first_out)
        )
        first_x, first_y, first_out = over_x(first_x), over_y(first_y), over_y(first_out)
        space_w = [near_x, far_x, near_y, far_y, core_x, over_core(far_x), core_y, over_core(far_y)]
        places = ((0, CHIP_X), (CHIP_Y, CHIP_X | CHIP_Y), (0, CHIP_Y), (CHIP_X, CHIP_X | CHIP_Y))
        attn_plan, in_plan, out_plan, out_rows = [], [], [], mlp_out.shape[0]
        for array in range(8):
            shift, lower = (0 if array < 4 else CORE), array % 4 < 2
            for index, owner in enumerate(places[array % 4]):
                owner = owner ^ shift
                attn_plan.append((array, index, 0, 0, half, 4 * D, owner, own_rows, 0 if lower else half, 0))
                array_of = array % 2 + (0 if array < 4 else 2)
                if lower:
                    in_plan.append((array_of, index, 0, 0, own_rows, ff, owner, own_rows, 0, 0))
                else:
                    out_plan.append((array_of, index, 0, 0, out_rows, D, owner, out_rows, 0, 0))
        in_targets, out_targets = targets_of(own_rows, ff, X_ORDER), targets_of(out_rows, D, Y_ORDER)
        in_shapes, out_shapes = [((4, own_rows, ff), BF)] * 2, [((4, out_rows, D), BF)] * 2
        attn_targets = [
            (side, 4 * lower + chip, 0, 0, half, 4 * D, (X_ORDER, Y_ORDER)[lower][chip] ^ shift, own_rows, lower * half, 0)
            for side, shift in enumerate((0, CORE)) for lower in range(2) for chip in range(4)
        ]
        attn_shapes = [((8, half, 4 * D), BF)] * 2
    else:
        slot = jnp.zeros((1,), jnp.int32)
        small = lax.all_gather(small, "fsdp", axis=0)
        space_w, attn_plan = gather_plain(attn_own[0])
        time_w, _ = gather_plain(attn_own[1])
        in_w, in_plan = gather_plain(mlp_in)
        out_w, _ = gather_plain(mlp_out)
        out_plan = [(0, 0, row, 0, FF_BLOCK, D, 0, 0, row, 0) for row in range(0, ff, FF_BLOCK)]
        in_targets, out_targets = plain_plan(D, ff), out_plan
        in_shapes, out_shapes = [((1, D, ff), BF)], [((1, ff, D), BF)]
        attn_targets, attn_shapes = plain_plan(D, 4 * D), [((1, D, 4 * D), BF)]
    slot = jnp.concatenate([slot, place[None]])
    small = small.astype(F32)

    def spread(first, count, inner):
        rows = small[:, first : first + count * inner].reshape(shards, count, inner, own_rows)
        return jnp.swapaxes(rows, 0, 1).reshape(count, shards * inner * own_rows)

    vectors = spread(0, 9, 1)
    qv, inb = spread(9, 2, 2), spread(13, 1, ff_rows)
    vectors, qv, space_w = tie((vectors, qv, space_w))

    state = [
        ((ROWS, D), BF), ((ROWS, 3 * D), BF), ((BLOCKS * PAIRS, 2 * CHUNK, CHUNK), BF), ((ROWS, D), BF), ((8, 128), F32),
    ]
    shares = [(split_shape[1:], BF)] * seq
    weight = ((D, 4 * D), BF)
    stripes = ((D // 128, ROWS, 128), F32)
    attn_flops = 2 * ROWS * D * 4 * D + 4 * BLOCKS * H * CHUNK * CHUNK * HD
    sums = ((8, D), F32)

    *parts, na0, proj0, soft0, ctx0, peak0 = call(
        functools.partial(space_forward_kernel, attn_plan, seq), shares + state, [((ROWS, D), F32), weight],
        attn_flops, slot, (tok, vectors, qv), space_w, sems=(len(attn_plan),), name="space_forward",
    )
    parts = swap(parts)
    if by_chip:
        na0, first_x, first_y, first_out = tie((na0, first_x, first_y, first_out))
        near_x, near_y = jnp.stack([low, first_x[:half]]), jnp.stack([high, first_y])
        far_x, far_y = over_y(near_x), over_x(near_y)
        in_near, out_near = jnp.stack([mlp_in, first_x[half:]]), jnp.stack([mlp_out, first_out])
        parts, near_x, near_y, far_x, far_y, in_near, out_near = tie((parts, near_x, near_y, far_x, far_y, in_near, out_near))
        time_w = [near_x, far_x, near_y, far_y] + [over_core(piece) for piece in (near_x, far_x, near_y, far_y)]
        in_far, out_far = over_y(in_near), over_x(out_near)
        time_w, cot = tie((time_w, cot))
    gy = lax.all_to_all(cot, "seq", split_axis=0, concat_axis=0, tiled=True)
    x1, x2, na1, proj1, soft1, ctx1, peak1 = call(
        functools.partial(time_forward_kernel, attn_plan, seq), [((ROWS, D), F32), ((ROWS, D), F32)] + state,
        [stripes, weight], attn_flops, slot, [vectors, qv] + parts, time_w, sems=(len(attn_plan),), name="time_forward",
    )
    if by_chip:
        in_core, out_core = over_core(in_near), over_core(out_near)
        x2, gy, in_core, out_core, in_far, out_far = tie((x2, gy, in_core, out_core, in_far, out_far))
        in_w = [in_near, in_far, in_core, over_core(in_far)]
        out_w = [out_near, out_far, out_core, over_core(out_far)]

    mlp_sums, *results = call(
        functools.partial(mlp_kernel, seq, in_plan, out_plan, in_targets, out_targets),
        [sums] + shares + [((ROWS, D), F32)],
        [((ROWS, D), BF)] * 2 + [((ROWS, D), F32)] * 2 + [stripes] + [((D, ff), BF), ((ff, D), BF)] * 2,
        10 * ROWS * D * ff, slot, (x2, vectors, inb, gy), in_w + out_w, in_shapes + out_shapes,
        ((ff // FF_BLOCK, len(in_plan)), len(out_plan), (ff // FF_BLOCK, len(in_targets)), len(out_targets)), name="mlp",
    )
    mixed, (g2, *mlp_grads) = results[:seq], results[seq:]
    in_grads, out_grads = mlp_grads[: len(in_shapes)], mlp_grads[len(in_shapes) :]

    if by_chip:
        (in_keep, in_send), (out_keep, out_send) = in_grads, out_grads
        in_got, out_got = over_core(in_send), over_core(out_send)
        in_pair, out_pair = pair_of(in_keep, in_got, 0), pair_of(out_keep, out_got, 0)
        g2, in_pair, out_pair = tie((g2, in_pair, out_pair))
        in_came, out_came = over_x(in_pair), over_y(out_pair)
    mixed = swap(mixed)
    *parts, gproj1, gbr1, time_sums = call(
        functools.partial(time_backward_kernel, attn_plan, seq),
        shares + [((ROWS, 3 * D), BF), ((ROWS, D), BF), sums],
        [((ROWS, D), BF), stripes, weight], 2 * attn_flops,
        slot, (g2, x1, vectors, proj1, soft1), time_w, sems=(len(attn_plan),), name="time_backward",
    )
    if by_chip:
        parts, mixed = tie((parts, mixed))
    parts = swap(parts)
    time_grads = call(
        functools.partial(weight_grad_kernel, attn_targets), [], [weight], attn_flops,
        slot, (na1, gproj1, ctx1, gbr1), (), attn_shapes, (len(attn_targets),), name="time_weight_grad", cost=COVER,
    )
    if by_chip:
        time_keep, time_send = time_grads
        parts[1], time_send, in_came, out_came = tie((parts[1], time_send, in_came, out_came))
        time_got = over_core(time_send)
        in_rest, out_rest = rest_of(in_keep, in_got, 0, in_came), rest_of(out_keep, out_got, 0, out_came)
        in_last, out_last = over_y(in_rest), over_x(out_rest)
        time_pairs = pair_of(time_keep, time_got, 0), pair_of(time_keep, time_got, 4)
        parts, time_pairs = tie((parts, time_pairs))
        time_came = over_x(time_pairs[0]), over_y(time_pairs[1])
    peaks = jnp.concatenate([peak0[0, :H], peak1[0, :H]])
    devices = shards * seq
    peaks = jnp.where(jnp.arange(devices)[:, None] == me * seq + place, peaks[None], 0.0).reshape(-1, D)
    g_tok, small_grads, *space_grads = call(
        functools.partial(space_backward_kernel, attn_plan, attn_targets, seq),
        [((local_len, D), F32), ((24 + peaks.shape[0], D), F32)],
        [((ROWS, D), F32), ((ROWS, 3 * D), BF), ((ROWS, D), BF), ((ROWS, D), BF), weight, weight], 2 * attn_flops,
        slot, [tok, vectors, mlp_sums, time_sums, peaks, na0, ctx0, proj0, soft0] + parts, space_w, attn_shapes, (len(attn_plan), len(attn_targets)),
        name="space_backward",
    )
    if by_chip:
        space_keep, space_send = space_grads
        space_send, in_last, out_last, time_came = tie((space_send, in_last, out_last, time_came))
        small_came = hop(small_grads, "seq", 2)
        space_got = over_core(space_send)
        mlp_keep, mlp_send = seq_halves(jnp.concatenate([
            own_of(in_keep, in_got, 0, in_came, in_last), pack_rows(own_of(out_keep, out_got, 0, out_came, out_last)),
        ]))
        space_got, mlp_send, small_came = tie((space_got, mlp_send, small_came))
        small_grads = small_grads + small_came
        mlp_came = hop(mlp_send, "seq", 1)
        space_pairs = pair_of(space_keep, space_got, 0), pair_of(space_keep, space_got, 4)
        space_came = over_x(space_pairs[0]), over_y(space_pairs[1])
        small_came = over_core(small_grads)
        mlp_came, time_came, small_came = tie((mlp_came, time_came, small_came))
        small_grads = small_grads + small_came
        small_came = hop(small_grads, "seq", 1)
        time_rests = rest_of(time_keep, time_got, 0, time_came[0]), rest_of(time_keep, time_got, 4, time_came[1])
        time_lasts = over_y(time_rests[0]), over_x(time_rests[1])
        mlp_part = (mlp_keep + mlp_came.astype(F32)).astype(BF)
        mlp_came = [hop(piece, "seq", 2) for piece in jnp.split(mlp_part, 2)]
    if by_chip:
        space_came, small_came = tie((space_came, small_came))
        small_grads = small_grads + small_came
        space_rests = rest_of(space_keep, space_got, 0, space_came[0]), rest_of(space_keep, space_got, 4, space_came[1])
        space_lasts = over_y(space_rests[0]), over_x(space_rests[1])
        time_keep, time_send = seq_halves(jnp.concatenate([
            own_of(time_keep, time_got, 0, time_came[0], time_lasts[0]), own_of(time_keep, time_got, 4, time_came[1], time_lasts[1]),
        ]))
        time_came = hop(time_send, "seq", 1)
        small_came = over_x(small_grads)
        space_lasts, small_came, mlp_came[0] = tie((space_lasts, small_came, mlp_came[0]))
        small_grads = small_grads + small_came
        space_keep, space_send = seq_halves(jnp.concatenate([
            own_of(space_keep, space_got, 0, space_came[0], space_lasts[0]),
            own_of(space_keep, space_got, 4, space_came[1], space_lasts[1]),
        ]))
        space_came = hop(space_send, "seq", 1)
        small_came = over_y(small_grads)
        time_part = (time_keep + time_came.astype(F32)).astype(BF)
        time_came = hop(time_part, "seq", 2)
        space_came, small_came, mlp_came = tie((space_came, small_came, mlp_came))
        small_grads = small_grads + small_came
        mlp_part = (mlp_part.astype(F32) + jnp.concatenate(mlp_came).astype(F32)).astype(BF)
        space_part = (space_keep + space_came.astype(F32)).astype(BF)
        space_came = hop(space_part, "seq", 2)
        mlp_came = hop(mlp_part, "seq", 1)
        space_came, time_came, small_grads = tie((space_came, time_came, small_grads))
        mlp_total = seq_join(mlp_part, mlp_came)
        grad_in, grad_mout = mlp_total[:own_rows], unpack_rows(mlp_total[own_rows:])
        space_part = (space_part.astype(F32) + space_came.astype(F32)).astype(BF)
        time_part = (time_part.astype(F32) + time_came.astype(F32)).astype(BF)
        attn_totals = [seq_join(part, hop(part, "seq", 1)) for part in (space_part, time_part)]
    else:
        small_grads = lax.psum(small_grads, ("fsdp", "seq"))
        (in_grads,), (out_grads,) = in_grads, out_grads
        in_total, out_total, time_total, space_total = (
            reduce_plain(value) for value in (in_grads, out_grads, time_grads[0], space_grads[0])
        )
        grad_in, grad_mout = seq_total(in_total), seq_total(out_total)
        attn_totals = [seq_total(space_total), seq_total(time_total)]
    grad_qkv = jnp.stack([value[:, : 3 * D] for value in attn_totals])
    grad_out = jnp.stack([value[:, 3 * D :] for value in attn_totals])

    logit_max = jnp.max(small_grads[24:].reshape(devices, 2, H), axis=0)

    def share(rows, width):
        return lax.dynamic_slice_in_dim(rows.reshape(-1, shards * width), me * width, width, axis=1)

    pick = lambda *rows: jnp.concatenate([small_grads[row : row + 1] for row in rows])
    vector_grads = share(pick(16, 8, 0, 17, 9, 1, 18, 10, 2), own_rows)
    grad_gain, grad_shift, grad_outb, grad_moutb = vector_grads[0:3], vector_grads[3:6], vector_grads[6:8], vector_grads[8]
    grad_qv = share(pick(19, 20, 11, 12), 2 * own_rows)
    grad_inb = share(small_grads[3:7], ff // shards)[0]

    factor = threshold / jnp.maximum(logit_max, threshold)
    column_scale = jnp.repeat(jnp.sqrt(factor), HD, axis=1)
    clipped = attn_qkv[:, :, : 2 * D].astype(F32) * jnp.concatenate([column_scale, column_scale], axis=1)[:, None, :]
    mixed = jnp.swapaxes(by_distance(jnp.stack(mixed), place), 0, 1).reshape(tokens.shape)
    return (
        mixed, g_tok.reshape(tokens.shape), grad_gain, grad_shift, grad_qkv, grad_qv, grad_out, grad_outb,
        grad_in, grad_inb, grad_mout, grad_moutb, logit_max, clipped,
    )


def solution(mesh):
    placed = (
        P("fsdp", "seq", None), P(None, "fsdp"), P(None, "fsdp"), P(None, "fsdp", None), P(None, "fsdp"),
        P(None, "fsdp", None), P(None, "fsdp"), P("fsdp", None), P("fsdp"), P("fsdp", None), P("fsdp"), P(),
        P("fsdp", "seq", None),
    )
    return jax.shard_map(
        on_device,
        mesh=mesh,
        in_specs=placed,
        out_specs=(
            P("fsdp", "seq", None), P("fsdp", "seq", None), P(None, "fsdp"), P(None, "fsdp"), P(None, "fsdp", None),
            P(None, "fsdp"), P(None, "fsdp", None), P(None, "fsdp"), P("fsdp", None), P("fsdp"), P("fsdp", None),
            P("fsdp"), P(), P(None, "fsdp", None),
        ),
        check_vma=False,
    )
```

```python
import functools
import itertools

import jax
import jax.numpy as jnp
from jax import lax
from jax.experimental import pallas as pl
from jax.experimental.pallas import tpu as pltpu
from jax.sharding import PartitionSpec as P

H = 12
PATCHES = 196
HD = 64
D = 768
PAIRS = H // 2
CHUNK = 208
BLOCKS = 2
ROWS = BLOCKS * CHUNK
FF_BLOCK = 768
EPSILON = 1e-06
NEGATIVE = -1e30
SCALE = HD ** (-0.5)
COST, COVER = 1000, 40 * 2**20
VMEM_LIMIT = 58 * 1024 * 1024
BF = jnp.bfloat16
F32 = jnp.float32


def mm(a, b):
    return lax.dot_general(a, b, (((1,), (0,)), ((), ())), preferred_element_type=F32)


def mm_nt(a, b):
    return lax.dot_general(a, b, (((1,), (1,)), ((), ())), preferred_element_type=F32)


def mm_tn(a, b):
    return lax.dot_general(a, b, (((0,), (0,)), ((), ())), preferred_element_type=F32)


def row_stats(rows):
    centre = jnp.mean(rows, axis=-1, keepdims=True)
    centred = rows - centre
    second = jnp.mean(centred * centred, axis=-1, keepdims=True)
    inverse = lax.rsqrt(second + EPSILON)
    return centred * inverse, inverse


def norm_backward(grad, unit, inverse, gain):
    weighted = grad * gain
    first = jnp.mean(weighted, axis=-1, keepdims=True)
    second = jnp.mean(weighted * unit, axis=-1, keepdims=True)
    return (weighted - first - unit * second) * inverse


def column_sum(values):
    return jnp.sum(values.astype(F32), axis=0, keepdims=True)


def masks(temporal, block, frames):
    row = lax.broadcasted_iota(jnp.int32, (2 * CHUNK, CHUNK), 0)
    col = lax.broadcasted_iota(jnp.int32, (2 * CHUNK, CHUNK), 1)
    if temporal:
        row = jnp.where(row >= CHUNK, row - CHUNK, row)
        allowed = (row // frames) == (col // frames)
    else:
        allowed = col < PATCHES
    return allowed


def lower_lanes(rows):
    return lax.broadcasted_iota(jnp.int32, (rows, 2 * HD), 1) < HD


def split_heads(pair, scale=None):
    low_half = lower_lanes(pair.shape[0])
    if scale is not None:
        pair = pair * jnp.asarray(scale, pair.dtype)
    zero = jnp.zeros_like(pair)
    return jnp.where(low_half, pair, zero), jnp.where(low_half, zero, pair)


def attend_forward(proj_ref, ctx_ref, soft_ref, peak_ref, temporal, frames, valid, send):
    lane = lax.broadcasted_iota(jnp.int32, (8, 128), 1)
    peaks = jnp.full((8, 128), NEGATIVE, F32)
    for block in range(BLOCKS):
        allowed = masks(temporal, block, frames)
        rows = slice(block * CHUNK, (block + 1) * CHUNK)
        row_id = lax.broadcasted_iota(jnp.int32, (CHUNK, 1), 0)
        for pair in range(PAIRS):
            cols = slice(pair * 128, pair * 128 + 128)
            q_a, q_b = split_heads(proj_ref[rows, cols], SCALE)
            keys = proj_ref[rows, D + pair * 128 : D + pair * 128 + 128]
            v_a, v_b = split_heads(proj_ref[rows, 2 * D + pair * 128 : 2 * D + pair * 128 + 128])
            scores = mm_nt(jnp.concatenate([q_a, q_b], axis=0), keys)
            scores = jnp.where(allowed, scores, NEGATIVE)
            top = jnp.max(scores, axis=1, keepdims=True)
            expo = jnp.exp(scores - top)
            total = jnp.sum(expo, axis=1, keepdims=True)
            soft = (expo / total).astype(BF)
            soft_ref[block * PAIRS + pair] = soft
            send(block * PAIRS + pair)
            ctx_ref[rows, cols] = (mm(soft[:CHUNK], v_a) + mm(soft[CHUNK:], v_b)).astype(BF)
            for side in range(2):
                seen = jnp.where(row_id < valid[block], top[side * CHUNK : (side + 1) * CHUNK], NEGATIVE)
                best = jnp.max(seen, axis=0, keepdims=True)
                peaks = jnp.where(lane == 2 * pair + side, jnp.maximum(peaks, best), peaks)
    peak_ref[...] = peaks


def attend_backward(proj_ref, soft_ref, gctx_ref, gproj_ref):
    for block in range(BLOCKS):
        rows = slice(block * CHUNK, (block + 1) * CHUNK)
        for pair in range(PAIRS):
            cols = slice(pair * 128, pair * 128 + 128)
            kcols = slice(D + pair * 128, D + pair * 128 + 128)
            vcols = slice(2 * D + pair * 128, 2 * D + pair * 128 + 128)
            q_pair = jnp.concatenate(split_heads(proj_ref[rows, cols], SCALE), axis=0)
            k_a, k_b = split_heads(proj_ref[rows, kcols], SCALE)
            values = proj_ref[rows, vcols]
            g_pair = jnp.concatenate(split_heads(gctx_ref[rows, cols]), axis=0)
            soft_low = soft_ref[block * PAIRS + pair]
            soft = soft_low.astype(F32)
            grad_soft = mm_nt(g_pair, values)
            inner = jnp.sum(soft * grad_soft, axis=1, keepdims=True)
            grad_scores = (soft * (grad_soft - inner)).astype(BF)
            gproj_ref[rows, cols] = (mm(grad_scores[:CHUNK], k_a) + mm(grad_scores[CHUNK:], k_b)).astype(BF)
            gproj_ref[rows, kcols] = mm_tn(grad_scores, q_pair).astype(BF)
            gproj_ref[rows, vcols] = mm_tn(soft_low, g_pair).astype(BF)


def blocks_between(slot_ref, arrays, plan, weight_ref):
    for array, index, row, column, height, width, place, scale, first, at in plan:
        start = pl.multiple_of(slot_ref[place] * scale + first, 16)
        yield (
            arrays[array].at[index, row : row + height, column : column + width],
            weight_ref.at[pl.ds(start, height), at : at + width],
        )


def fetch(slot_ref, pieces, plan, weight_ref, sems):
    copies = []
    for number, (piece, part) in enumerate(blocks_between(slot_ref, pieces, plan, weight_ref)):
        copies.append(pltpu.make_async_copy(piece, part, sems.at[number]))
        copies[-1].start()
    return copies


def deliver(slot_ref, weight_ref, targets, plan, sems):
    copies = []
    for number, (piece, part) in enumerate(blocks_between(slot_ref, targets, plan, weight_ref)):
        copies.append(pltpu.make_async_copy(part, piece, sems.at[number]))
        copies[-1].start()
    return copies


def take(refs, plan):
    count = 1 + max(entry[0] for entry in plan)
    return refs[:count], refs[count:]


def sender(sources, targets, sems):
    started = []

    def send(number):
        copy = pltpu.make_async_copy(sources[number], targets[number], sems.at[number])
        copy.start()
        started.append(copy)

    return send, started


def saved_state(refs):
    targets, (na_ref, proj_ref, soft_ref, ctx_ref), sems = refs[:4], refs[4:8], refs[8]
    count = soft_ref.shape[0]
    sources = [soft_ref.at[k] for k in range(count)] + [na_ref, proj_ref, ctx_ref]
    places = [targets[2].at[k] for k in range(count)] + [targets[0], targets[1], targets[3]]
    send, started = sender(sources, places, sems)
    return na_ref, proj_ref, soft_ref, ctx_ref, count, send, started


def finish(copies):
    for copy in copies:
        copy.wait()


def project(na_ref, qkv_ref, qv, proj_ref):
    for part in range(3):
        cols = slice(part * D, (part + 1) * D)
        value = mm(na_ref[...], qkv_ref[:, cols])
        if part != 1:
            at = 0 if part == 0 else D
            value = value + qv[:, at : at + D]
        proj_ref[:, cols] = value.astype(BF)


def pad_frames(tok_ref, rows_ref):
    count = tok_ref.shape[0]
    flat = tok_ref[...].astype(F32)
    rows_ref[0:count, :] = flat
    rows_ref[CHUNK : CHUNK + PATCHES, :] = flat[PATCHES:, :]
    rows_ref[PATCHES:CHUNK, :] = jnp.zeros((CHUNK - PATCHES, D), F32)
    rows_ref[CHUNK + PATCHES :, :] = jnp.zeros((CHUNK - PATCHES, D), F32)


def space_forward_kernel(plan, seq, slot_ref, tok_ref, vec_ref, qv_ref, *refs):
    pieces, refs = take(refs, plan)
    part_refs, refs = refs[:seq], refs[seq:]
    peak_ref, *refs = refs
    na_ref, proj_ref, soft_ref, ctx_ref, count, send, started = saved_state(refs[:4] + refs[6:11])
    rows_ref, weight_ref, sems = refs[4], refs[5], refs[-1]
    copies = fetch(slot_ref, pieces, plan, weight_ref, sems)
    pad_frames(tok_ref, rows_ref)
    unit, _ = row_stats(rows_ref[...])
    na_ref[...] = (unit * vec_ref[0:1] + vec_ref[3:4]).astype(BF)
    send(count)
    finish(copies)
    project(na_ref, weight_ref, qv_ref[0:1], proj_ref)
    send(count + 1)
    attend_forward(proj_ref, ctx_ref, soft_ref, peak_ref, False, 0, (PATCHES, PATCHES), send)
    send(count + 2)
    rows_ref[...] = rows_ref[...] + mm(ctx_ref[...], weight_ref[:, 3 * D :]) + vec_ref[6:7]
    frames, width = part_refs[0].shape[0], part_refs[0].shape[1]

    def body(place):
        for distance in range(seq):
            for frame in range(frames):
                start = frame * CHUNK + (place ^ distance) * width
                part_refs[distance][frame] = rows_ref[start : start + width, :].astype(BF)

    for_place(slot_ref, seq, body)
    finish(started)


def for_place(slot_ref, count, body):
    for place in range(count):
        pl.when(slot_ref[slot_ref.shape[0] - 1] == place)(functools.partial(body, place))


def interleave(slot_ref, part_refs, stripes_ref, rows_ref):
    shares, frames, width = len(part_refs), part_refs[0].shape[0], part_refs[0].shape[1]
    total = shares * frames
    place = 0 if slot_ref is None else slot_ref[slot_ref.shape[0] - 1]
    for stripe in range(D // 128):
        cols = slice(stripe * 128, stripe * 128 + 128)
        for distance in range(shares):
            for frame in range(frames):
                first = (place ^ distance) * frames + frame
                stripes_ref[stripe, pl.ds(first, width, stride=total), :] = part_refs[distance][frame, :, cols].astype(F32)
        stripes_ref[stripe, total * width :, :] = jnp.zeros((ROWS - total * width, 128), F32)
        rows_ref[:, cols] = stripes_ref[stripe].astype(rows_ref.dtype)


def separate(slot_ref, rows, stripes_ref, part_refs):
    shares, frames, width = len(part_refs), part_refs[0].shape[0], part_refs[0].shape[1]
    total = shares * frames
    place = slot_ref[slot_ref.shape[0] - 1]
    for stripe in range(D // 128):
        cols = slice(stripe * 128, stripe * 128 + 128)
        stripes_ref[stripe] = rows[:, cols]
        for distance in range(shares):
            for frame in range(frames):
                first = (place ^ distance) * frames + frame
                part_refs[distance][frame, :, cols] = stripes_ref[stripe, pl.ds(first, width, stride=total), :].astype(
                    part_refs[distance].dtype
                )


def time_forward_kernel(plan, seq, slot_ref, vec_ref, qv_ref, *refs):
    part_refs, refs = refs[:seq], refs[seq:]
    pieces, refs = take(refs, plan)
    x1_ref, x2_ref, peak_ref, *refs = refs
    na_ref, proj_ref, soft_ref, ctx_ref, count, send, started = saved_state(refs[:4] + refs[6:11])
    stripes_ref, weight_ref, sems = refs[4], refs[5], refs[-1]
    copies = fetch(slot_ref, pieces, plan, weight_ref, sems)
    frames = seq * part_refs[0].shape[0]
    tokens = frames * part_refs[0].shape[1]
    interleave(slot_ref, part_refs, stripes_ref, x1_ref)
    unit, _ = row_stats(x1_ref[...].astype(F32))
    na_ref[...] = (unit * vec_ref[1:2] + vec_ref[4:5]).astype(BF)
    send(count)
    finish(copies)
    project(na_ref, weight_ref, qv_ref[1:2], proj_ref)
    send(count + 1)
    attend_forward(proj_ref, ctx_ref, soft_ref, peak_ref, True, frames, (CHUNK, tokens - CHUNK), send)
    send(count + 2)
    x2_ref[...] = x1_ref[...].astype(F32) + mm(ctx_ref[...], weight_ref[:, 3 * D :]) + vec_ref[7:8]
    finish(started)


def mlp_kernel(seq, in_plan, out_plan, in_targets, out_targets, slot_ref, x2_ref, vec_ref, inb_ref, gy_ref, *refs):
    in_pieces, refs = take(refs, in_plan)
    out_pieces, refs = take(refs, out_plan)
    sums_ref, *refs = refs
    mixed_refs, refs = refs[:seq], refs[seq:]
    g2_ref, *refs = refs
    gin_arrays, refs = take(refs, in_targets)
    gout_arrays, refs = take(refs, out_targets)
    (
        n2_ref, gyl_ref, rows_ref, back_ref, stripes_ref, in_ref, out_ref, gin_ref, gout_ref,
        in_sems, out_sems, gin_sems, gout_sems,
    ) = refs
    blocks = in_ref.shape[1] // FF_BLOCK
    out_height = out_plan[0][4]
    rows_each = FF_BLOCK // out_height

    def span_of(step):
        return pl.ds(pl.multiple_of(step * FF_BLOCK, FF_BLOCK), FF_BLOCK)

    def in_copies(step):
        return [
            pltpu.make_async_copy(piece.at[:, span_of(step)], part.at[:, span_of(step)], in_sems.at[step, number])
            for number, (piece, part) in enumerate(blocks_between(slot_ref, in_pieces, in_plan, in_ref))
        ]

    def gin_copies(step):
        return [
            pltpu.make_async_copy(part.at[:, span_of(step)], piece.at[:, span_of(step)], gin_sems.at[step, number])
            for number, (piece, part) in enumerate(blocks_between(slot_ref, gin_arrays, in_targets, gin_ref))
        ]

    def first_row(entry):
        return slot_ref[entry[6]] * entry[7] + entry[8]

    for step in range(blocks):
        for copy in in_copies(step):
            copy.start()
        if step == 0:
            for entry, (piece, part) in zip(out_plan, blocks_between(slot_ref, out_pieces, out_plan, out_ref)):
                pltpu.make_async_copy(piece, part, out_sems.at[first_row(entry) // out_height]).start()
    unit, _ = row_stats(x2_ref[...])
    n2_ref[...] = (unit * vec_ref[2:3] + vec_ref[5:6]).astype(BF)
    interleave(None, [gy_ref.at[share] for share in range(seq)], stripes_ref, gyl_ref)
    sums_ref[2:3] = column_sum(gyl_ref[...])
    rows_ref[...] = jnp.zeros_like(rows_ref)
    back_ref[...] = jnp.zeros_like(back_ref)
    gout_copies = [
        pltpu.make_async_copy(part, piece, gout_sems.at[number])
        for number, (piece, part) in enumerate(blocks_between(slot_ref, gout_arrays, out_targets, gout_ref))
    ]

    @pl.loop(0, blocks)
    def _(step):
        span = span_of(step)
        for copy in in_copies(step):
            copy.wait()
        for number in range(rows_each):
            part = out_ref.at[0:out_height, :]
            pltpu.make_async_copy(part, part, out_sems.at[step * rows_each + number]).wait()
        hidden = mm(n2_ref[...], in_ref[:, span]) + inb_ref[:, span]
        cumulative = 0.5 * (1.0 + lax.erf(hidden * (2.0 ** -0.5)))
        act = (hidden * cumulative).astype(BF)
        slope = cumulative + hidden * jnp.exp(-0.5 * hidden * hidden) * 0.3989422804014327
        rows_ref[...] += mm(act, out_ref[span, :])
        gout_ref[span, :] = mm_tn(act, gyl_ref[...]).astype(BF)
        for copy, entry in zip(gout_copies, out_targets):
            pl.when(first_row(entry) // FF_BLOCK == step)(copy.start)
        ghid = (mm_nt(gyl_ref[...], out_ref[span, :]) * slope).astype(BF)
        sums_ref[pl.ds(3 + step, 1), :] = column_sum(ghid)
        gin_ref[:, span] = mm_tn(n2_ref[...], ghid).astype(BF)
        for copy in gin_copies(step):
            copy.start()
        back_ref[...] += mm_nt(ghid, in_ref[:, span])

    separate(slot_ref, x2_ref[...] + rows_ref[...] + vec_ref[8:9], stripes_ref, mixed_refs)
    unit, inverse = row_stats(x2_ref[...])
    grad = back_ref[...]
    sums_ref[0:1] = column_sum(grad * unit)
    sums_ref[1:2] = column_sum(grad)
    sums_ref[7:8] = jnp.zeros((1, D), F32)
    g2_ref[...] = gyl_ref[...].astype(F32) + norm_backward(grad, unit, inverse, vec_ref[2:3])
    for step in range(blocks):
        finish(gin_copies(step))
    finish(gout_copies)


def branch_backward(g_ref, proj_ref, soft_ref, weight_ref, sums_ref, gproj_ref, gbr_ref, gctx_ref, awaited):
    gbr_ref[...] = g_ref[...].astype(BF)
    sums_ref[2:3] = column_sum(gbr_ref[...])
    gctx_ref[...] = mm_nt(gbr_ref[...], weight_ref[:, 3 * D :]).astype(BF)
    finish(awaited)
    attend_backward(proj_ref, soft_ref, gctx_ref, gproj_ref)
    sums_ref[3:4] = column_sum(gproj_ref[:, 0:D])
    sums_ref[4:5] = column_sum(gproj_ref[:, 2 * D :])
    sums_ref[5:8] = jnp.zeros((3, D), F32)


def projection_backward(gproj_ref, weight_ref):
    total = mm_nt(gproj_ref[:, 0:D], weight_ref[:, 0:D])
    for part in range(1, 3):
        cols = slice(part * D, (part + 1) * D)
        total = total + mm_nt(gproj_ref[:, cols], weight_ref[:, cols])
    return total


def weight_grads(na_ref, gproj_ref, ctx_ref, gbr_ref, grad_ref):
    grad_ref[:, 3 * D :] = mm_tn(ctx_ref[...], gbr_ref[...]).astype(BF)
    for part in range(3):
        cols = slice(part * D, (part + 1) * D)
        grad_ref[:, cols] = mm_tn(na_ref[...], gproj_ref[:, cols]).astype(BF)


def time_backward_kernel(plan, seq, slot_ref, g_ref, x1_ref, vec_ref, *refs):
    pieces, refs = take(refs, plan)
    kept, refs = refs[:2], refs[2:]
    part_refs, refs = refs[:seq], refs[seq:]
    sums_ref, gproj_to, gbr_to, gproj_ref, gbr_ref, proj_ref, soft_ref, gctx_ref, stripes_ref, weight_ref, sems, more = refs
    copies = fetch(slot_ref, pieces, plan, weight_ref, sems)
    send, started = sender((kept[0], kept[1], gproj_ref, gbr_ref), (proj_ref, soft_ref, gproj_to, gbr_to), more)
    send(0)
    send(1)
    finish(copies)
    branch_backward(g_ref, proj_ref, soft_ref, weight_ref, sums_ref, gproj_ref, gbr_ref, gctx_ref, started)
    send(2)
    send(3)
    grad = projection_backward(gproj_ref, weight_ref)
    unit, inverse = row_stats(x1_ref[...].astype(F32))
    sums_ref[0:1] = column_sum(grad * unit)
    sums_ref[1:2] = column_sum(grad)
    separate(slot_ref, g_ref[...] + norm_backward(grad, unit, inverse, vec_ref[1:2]), stripes_ref, part_refs)
    finish(started[2:])


def weight_grad_kernel(targets, slot_ref, na_ref, gproj_ref, ctx_ref, gbr_ref, *refs):
    outs, (grad_ref, sems) = take(refs, targets)
    weight_grads(na_ref, gproj_ref, ctx_ref, gbr_ref, grad_ref)
    finish(deliver(slot_ref, grad_ref, outs, targets, sems))


def space_backward_kernel(
    plan, targets, seq, slot_ref, tok_ref, vec_ref, mlp_sums_ref, time_sums_ref, peaks_ref, *refs
):
    part_refs, refs = refs[:seq], refs[seq:]
    pieces, refs = take(refs, plan)
    kept, refs = refs[:4], refs[4:]
    gtok_ref, all_sums_ref, *refs = refs
    sums_ref = all_sums_ref.at[16:24]
    outs, refs = take(refs, targets)
    g_ref, gproj_ref, gbr_ref, gctx_ref, weight_ref, grad_ref, *local, sems, grad_sems, more = refs
    copies = fetch(slot_ref, pieces, plan, weight_ref, sems)
    send, started = sender(kept, local, more)
    for number in range(4):
        send(number)
    proj_ref, soft_ref, na_ref, ctx_ref = local
    frames, width = part_refs[0].shape[0], part_refs[0].shape[1]

    def body(place):
        for frame in range(frames):
            for distance in range(seq):
                start = frame * CHUNK + (place ^ distance) * width
                g_ref[start : start + width, :] = part_refs[distance][frame].astype(F32)

    for_place(slot_ref, seq, body)
    all_sums_ref[0:8] = mlp_sums_ref[...]
    all_sums_ref[8:16] = time_sums_ref[...]
    all_sums_ref[24:] = peaks_ref[...]
    for frame in range(frames):
        g_ref[frame * CHUNK + PATCHES : (frame + 1) * CHUNK, :] = jnp.zeros((CHUNK - PATCHES, D), F32)
    finish(copies)
    branch_backward(g_ref, proj_ref, soft_ref, weight_ref, sums_ref, gproj_ref, gbr_ref, gctx_ref, started)
    weight_grads(na_ref, gproj_ref, ctx_ref, gbr_ref, grad_ref)
    copies = deliver(slot_ref, grad_ref, outs, targets, grad_sems)
    grad = projection_backward(gproj_ref, weight_ref)
    total = g_ref[...]
    pad_frames(tok_ref, g_ref)
    unit, inverse = row_stats(g_ref[...])
    sums_ref[0:1] = column_sum(grad * unit)
    sums_ref[1:2] = column_sum(grad)
    g_ref[...] = total + norm_backward(grad, unit, inverse, vec_ref[0:1])
    gtok_ref[0:PATCHES, :] = g_ref[0:PATCHES, :]
    gtok_ref[PATCHES:, :] = g_ref[CHUNK : CHUNK + PATCHES, :]
    finish(copies)


def call(kernel, outs, scratch, flops, slot, operands, pieces=(), targets=(), sems=(), *, name, cost=COST):
    whole = pl.BlockSpec(memory_space=pltpu.VMEM)
    far = pl.BlockSpec(memory_space=pl.ANY)
    return pl.pallas_call(
        kernel,
        in_specs=[pl.BlockSpec(memory_space=pltpu.SMEM)] + [whole] * len(operands) + [far] * len(pieces),
        out_specs=[whole] * len(outs) + [far] * len(targets),
        out_shape=[jax.ShapeDtypeStruct(shape, dtype) for shape, dtype in list(outs) + list(targets)],
        scratch_shapes=[pltpu.VMEM(shape, dtype) for shape, dtype in scratch]
        + [pltpu.SemaphoreType.DMA(count if isinstance(count, tuple) else (count,)) for count in sems],
        compiler_params=pltpu.CompilerParams(vmem_limit_bytes=VMEM_LIMIT),
        cost_estimate=pl.CostEstimate(flops=1000, bytes_accessed=cost, transcendentals=0),
        name=name,
    )(slot, *operands, *pieces)


def hop(value, axis, bit):
    return lax.ppermute(value, axis, [(index, index ^ bit) for index in range(lax.axis_size(axis))])


CORE, CHIP_X, CHIP_Y = 1, 2, 4
X_ORDER = (0, CHIP_Y, CHIP_X, CHIP_X | CHIP_Y)
Y_ORDER = (0, CHIP_X, CHIP_Y, CHIP_X | CHIP_Y)


def pack_rows(value):
    return jnp.concatenate(jnp.split(value, 4, axis=0), axis=1)


def unpack_rows(value):
    return jnp.concatenate(jnp.split(value, 4, axis=1), axis=0)


def targets_of(height, width, order):
    return [
        (side, chip, 0, 0, height, width, order[chip] ^ shift, height, 0, 0)
        for side, shift in enumerate((0, CORE)) for chip in range(4)
    ]


def gather_plain(own):
    full = lax.all_gather(own[None], "fsdp", axis=1, tiled=True)
    return [full], plain_plan(full.shape[1], full.shape[2])


def plain_plan(rows, columns):
    return [(0, 0, 0, 0, rows, columns, 0, 0, 0, 0)]


tie = lax.optimization_barrier


def sums_of(keep, got):
    return lambda part: keep[part].astype(F32) + got[part].astype(F32)


def pair_of(keep, got, first):
    return sums_of(keep, got)(slice(first + 2, first + 4)).astype(BF)


def rest_of(keep, got, first, came):
    return (sums_of(keep, got)(first + 1) + came[1].astype(F32)).astype(BF)


def own_of(keep, got, first, came, last):
    return sums_of(keep, got)(first) + came[0].astype(F32) + last.astype(F32)


def over_x(value):
    return hop(value, "fsdp", CHIP_X)


def over_y(value):
    return hop(value, "fsdp", CHIP_Y)


def over_core(value):
    return hop(value, "fsdp", CORE)


def reduce_plain(grad):
    return lax.psum_scatter(grad[0], "fsdp", scatter_dimension=0, tiled=True).astype(F32)


def seq_halves(value):
    odd = (lax.axis_index("seq") & 1) == 1
    half = value.shape[0] // 2
    low, high = value[:half], value[half:]
    return jnp.where(odd, high, low), jnp.where(odd, low, high).astype(BF)


def seq_first(value):
    mine, other = seq_halves(value)
    return (mine + hop(other, "seq", 1).astype(F32)).astype(BF)


def seq_second(part):
    return (part.astype(F32) + hop(part, "seq", 2).astype(F32)).astype(BF)


def seq_join(part, other):
    odd = (lax.axis_index("seq") & 1) == 1
    return jnp.where(odd, jnp.concatenate([other, part]), jnp.concatenate([part, other])).astype(F32)


def seq_total(value):
    if lax.axis_size("seq") != 4:
        return lax.psum(value.astype(BF), "seq").astype(F32)
    part = seq_second(seq_first(value))
    return seq_join(part, hop(part, "seq", 1))


def by_distance(parts, place):
    shape = parts.shape
    bit = 1
    while bit < shape[0]:
        paired = parts.reshape((shape[0] // (2 * bit), 2, bit) + shape[1:])
        parts = jnp.where((place & bit) != 0, paired[:, ::-1], paired).reshape(shape)
        bit *= 2
    return parts


def swap(parts):
    return [parts[0]] + [hop(parts[distance], "seq", distance) for distance in range(1, len(parts))]


def on_device(
    tokens, norm_gain, norm_bias, attn_qkv, attn_qv_bias, attn_out, attn_out_bias,
    mlp_in, mlp_in_bias, mlp_out, mlp_out_bias, threshold, cotangent,
):
    clip_count, local_len, _ = tokens.shape
    seq, shards = lax.axis_size("seq"), lax.axis_size("fsdp")
    me = lax.axis_index("fsdp")
    frames = local_len // PATCHES
    width = PATCHES // seq
    own_rows = D // shards
    ff = mlp_in.shape[1]
    split_shape = (seq, frames, width, D)
    tok = tokens.reshape(local_len, D)
    cot = jnp.swapaxes(cotangent.reshape(frames, seq, width, D), 0, 1)
    by_chip = shards == 8

    attn_own = [jnp.concatenate([attn_qkv[a], attn_out[a]], axis=1) for a in range(2)]
    small = jnp.concatenate([
        norm_gain, norm_bias, attn_out_bias, mlp_out_bias.reshape(1, own_rows), attn_qv_bias.reshape(-1, own_rows),
        mlp_in_bias.reshape(-1, own_rows),
    ])
    place = lax.axis_index("seq")
    half = own_rows // 2
    ff_rows = ff // D
    if by_chip:
        slot = me ^ jnp.arange(shards, dtype=jnp.int32)
        low, high = attn_own[0][:half], attn_own[0][half:]
        near_x, near_y = jnp.stack([low, over_x(low)]), jnp.stack([high, over_y(high)])
        core_x, core_y = over_core(near_x), over_core(near_y)
        core_x, core_y, small = tie((core_x, core_y, small))
        small = jnp.stack([small, over_x(small), over_y(small), hop(small, "fsdp", CHIP_X | CHIP_Y)])
        far_x, far_y = over_y(near_x), over_x(near_y)
        small = jnp.stack([small, over_core(small)], axis=1).reshape((shards,) + small.shape[1:])
        small = by_distance(small, me)
        low, high = attn_own[1][:half], attn_own[1][half:]
        first_x, first_y, first_out = jnp.concatenate([low, mlp_in]), high, mlp_out
        far_x, far_y, core_x, core_y, first_x, first_y, first_out = tie(
            (far_x, far_y, core_x, core_y, first_x, first_y, first_out)
        )
        first_x, first_y, first_out = over_x(first_x), over_y(first_y), over_y(first_out)
        space_w = [near_x, far_x, near_y, far_y, core_x, over_core(far_x), core_y, over_core(far_y)]
        places = ((0, CHIP_X), (CHIP_Y, CHIP_X | CHIP_Y), (0, CHIP_Y), (CHIP_X, CHIP_X | CHIP_Y))
        attn_plan, in_plan, out_plan, out_rows = [], [], [], mlp_out.shape[0]
        for array in range(8):
            shift, lower = (0 if array < 4 else CORE), array % 4 < 2
            for index, owner in enumerate(places[array % 4]):
                owner = owner ^ shift
                attn_plan.append((array, index, 0, 0, half, 4 * D, owner, own_rows, 0 if lower else half, 0))
                array_of = array % 2 + (0 if array < 4 else 2)
                if lower:
                    in_plan.append((array_of, index, 0, 0, own_rows, ff, owner, own_rows, 0, 0))
                else:
                    out_plan.append((array_of, index, 0, 0, out_rows, D, owner, out_rows, 0, 0))
        in_targets, out_targets = targets_of(own_rows, ff, X_ORDER), targets_of(out_rows, D, Y_ORDER)
        in_shapes, out_shapes = [((4, own_rows, ff), BF)] * 2, [((4, out_rows, D), BF)] * 2
        attn_targets = [
            (side, 4 * lower + chip, 0, 0, half, 4 * D, (X_ORDER, Y_ORDER)[lower][chip] ^ shift, own_rows, lower * half, 0)
            for side, shift in enumerate((0, CORE)) for lower in range(2) for chip in range(4)
        ]
        attn_shapes = [((8, half, 4 * D), BF)] * 2
    else:
        slot = jnp.zeros((1,), jnp.int32)
        small = lax.all_gather(small, "fsdp", axis=0)
        space_w, attn_plan = gather_plain(attn_own[0])
        time_w, _ = gather_plain(attn_own[1])
        in_w, in_plan = gather_plain(mlp_in)
        out_w, _ = gather_plain(mlp_out)
        out_plan = [(0, 0, row, 0, FF_BLOCK, D, 0, 0, row, 0) for row in range(0, ff, FF_BLOCK)]
        in_targets, out_targets = plain_plan(D, ff), out_plan
        in_shapes, out_shapes = [((1, D, ff), BF)], [((1, ff, D), BF)]
        attn_targets, attn_shapes = plain_plan(D, 4 * D), [((1, D, 4 * D), BF)]
    slot = jnp.concatenate([slot, place[None]])
    small = small.astype(F32)

    def spread(first, count, inner):
        rows = small[:, first : first + count * inner].reshape(shards, count, inner, own_rows)
        return jnp.swapaxes(rows, 0, 1).reshape(count, shards * inner * own_rows)

    vectors = spread(0, 9, 1)
    qv, inb = spread(9, 2, 2), spread(13, 1, ff_rows)
    vectors, qv, space_w = tie((vectors, qv, space_w))

    state = [((ROWS, D), BF), ((ROWS, 3 * D), BF), ((BLOCKS * PAIRS, 2 * CHUNK, CHUNK), BF), ((ROWS, D), BF)]
    state_sems, peak = BLOCKS * PAIRS + 3, ((8, 128), F32)
    shares = [(split_shape[1:], BF)] * seq
    weight = ((D, 4 * D), BF)
    stripes = ((D // 128, ROWS, 128), F32)
    attn_flops = 2 * ROWS * D * 4 * D + 4 * BLOCKS * H * CHUNK * CHUNK * HD
    sums = ((8, D), F32)

    *parts, peak0, na0, proj0, soft0, ctx0 = call(
        functools.partial(space_forward_kernel, attn_plan, seq), shares + [peak], [((ROWS, D), F32), weight] + state,
        attn_flops, slot, (tok, vectors, qv), space_w, state, (state_sems, len(attn_plan)), name="space_forward",
    )
    parts = swap(parts)
    if by_chip:
        na0, first_x, first_y, first_out = tie((na0, first_x, first_y, first_out))
        near_x, near_y = jnp.stack([low, first_x[:half]]), jnp.stack([high, first_y])
        far_x, far_y = over_y(near_x), over_x(near_y)
        in_near, out_near = jnp.stack([mlp_in, first_x[half:]]), jnp.stack([mlp_out, first_out])
        parts, near_x, near_y, far_x, far_y, in_near, out_near = tie((parts, near_x, near_y, far_x, far_y, in_near, out_near))
        time_w = [near_x, far_x, near_y, far_y] + [over_core(piece) for piece in (near_x, far_x, near_y, far_y)]
        in_far, out_far = over_y(in_near), over_x(out_near)
        time_w, cot = tie((time_w, cot))
    gy = lax.all_to_all(cot, "seq", split_axis=0, concat_axis=0, tiled=True)
    x1, x2, peak1, na1, proj1, soft1, ctx1 = call(
        functools.partial(time_forward_kernel, attn_plan, seq), [((ROWS, D), BF), ((ROWS, D), F32), peak],
        [stripes, weight] + state, attn_flops, slot, [vectors, qv] + parts, time_w, state, (state_sems, len(attn_plan)),
        name="time_forward",
    )
    if by_chip:
        in_core, out_core = over_core(in_near), over_core(out_near)
        x2, gy, in_core, out_core, in_far, out_far = tie((x2, gy, in_core, out_core, in_far, out_far))
        in_w = [in_near, in_far, in_core, over_core(in_far)]
        out_w = [out_near, out_far, out_core, over_core(out_far)]

    mlp_sums, *results = call(
        functools.partial(mlp_kernel, seq, in_plan, out_plan, in_targets, out_targets),
        [sums] + shares + [((ROWS, D), F32)],
        [((ROWS, D), BF)] * 2 + [((ROWS, D), F32)] * 2 + [stripes] + [((D, ff), BF), ((ff, D), BF)] * 2,
        10 * ROWS * D * ff, slot, (x2, vectors, inb, gy), in_w + out_w, in_shapes + out_shapes,
        ((ff // FF_BLOCK, len(in_plan)), len(out_plan), (ff // FF_BLOCK, len(in_targets)), len(out_targets)), name="mlp",
    )
    mixed, (g2, *mlp_grads) = results[:seq], results[seq:]
    in_grads, out_grads = mlp_grads[: len(in_shapes)], mlp_grads[len(in_shapes) :]

    if by_chip:
        (in_keep, in_send), (out_keep, out_send) = in_grads, out_grads
        in_got, out_got = over_core(in_send), over_core(out_send)
        in_pair, out_pair = pair_of(in_keep, in_got, 0), pair_of(out_keep, out_got, 0)
        g2, in_pair, out_pair = tie((g2, in_pair, out_pair))
        in_came, out_came = over_x(in_pair), over_y(out_pair)
    mixed = swap(mixed)
    *parts, time_sums, gproj1, gbr1 = call(
        functools.partial(time_backward_kernel, attn_plan, seq),
        shares + [sums], [state[1], state[0], state[1], state[2], ((ROWS, D), BF), stripes, weight], 2 * attn_flops,
        slot, (g2, x1, vectors), time_w + [proj1, soft1], [state[1], state[0]], (len(attn_plan), 4), name="time_backward",
    )
    if by_chip:
        parts, mixed = tie((parts, mixed))
    parts = swap(parts)
    time_grads = call(
        functools.partial(weight_grad_kernel, attn_targets), [], [weight], attn_flops,
        slot, (na1, gproj1, ctx1, gbr1), (), attn_shapes, (len(attn_targets),), name="time_weight_grad", cost=COVER,
    )
    if by_chip:
        time_keep, time_send = time_grads
        parts[1], time_send, in_came, out_came = tie((parts[1], time_send, in_came, out_came))
        time_got = over_core(time_send)
        in_rest, out_rest = rest_of(in_keep, in_got, 0, in_came), rest_of(out_keep, out_got, 0, out_came)
        in_last, out_last = over_y(in_rest), over_x(out_rest)
        time_pairs = pair_of(time_keep, time_got, 0), pair_of(time_keep, time_got, 4)
        parts, time_pairs = tie((parts, time_pairs))
        time_came = over_x(time_pairs[0]), over_y(time_pairs[1])
    peaks = jnp.concatenate([peak0[0, :H], peak1[0, :H]])
    devices = shards * seq
    peaks = jnp.where(jnp.arange(devices)[:, None] == me * seq + place, peaks[None], 0.0).reshape(-1, D)
    g_tok, small_grads, *space_grads = call(
        functools.partial(space_backward_kernel, attn_plan, attn_targets, seq),
        [((local_len, D), F32), ((24 + peaks.shape[0], D), F32)],
        [((ROWS, D), F32), ((ROWS, 3 * D), BF), ((ROWS, D), BF), ((ROWS, D), BF), weight, weight]
        + [state[1], state[2], state[0], state[3]], 2 * attn_flops,
        slot, [tok, vectors, mlp_sums, time_sums, peaks] + parts, space_w + [proj0, soft0, na0, ctx0], attn_shapes,
        (len(attn_plan), len(attn_targets), 4),
        name="space_backward",
    )
    if by_chip:
        space_keep, space_send = space_grads
        space_send, in_last, out_last, time_came = tie((space_send, in_last, out_last, time_came))
        space_got = over_core(space_send)
        mlp_keep, mlp_send = seq_halves(jnp.concatenate([
            own_of(in_keep, in_got, 0, in_came, in_last), pack_rows(own_of(out_keep, out_got, 0, out_came, out_last)),
        ]))
        space_got, mlp_send, small_grads = tie((space_got, mlp_send, small_grads))
        mlp_came = hop(mlp_send, "seq", 1)
        space_pairs = pair_of(space_keep, space_got, 0), pair_of(space_keep, space_got, 4)
        space_came = over_x(space_pairs[0]), over_y(space_pairs[1])
        small_came = over_core(small_grads)
        mlp_came, time_came, small_came = tie((mlp_came, time_came, small_came))
        small_grads = small_grads + small_came
        time_rests = rest_of(time_keep, time_got, 0, time_came[0]), rest_of(time_keep, time_got, 4, time_came[1])
        time_lasts = over_y(time_rests[0]), over_x(time_rests[1])
        mlp_part = (mlp_keep + mlp_came.astype(F32)).astype(BF)
        mlp_came = [hop(piece, "seq", 2) for piece in jnp.split(mlp_part, 2)]
    if by_chip:
        space_came, small_grads, mixed, g_tok = tie((space_came, small_grads, mixed, g_tok))
        space_rests = rest_of(space_keep, space_got, 0, space_came[0]), rest_of(space_keep, space_got, 4, space_came[1])
        space_lasts = over_y(space_rests[0]), over_x(space_rests[1])
        time_keep, time_send = seq_halves(jnp.concatenate([
            own_of(time_keep, time_got, 0, time_came[0], time_lasts[0]), own_of(time_keep, time_got, 4, time_came[1], time_lasts[1]),
        ]))
        time_came = hop(time_send, "seq", 1)
        small_came = over_x(small_grads)
        space_lasts, small_came = tie((space_lasts, small_came))
        small_grads = small_grads + small_came
        space_keep, space_send = seq_halves(jnp.concatenate([
            own_of(space_keep, space_got, 0, space_came[0], space_lasts[0]),
            own_of(space_keep, space_got, 4, space_came[1], space_lasts[1]),
        ]))
        space_came = hop(space_send, "seq", 1)
        small_came = over_y(small_grads)
        time_part = (time_keep + time_came.astype(F32)).astype(BF)
        time_came = hop(time_part, "seq", 2)
        space_came, small_came, mlp_came = tie((space_came, small_came, mlp_came))
        small_grads = small_grads + small_came
        small_came = hop(small_grads, "seq", 1)
        mlp_part = (mlp_part.astype(F32) + jnp.concatenate(mlp_came).astype(F32)).astype(BF)
        space_part = (space_keep + space_came.astype(F32)).astype(BF)
        space_came = hop(space_part, "seq", 2)
        mlp_came = hop(mlp_part, "seq", 1)
        space_came, time_came, small_came = tie((space_came, time_came, small_came))
        small_grads = small_grads + small_came
        small_grads = small_grads + hop(small_grads, "seq", 2)
        mlp_total = seq_join(mlp_part, mlp_came)
        grad_in, grad_mout = mlp_total[:own_rows], unpack_rows(mlp_total[own_rows:])
        space_part = (space_part.astype(F32) + space_came.astype(F32)).astype(BF)
        time_part = (time_part.astype(F32) + time_came.astype(F32)).astype(BF)
        attn_totals = [seq_join(part, hop(part, "seq", 1)) for part in (space_part, time_part)]
    else:
        small_grads = lax.psum(small_grads, ("fsdp", "seq"))
        (in_grads,), (out_grads,) = in_grads, out_grads
        in_total, out_total, time_total, space_total = (
            reduce_plain(value) for value in (in_grads, out_grads, time_grads[0], space_grads[0])
        )
        grad_in, grad_mout = seq_total(in_total), seq_total(out_total)
        attn_totals = [seq_total(space_total), seq_total(time_total)]
    grad_qkv = jnp.stack([value[:, : 3 * D] for value in attn_totals])
    grad_out = jnp.stack([value[:, 3 * D :] for value in attn_totals])

    logit_max = jnp.max(small_grads[24:].reshape(devices, 2, H), axis=0)

    def share(rows, width):
        return lax.dynamic_slice_in_dim(rows.reshape(-1, shards * width), me * width, width, axis=1)

    pick = lambda *rows: jnp.concatenate([small_grads[row : row + 1] for row in rows])
    vector_grads = share(pick(16, 8, 0, 17, 9, 1, 18, 10, 2), own_rows)
    grad_gain, grad_shift, grad_outb, grad_moutb = vector_grads[0:3], vector_grads[3:6], vector_grads[6:8], vector_grads[8]
    grad_qv = share(pick(19, 20, 11, 12), 2 * own_rows)
    grad_inb = share(small_grads[3:7], ff // shards)[0]

    factor = threshold / jnp.maximum(logit_max, threshold)
    column_scale = jnp.repeat(jnp.sqrt(factor), HD, axis=1)
    clipped = attn_qkv[:, :, : 2 * D].astype(F32) * jnp.concatenate([column_scale, column_scale], axis=1)[:, None, :]
    mixed = jnp.swapaxes(by_distance(jnp.stack(mixed), place), 0, 1).reshape(tokens.shape)
    return (
        mixed, g_tok.reshape(tokens.shape), grad_gain, grad_shift, grad_qkv, grad_qv, grad_out, grad_outb,
        grad_in, grad_inb, grad_mout, grad_moutb, logit_max, clipped,
    )


def solution(mesh):
    placed = (
        P("fsdp", "seq", None), P(None, "fsdp"), P(None, "fsdp"), P(None, "fsdp", None), P(None, "fsdp"),
        P(None, "fsdp", None), P(None, "fsdp"), P("fsdp", None), P("fsdp"), P("fsdp", None), P("fsdp"), P(),
        P("fsdp", "seq", None),
    )
    return jax.shard_map(
        on_device,
        mesh=mesh,
        in_specs=placed,
        out_specs=(
            P("fsdp", "seq", None), P("fsdp", "seq", None), P(None, "fsdp"), P(None, "fsdp"), P(None, "fsdp", None),
            P(None, "fsdp"), P(None, "fsdp", None), P(None, "fsdp"), P("fsdp", None), P("fsdp"), P("fsdp", None),
            P("fsdp"), P(), P(None, "fsdp", None),
        ),
        check_vma=False,
    )
```

```python
import functools
import itertools

import jax
import jax.numpy as jnp
from jax import lax
from jax.experimental import pallas as pl
from jax.experimental.pallas import tpu as pltpu
from jax.sharding import PartitionSpec as P

H = 12
PATCHES = 196
HD = 64
D = 768
PAIRS = H // 2
CHUNK = 208
BLOCKS = 2
ROWS = BLOCKS * CHUNK
FF_BLOCK = 768
EPSILON = 1e-06
NEGATIVE = -1e30
SCALE = HD ** (-0.5)
COST, COVER = 1000, 40 * 2**20
VMEM_LIMIT = 58 * 1024 * 1024
BF = jnp.bfloat16
F32 = jnp.float32


def mm(a, b):
    return lax.dot_general(a, b, (((1,), (0,)), ((), ())), preferred_element_type=F32)


def mm_nt(a, b):
    return lax.dot_general(a, b, (((1,), (1,)), ((), ())), preferred_element_type=F32)


def mm_tn(a, b):
    return lax.dot_general(a, b, (((0,), (0,)), ((), ())), preferred_element_type=F32)


def row_stats(rows):
    centre = jnp.mean(rows, axis=-1, keepdims=True)
    centred = rows - centre
    second = jnp.mean(centred * centred, axis=-1, keepdims=True)
    inverse = lax.rsqrt(second + EPSILON)
    return centred * inverse, inverse


def norm_backward(grad, unit, inverse, gain):
    weighted = grad * gain
    first = jnp.mean(weighted, axis=-1, keepdims=True)
    second = jnp.mean(weighted * unit, axis=-1, keepdims=True)
    return (weighted - first - unit * second) * inverse


def column_sum(values):
    return jnp.sum(values.astype(F32), axis=0, keepdims=True)


def masks(temporal, block, frames):
    row = lax.broadcasted_iota(jnp.int32, (2 * CHUNK, CHUNK), 0)
    col = lax.broadcasted_iota(jnp.int32, (2 * CHUNK, CHUNK), 1)
    if temporal:
        row = jnp.where(row >= CHUNK, row - CHUNK, row)
        allowed = (row // frames) == (col // frames)
    else:
        allowed = col < PATCHES
    return allowed


def lower_lanes(rows):
    return lax.broadcasted_iota(jnp.int32, (rows, 2 * HD), 1) < HD


def split_heads(pair, scale=None):
    low_half = lower_lanes(pair.shape[0])
    if scale is not None:
        pair = pair * jnp.asarray(scale, pair.dtype)
    zero = jnp.zeros_like(pair)
    return jnp.where(low_half, pair, zero), jnp.where(low_half, zero, pair)


def attend_forward(proj_ref, ctx_ref, soft_ref, peak_ref, temporal, frames, valid, send):
    lane = lax.broadcasted_iota(jnp.int32, (8, 128), 1)
    peaks = jnp.full((8, 128), NEGATIVE, F32)
    for block in range(BLOCKS):
        allowed = masks(temporal, block, frames)
        rows = slice(block * CHUNK, (block + 1) * CHUNK)
        row_id = lax.broadcasted_iota(jnp.int32, (CHUNK, 1), 0)
        for pair in range(PAIRS):
            cols = slice(pair * 128, pair * 128 + 128)
            q_a, q_b = split_heads(proj_ref[rows, cols], SCALE)
            keys = proj_ref[rows, D + pair * 128 : D + pair * 128 + 128]
            v_a, v_b = split_heads(proj_ref[rows, 2 * D + pair * 128 : 2 * D + pair * 128 + 128])
            scores = mm_nt(jnp.concatenate([q_a, q_b], axis=0), keys)
            scores = jnp.where(allowed, scores, NEGATIVE)
            top = jnp.max(scores, axis=1, keepdims=True)
            expo = jnp.exp(scores - top)
            total = jnp.sum(expo, axis=1, keepdims=True)
            soft = (expo / total).astype(BF)
            soft_ref[block * PAIRS + pair] = soft
            send(block * PAIRS + pair)
            ctx_ref[rows, cols] = (mm(soft[:CHUNK], v_a) + mm(soft[CHUNK:], v_b)).astype(BF)
            for side in range(2):
                seen = jnp.where(row_id < valid[block], top[side * CHUNK : (side + 1) * CHUNK], NEGATIVE)
                best = jnp.max(seen, axis=0, keepdims=True)
                peaks = jnp.where(lane == 2 * pair + side, jnp.maximum(peaks, best), peaks)
    peak_ref[...] = peaks


def attend_backward(proj_ref, soft_ref, gctx_ref, gproj_ref):
    for block in range(BLOCKS):
        rows = slice(block * CHUNK, (block + 1) * CHUNK)
        for pair in range(PAIRS):
            cols = slice(pair * 128, pair * 128 + 128)
            kcols = slice(D + pair * 128, D + pair * 128 + 128)
            vcols = slice(2 * D + pair * 128, 2 * D + pair * 128 + 128)
            q_pair = jnp.concatenate(split_heads(proj_ref[rows, cols], SCALE), axis=0)
            k_a, k_b = split_heads(proj_ref[rows, kcols], SCALE)
            values = proj_ref[rows, vcols]
            g_pair = jnp.concatenate(split_heads(gctx_ref[rows, cols]), axis=0)
            soft_low = soft_ref[block * PAIRS + pair]
            soft = soft_low.astype(F32)
            grad_soft = mm_nt(g_pair, values)
            inner = jnp.sum(soft * grad_soft, axis=1, keepdims=True)
            grad_scores = (soft * (grad_soft - inner)).astype(BF)
            gproj_ref[rows, cols] = (mm(grad_scores[:CHUNK], k_a) + mm(grad_scores[CHUNK:], k_b)).astype(BF)
            gproj_ref[rows, kcols] = mm_tn(grad_scores, q_pair).astype(BF)
            gproj_ref[rows, vcols] = mm_tn(soft_low, g_pair).astype(BF)


def blocks_between(slot_ref, arrays, plan, weight_ref):
    for array, index, row, column, height, width, place, scale, first, at in plan:
        start = pl.multiple_of(slot_ref[place] * scale + first, 16)
        yield (
            arrays[array].at[index, row : row + height, column : column + width],
            weight_ref.at[pl.ds(start, height), at : at + width],
        )


def fetch(slot_ref, pieces, plan, weight_ref, sems):
    copies = []
    for number, (piece, part) in enumerate(blocks_between(slot_ref, pieces, plan, weight_ref)):
        copies.append(pltpu.make_async_copy(piece, part, sems.at[number]))
        copies[-1].start()
    return copies


def deliver(slot_ref, weight_ref, targets, plan, sems):
    copies = []
    for number, (piece, part) in enumerate(blocks_between(slot_ref, targets, plan, weight_ref)):
        copies.append(pltpu.make_async_copy(part, piece, sems.at[number]))
        copies[-1].start()
    return copies


def take(refs, plan):
    count = 1 + max(entry[0] for entry in plan)
    return refs[:count], refs[count:]


def sender(sources, targets, sems):
    started = []

    def send(number):
        copy = pltpu.make_async_copy(sources[number], targets[number], sems.at[number])
        copy.start()
        started.append(copy)

    return send, started


def saved_state(refs):
    targets, (na_ref, proj_ref, soft_ref, ctx_ref), sems = refs[:4], refs[4:8], refs[8]
    count = soft_ref.shape[0]
    sources = [soft_ref.at[k] for k in range(count)] + [na_ref, proj_ref, ctx_ref]
    places = [targets[2].at[k] for k in range(count)] + [targets[0], targets[1], targets[3]]
    send, started = sender(sources, places, sems)
    return na_ref, proj_ref, soft_ref, ctx_ref, count, send, started


def finish(copies):
    for copy in copies:
        copy.wait()


def project(na_ref, qkv_ref, qv, proj_ref):
    for part in range(3):
        cols = slice(part * D, (part + 1) * D)
        value = mm(na_ref[...], qkv_ref[:, cols])
        if part != 1:
            at = 0 if part == 0 else D
            value = value + qv[:, at : at + D]
        proj_ref[:, cols] = value.astype(BF)


def pad_frames(tok_ref, rows_ref):
    count = tok_ref.shape[0]
    flat = tok_ref[...].astype(F32)
    rows_ref[0:count, :] = flat
    rows_ref[CHUNK : CHUNK + PATCHES, :] = flat[PATCHES:, :]
    rows_ref[PATCHES:CHUNK, :] = jnp.zeros((CHUNK - PATCHES, D), F32)
    rows_ref[CHUNK + PATCHES :, :] = jnp.zeros((CHUNK - PATCHES, D), F32)


def space_forward_kernel(plan, seq, slot_ref, tok_ref, vec_ref, qv_ref, *refs):
    pieces, refs = take(refs, plan)
    part_refs, refs = refs[:seq], refs[seq:]
    peak_ref, *refs = refs
    na_ref, proj_ref, soft_ref, ctx_ref, count, send, started = saved_state(refs[:4] + refs[6:11])
    rows_ref, weight_ref, sems = refs[4], refs[5], refs[-1]
    copies = fetch(slot_ref, pieces, plan, weight_ref, sems)
    pad_frames(tok_ref, rows_ref)
    unit, _ = row_stats(rows_ref[...])
    na_ref[...] = (unit * vec_ref[0:1] + vec_ref[3:4]).astype(BF)
    send(count)
    finish(copies)
    project(na_ref, weight_ref, qv_ref[0:1], proj_ref)
    send(count + 1)
    attend_forward(proj_ref, ctx_ref, soft_ref, peak_ref, False, 0, (PATCHES, PATCHES), send)
    send(count + 2)
    rows_ref[...] = rows_ref[...] + mm(ctx_ref[...], weight_ref[:, 3 * D :]) + vec_ref[6:7]
    frames, width = part_refs[0].shape[0], part_refs[0].shape[1]

    def body(place):
        for distance in range(seq):
            for frame in range(frames):
                start = frame * CHUNK + (place ^ distance) * width
                part_refs[distance][frame] = rows_ref[start : start + width, :].astype(BF)

    for_place(slot_ref, seq, body)
    finish(started)


def for_place(slot_ref, count, body):
    for place in range(count):
        pl.when(slot_ref[slot_ref.shape[0] - 1] == place)(functools.partial(body, place))


def interleave(slot_ref, part_refs, stripes_ref, rows_ref):
    shares, frames, width = len(part_refs), part_refs[0].shape[0], part_refs[0].shape[1]
    total = shares * frames
    place = 0 if slot_ref is None else slot_ref[slot_ref.shape[0] - 1]
    for stripe in range(D // 128):
        cols = slice(stripe * 128, stripe * 128 + 128)
        for distance in range(shares):
            for frame in range(frames):
                first = (place ^ distance) * frames + frame
                stripes_ref[stripe, pl.ds(first, width, stride=total), :] = part_refs[distance][frame, :, cols].astype(F32)
        stripes_ref[stripe, total * width :, :] = jnp.zeros((ROWS - total * width, 128), F32)
        rows_ref[:, cols] = stripes_ref[stripe].astype(rows_ref.dtype)


def separate(slot_ref, rows, stripes_ref, part_refs):
    shares, frames, width = len(part_refs), part_refs[0].shape[0], part_refs[0].shape[1]
    total = shares * frames
    place = slot_ref[slot_ref.shape[0] - 1]
    for stripe in range(D // 128):
        cols = slice(stripe * 128, stripe * 128 + 128)
        stripes_ref[stripe] = rows[:, cols]
        for distance in range(shares):
            for frame in range(frames):
                first = (place ^ distance) * frames + frame
                part_refs[distance][frame, :, cols] = stripes_ref[stripe, pl.ds(first, width, stride=total), :].astype(
                    part_refs[distance].dtype
                )


def time_forward_kernel(plan, seq, slot_ref, vec_ref, qv_ref, *refs):
    part_refs, refs = refs[:seq], refs[seq:]
    pieces, refs = take(refs, plan)
    x1_ref, x2_ref, peak_ref, *refs = refs
    na_ref, proj_ref, soft_ref, ctx_ref, count, send, started = saved_state(refs[:4] + refs[6:11])
    stripes_ref, weight_ref, sems = refs[4], refs[5], refs[-1]
    copies = fetch(slot_ref, pieces, plan, weight_ref, sems)
    frames = seq * part_refs[0].shape[0]
    tokens = frames * part_refs[0].shape[1]
    interleave(slot_ref, part_refs, stripes_ref, x1_ref)
    unit, _ = row_stats(x1_ref[...].astype(F32))
    na_ref[...] = (unit * vec_ref[1:2] + vec_ref[4:5]).astype(BF)
    send(count)
    finish(copies)
    project(na_ref, weight_ref, qv_ref[1:2], proj_ref)
    send(count + 1)
    attend_forward(proj_ref, ctx_ref, soft_ref, peak_ref, True, frames, (CHUNK, tokens - CHUNK), send)
    send(count + 2)
    x2_ref[...] = x1_ref[...].astype(F32) + mm(ctx_ref[...], weight_ref[:, 3 * D :]) + vec_ref[7:8]
    finish(started)


def mlp_kernel(seq, in_plan, out_plan, in_targets, out_targets, slot_ref, x2_ref, vec_ref, inb_ref, gy_ref, *refs):
    in_pieces, refs = take(refs, in_plan)
    out_pieces, refs = take(refs, out_plan)
    sums_ref, *refs = refs
    mixed_refs, refs = refs[:seq], refs[seq:]
    g2_ref, *refs = refs
    gin_arrays, refs = take(refs, in_targets)
    gout_arrays, refs = take(refs, out_targets)
    (
        n2_ref, gyl_ref, rows_ref, back_ref, stripes_ref, in_ref, out_ref, gin_ref, gout_ref,
        in_sems, out_sems, gin_sems, gout_sems,
    ) = refs
    blocks = in_ref.shape[1] // FF_BLOCK
    out_height = out_plan[0][4]
    rows_each = FF_BLOCK // out_height

    def span_of(step):
        return pl.ds(pl.multiple_of(step * FF_BLOCK, FF_BLOCK), FF_BLOCK)

    def in_copies(step):
        return [
            pltpu.make_async_copy(piece.at[:, span_of(step)], part.at[:, span_of(step)], in_sems.at[step, number])
            for number, (piece, part) in enumerate(blocks_between(slot_ref, in_pieces, in_plan, in_ref))
        ]

    def gin_copies(step):
        return [
            pltpu.make_async_copy(part.at[:, span_of(step)], piece.at[:, span_of(step)], gin_sems.at[step, number])
            for number, (piece, part) in enumerate(blocks_between(slot_ref, gin_arrays, in_targets, gin_ref))
        ]

    def first_row(entry):
        return slot_ref[entry[6]] * entry[7] + entry[8]

    for step in range(blocks):
        for copy in in_copies(step):
            copy.start()
        if step == 0:
            for entry, (piece, part) in zip(out_plan, blocks_between(slot_ref, out_pieces, out_plan, out_ref)):
                pltpu.make_async_copy(piece, part, out_sems.at[first_row(entry) // out_height]).start()
    unit, _ = row_stats(x2_ref[...])
    n2_ref[...] = (unit * vec_ref[2:3] + vec_ref[5:6]).astype(BF)
    interleave(None, [gy_ref.at[share] for share in range(seq)], stripes_ref, gyl_ref)
    sums_ref[2:3] = column_sum(gyl_ref[...])
    rows_ref[...] = jnp.zeros_like(rows_ref)
    back_ref[...] = jnp.zeros_like(back_ref)
    gout_copies = [
        pltpu.make_async_copy(part, piece, gout_sems.at[number])
        for number, (piece, part) in enumerate(blocks_between(slot_ref, gout_arrays, out_targets, gout_ref))
    ]

    @pl.loop(0, blocks)
    def _(step):
        span = span_of(step)
        for copy in in_copies(step):
            copy.wait()
        for number in range(rows_each):
            part = out_ref.at[0:out_height, :]
            pltpu.make_async_copy(part, part, out_sems.at[step * rows_each + number]).wait()
        hidden = mm(n2_ref[...], in_ref[:, span]) + inb_ref[:, span]
        cumulative = 0.5 * (1.0 + lax.erf(hidden * (2.0 ** -0.5)))
        act = (hidden * cumulative).astype(BF)
        slope = cumulative + hidden * jnp.exp(-0.5 * hidden * hidden) * 0.3989422804014327
        rows_ref[...] += mm(act, out_ref[span, :])
        gout_ref[span, :] = mm_tn(act, gyl_ref[...]).astype(BF)
        for copy, entry in zip(gout_copies, out_targets):
            pl.when(first_row(entry) // FF_BLOCK == step)(copy.start)
        ghid = (mm_nt(gyl_ref[...], out_ref[span, :]) * slope).astype(BF)
        sums_ref[pl.ds(3 + step, 1), :] = column_sum(ghid)
        gin_ref[:, span] = mm_tn(n2_ref[...], ghid).astype(BF)
        for copy in gin_copies(step):
            copy.start()
        back_ref[...] += mm_nt(ghid, in_ref[:, span])

    separate(slot_ref, x2_ref[...] + rows_ref[...] + vec_ref[8:9], stripes_ref, mixed_refs)
    unit, inverse = row_stats(x2_ref[...])
    grad = back_ref[...]
    sums_ref[0:1] = column_sum(grad * unit)
    sums_ref[1:2] = column_sum(grad)
    sums_ref[7:8] = jnp.zeros((1, D), F32)
    g2_ref[...] = gyl_ref[...].astype(F32) + norm_backward(grad, unit, inverse, vec_ref[2:3])
    for step in range(blocks):
        finish(gin_copies(step))
    finish(gout_copies)


def branch_backward(g_ref, proj_ref, soft_ref, weight_ref, sums_ref, gproj_ref, gbr_ref, gctx_ref, awaited):
    gbr_ref[...] = g_ref[...].astype(BF)
    sums_ref[2:3] = column_sum(gbr_ref[...])
    gctx_ref[...] = mm_nt(gbr_ref[...], weight_ref[:, 3 * D :]).astype(BF)
    finish(awaited)
    attend_backward(proj_ref, soft_ref, gctx_ref, gproj_ref)
    sums_ref[3:4] = column_sum(gproj_ref[:, 0:D])
    sums_ref[4:5] = column_sum(gproj_ref[:, 2 * D :])
    sums_ref[5:8] = jnp.zeros((3, D), F32)


def projection_backward(gproj_ref, weight_ref):
    total = mm_nt(gproj_ref[:, 0:D], weight_ref[:, 0:D])
    for part in range(1, 3):
        cols = slice(part * D, (part + 1) * D)
        total = total + mm_nt(gproj_ref[:, cols], weight_ref[:, cols])
    return total


def weight_grads(na_ref, gproj_ref, ctx_ref, gbr_ref, grad_ref):
    grad_ref[:, 3 * D :] = mm_tn(ctx_ref[...], gbr_ref[...]).astype(BF)
    for part in range(3):
        cols = slice(part * D, (part + 1) * D)
        grad_ref[:, cols] = mm_tn(na_ref[...], gproj_ref[:, cols]).astype(BF)


def time_backward_kernel(plan, seq, slot_ref, g_ref, x1_ref, vec_ref, *refs):
    pieces, refs = take(refs, plan)
    kept, refs = refs[:2], refs[2:]
    part_refs, refs = refs[:seq], refs[seq:]
    sums_ref, gproj_to, gbr_to, gproj_ref, gbr_ref, proj_ref, soft_ref, gctx_ref, stripes_ref, weight_ref, sems, more = refs
    copies = fetch(slot_ref, pieces, plan, weight_ref, sems)
    send, started = sender((kept[0], kept[1], gproj_ref, gbr_ref), (proj_ref, soft_ref, gproj_to, gbr_to), more)
    send(0)
    send(1)
    finish(copies)
    branch_backward(g_ref, proj_ref, soft_ref, weight_ref, sums_ref, gproj_ref, gbr_ref, gctx_ref, started)
    send(2)
    send(3)
    grad = projection_backward(gproj_ref, weight_ref)
    unit, inverse = row_stats(x1_ref[...].astype(F32))
    sums_ref[0:1] = column_sum(grad * unit)
    sums_ref[1:2] = column_sum(grad)
    separate(slot_ref, g_ref[...] + norm_backward(grad, unit, inverse, vec_ref[1:2]), stripes_ref, part_refs)
    finish(started[2:])


def weight_grad_kernel(targets, slot_ref, na_ref, gproj_ref, ctx_ref, gbr_ref, *refs):
    outs, (grad_ref, sems) = take(refs, targets)
    weight_grads(na_ref, gproj_ref, ctx_ref, gbr_ref, grad_ref)
    finish(deliver(slot_ref, grad_ref, outs, targets, sems))


def space_backward_kernel(
    plan, targets, seq, slot_ref, tok_ref, vec_ref, mlp_sums_ref, time_sums_ref, peaks_ref, *refs
):
    part_refs, refs = refs[:seq], refs[seq:]
    pieces, refs = take(refs, plan)
    kept, refs = refs[:4], refs[4:]
    gtok_ref, all_sums_ref, *refs = refs
    sums_ref = all_sums_ref.at[16:24]
    outs, refs = take(refs, targets)
    g_ref, gproj_ref, gbr_ref, gctx_ref, weight_ref, grad_ref, *local, sems, grad_sems, more = refs
    copies = fetch(slot_ref, pieces, plan, weight_ref, sems)
    send, started = sender(kept, local, more)
    for number in range(4):
        send(number)
    proj_ref, soft_ref, na_ref, ctx_ref = local
    frames, width = part_refs[0].shape[0], part_refs[0].shape[1]

    def body(place):
        for frame in range(frames):
            for distance in range(seq):
                start = frame * CHUNK + (place ^ distance) * width
                g_ref[start : start + width, :] = part_refs[distance][frame].astype(F32)

    for_place(slot_ref, seq, body)
    all_sums_ref[0:8] = mlp_sums_ref[...]
    all_sums_ref[8:16] = time_sums_ref[...]
    all_sums_ref[24:] = peaks_ref[...]
    for frame in range(frames):
        g_ref[frame * CHUNK + PATCHES : (frame + 1) * CHUNK, :] = jnp.zeros((CHUNK - PATCHES, D), F32)
    finish(copies)
    branch_backward(g_ref, proj_ref, soft_ref, weight_ref, sums_ref, gproj_ref, gbr_ref, gctx_ref, started)
    weight_grads(na_ref, gproj_ref, ctx_ref, gbr_ref, grad_ref)
    copies = deliver(slot_ref, grad_ref, outs, targets, grad_sems)
    grad = projection_backward(gproj_ref, weight_ref)
    total = g_ref[...]
    pad_frames(tok_ref, g_ref)
    unit, inverse = row_stats(g_ref[...])
    sums_ref[0:1] = column_sum(grad * unit)
    sums_ref[1:2] = column_sum(grad)
    g_ref[...] = total + norm_backward(grad, unit, inverse, vec_ref[0:1])
    gtok_ref[0:PATCHES, :] = g_ref[0:PATCHES, :]
    gtok_ref[PATCHES:, :] = g_ref[CHUNK : CHUNK + PATCHES, :]
    finish(copies)


def call(kernel, outs, scratch, flops, slot, operands, pieces=(), targets=(), sems=(), *, name, cost=COST):
    whole = pl.BlockSpec(memory_space=pltpu.VMEM)
    far = pl.BlockSpec(memory_space=pl.ANY)
    return pl.pallas_call(
        kernel,
        in_specs=[pl.BlockSpec(memory_space=pltpu.SMEM)] + [whole] * len(operands) + [far] * len(pieces),
        out_specs=[whole] * len(outs) + [far] * len(targets),
        out_shape=[jax.ShapeDtypeStruct(shape, dtype) for shape, dtype in list(outs) + list(targets)],
        scratch_shapes=[pltpu.VMEM(shape, dtype) for shape, dtype in scratch]
        + [pltpu.SemaphoreType.DMA(count if isinstance(count, tuple) else (count,)) for count in sems],
        compiler_params=pltpu.CompilerParams(vmem_limit_bytes=VMEM_LIMIT),
        cost_estimate=pl.CostEstimate(flops=1000, bytes_accessed=cost, transcendentals=0),
        name=name,
    )(slot, *operands, *pieces)


def hop(value, axis, bit):
    return lax.ppermute(value, axis, [(index, index ^ bit) for index in range(lax.axis_size(axis))])


CORE, CHIP_X, CHIP_Y = 1, 2, 4
X_ORDER = (0, CHIP_Y, CHIP_X, CHIP_X | CHIP_Y)
Y_ORDER = (0, CHIP_X, CHIP_Y, CHIP_X | CHIP_Y)


def pack_rows(value):
    return jnp.concatenate(jnp.split(value, 4, axis=0), axis=1)


def unpack_rows(value):
    return jnp.concatenate(jnp.split(value, 4, axis=1), axis=0)


def targets_of(height, width, order):
    return [
        (side, chip, 0, 0, height, width, order[chip] ^ shift, height, 0, 0)
        for side, shift in enumerate((0, CORE)) for chip in range(4)
    ]


def gather_plain(own):
    full = lax.all_gather(own[None], "fsdp", axis=1, tiled=True)
    return [full], plain_plan(full.shape[1], full.shape[2])


def plain_plan(rows, columns):
    return [(0, 0, 0, 0, rows, columns, 0, 0, 0, 0)]


tie = lax.optimization_barrier


def sums_of(keep, got):
    return lambda part: keep[part].astype(F32) + got[part].astype(F32)


def pair_of(keep, got, first):
    return sums_of(keep, got)(slice(first + 2, first + 4)).astype(BF)


def rest_of(keep, got, first, came):
    return (sums_of(keep, got)(first + 1) + came[1].astype(F32)).astype(BF)


def own_of(keep, got, first, came, last):
    return sums_of(keep, got)(first) + came[0].astype(F32) + last.astype(F32)


def over_x(value):
    return hop(value, "fsdp", CHIP_X)


def over_y(value):
    return hop(value, "fsdp", CHIP_Y)


def over_core(value):
    return hop(value, "fsdp", CORE)


def reduce_plain(grad):
    return lax.psum_scatter(grad[0], "fsdp", scatter_dimension=0, tiled=True).astype(F32)


def seq_halves(value):
    odd = (lax.axis_index("seq") & 1) == 1
    half = value.shape[0] // 2
    low, high = value[:half], value[half:]
    return jnp.where(odd, high, low), jnp.where(odd, low, high).astype(BF)


def seq_first(value):
    mine, other = seq_halves(value)
    return (mine + hop(other, "seq", 1).astype(F32)).astype(BF)


def seq_second(part):
    return (part.astype(F32) + hop(part, "seq", 2).astype(F32)).astype(BF)


def seq_join(part, other):
    odd = (lax.axis_index("seq") & 1) == 1
    return jnp.where(odd, jnp.concatenate([other, part]), jnp.concatenate([part, other])).astype(F32)


def seq_total(value):
    if lax.axis_size("seq") != 4:
        return lax.psum(value.astype(BF), "seq").astype(F32)
    part = seq_second(seq_first(value))
    return seq_join(part, hop(part, "seq", 1))


def by_distance(parts, place):
    shape = parts.shape
    bit = 1
    while bit < shape[0]:
        paired = parts.reshape((shape[0] // (2 * bit), 2, bit) + shape[1:])
        parts = jnp.where((place & bit) != 0, paired[:, ::-1], paired).reshape(shape)
        bit *= 2
    return parts


def swap(parts):
    return [parts[0]] + [hop(parts[distance], "seq", distance) for distance in range(1, len(parts))]


def on_device(
    tokens, norm_gain, norm_bias, attn_qkv, attn_qv_bias, attn_out, attn_out_bias,
    mlp_in, mlp_in_bias, mlp_out, mlp_out_bias, threshold, cotangent,
):
    clip_count, local_len, _ = tokens.shape
    seq, shards = lax.axis_size("seq"), lax.axis_size("fsdp")
    me = lax.axis_index("fsdp")
    frames = local_len // PATCHES
    width = PATCHES // seq
    own_rows = D // shards
    ff = mlp_in.shape[1]
    split_shape = (seq, frames, width, D)
    tok = tokens.reshape(local_len, D)
    cot = jnp.swapaxes(cotangent.reshape(frames, seq, width, D), 0, 1)
    by_chip = shards == 8

    attn_own = [jnp.concatenate([attn_qkv[a], attn_out[a]], axis=1) for a in range(2)]
    small = jnp.concatenate([
        norm_gain, norm_bias, attn_out_bias, mlp_out_bias.reshape(1, own_rows), attn_qv_bias.reshape(-1, own_rows),
        mlp_in_bias.reshape(-1, own_rows),
    ])
    place = lax.axis_index("seq")
    half = own_rows // 2
    ff_rows = ff // D
    if by_chip:
        slot = me ^ jnp.arange(shards, dtype=jnp.int32)
        low, high = attn_own[0][:half], attn_own[0][half:]
        near_x, near_y = jnp.stack([low, over_x(low)]), jnp.stack([high, over_y(high)])
        core_x, core_y = over_core(near_x), over_core(near_y)
        core_x, core_y, small = tie((core_x, core_y, small))
        small = jnp.stack([small, over_x(small), over_y(small), hop(small, "fsdp", CHIP_X | CHIP_Y)])
        far_x, far_y = over_y(near_x), over_x(near_y)
        small = jnp.stack([small, over_core(small)], axis=1).reshape((shards,) + small.shape[1:])
        small = by_distance(small, me)
        low, high = attn_own[1][:half], attn_own[1][half:]
        first_x, first_y, first_out = jnp.concatenate([low, mlp_in]), high, mlp_out
        far_x, far_y, core_x, core_y, first_x, first_y, first_out = tie(
            (far_x, far_y, core_x, core_y, first_x, first_y, first_out)
        )
        first_x, first_y, first_out = over_x(first_x), over_y(first_y), over_y(first_out)
        space_w = [near_x, far_x, near_y, far_y, core_x, over_core(far_x), core_y, over_core(far_y)]
        places = ((0, CHIP_X), (CHIP_Y, CHIP_X | CHIP_Y), (0, CHIP_Y), (CHIP_X, CHIP_X | CHIP_Y))
        attn_plan, in_plan, out_plan, out_rows = [], [], [], mlp_out.shape[0]
        for array in range(8):
            shift, lower = (0 if array < 4 else CORE), array % 4 < 2
            for index, owner in enumerate(places[array % 4]):
                owner = owner ^ shift
                attn_plan.append((array, index, 0, 0, half, 4 * D, owner, own_rows, 0 if lower else half, 0))
                array_of = array % 2 + (0 if array < 4 else 2)
                if lower:
                    in_plan.append((array_of, index, 0, 0, own_rows, ff, owner, own_rows, 0, 0))
                else:
                    out_plan.append((array_of, index, 0, 0, out_rows, D, owner, out_rows, 0, 0))
        in_targets, out_targets = targets_of(own_rows, ff, X_ORDER), targets_of(out_rows, D, Y_ORDER)
        in_shapes, out_shapes = [((4, own_rows, ff), BF)] * 2, [((4, out_rows, D), BF)] * 2
        attn_targets = [
            (side, 4 * lower + chip, 0, 0, half, 4 * D, (X_ORDER, Y_ORDER)[lower][chip] ^ shift, own_rows, lower * half, 0)
            for side, shift in enumerate((0, CORE)) for lower in range(2) for chip in range(4)
        ]
        attn_shapes = [((8, half, 4 * D), BF)] * 2
    else:
        slot = jnp.zeros((1,), jnp.int32)
        small = lax.all_gather(small, "fsdp", axis=0)
        space_w, attn_plan = gather_plain(attn_own[0])
        time_w, _ = gather_plain(attn_own[1])
        in_w, in_plan = gather_plain(mlp_in)
        out_w, _ = gather_plain(mlp_out)
        out_plan = [(0, 0, row, 0, FF_BLOCK, D, 0, 0, row, 0) for row in range(0, ff, FF_BLOCK)]
        in_targets, out_targets = plain_plan(D, ff), out_plan
        in_shapes, out_shapes = [((1, D, ff), BF)], [((1, ff, D), BF)]
        attn_targets, attn_shapes = plain_plan(D, 4 * D), [((1, D, 4 * D), BF)]
    slot = jnp.concatenate([slot, place[None]])
    small = small.astype(F32)

    def spread(first, count, inner):
        rows = small[:, first : first + count * inner].reshape(shards, count, inner, own_rows)
        return jnp.swapaxes(rows, 0, 1).reshape(count, shards * inner * own_rows)

    vectors = spread(0, 9, 1)
    qv, inb = spread(9, 2, 2), spread(13, 1, ff_rows)
    vectors, qv, space_w = tie((vectors, qv, space_w))

    state = [((ROWS, D), BF), ((ROWS, 3 * D), BF), ((BLOCKS * PAIRS, 2 * CHUNK, CHUNK), BF), ((ROWS, D), BF)]
    state_sems, peak = BLOCKS * PAIRS + 3, ((8, 128), F32)
    shares = [(split_shape[1:], BF)] * seq
    weight = ((D, 4 * D), BF)
    stripes = ((D // 128, ROWS, 128), F32)
    attn_flops = 2 * ROWS * D * 4 * D + 4 * BLOCKS * H * CHUNK * CHUNK * HD
    sums = ((8, D), F32)

    *parts, peak0, na0, proj0, soft0, ctx0 = call(
        functools.partial(space_forward_kernel, attn_plan, seq), shares + [peak], [((ROWS, D), F32), weight] + state,
        attn_flops, slot, (tok, vectors, qv), space_w, state, (state_sems, len(attn_plan)), name="space_forward",
    )
    parts = swap(parts)
    if by_chip:
        na0, first_x, first_y, first_out = tie((na0, first_x, first_y, first_out))
        near_x, near_y = jnp.stack([low, first_x[:half]]), jnp.stack([high, first_y])
        far_x, far_y = over_y(near_x), over_x(near_y)
        in_near, out_near = jnp.stack([mlp_in, first_x[half:]]), jnp.stack([mlp_out, first_out])
        parts, near_x, near_y, far_x, far_y, in_near, out_near = tie((parts, near_x, near_y, far_x, far_y, in_near, out_near))
        time_w = [near_x, far_x, near_y, far_y] + [over_core(piece) for piece in (near_x, far_x, near_y, far_y)]
        in_far, out_far = over_y(in_near), over_x(out_near)
        time_w, cot = tie((time_w, cot))
    gy = lax.all_to_all(cot, "seq", split_axis=0, concat_axis=0, tiled=True)
    x1, x2, peak1, na1, proj1, soft1, ctx1 = call(
        functools.partial(time_forward_kernel, attn_plan, seq), [((ROWS, D), BF), ((ROWS, D), F32), peak],
        [stripes, weight] + state, attn_flops, slot, [vectors, qv] + parts, time_w, state, (state_sems, len(attn_plan)),
        name="time_forward",
    )
    if by_chip:
        in_core, out_core = over_core(in_near), over_core(out_near)
        x2, gy, in_core, out_core, in_far, out_far = tie((x2, gy, in_core, out_core, in_far, out_far))
        in_w = [in_near, in_far, in_core, over_core(in_far)]
        out_w = [out_near, out_far, out_core, over_core(out_far)]

    mlp_sums, *results = call(
        functools.partial(mlp_kernel, seq, in_plan, out_plan, in_targets, out_targets),
        [sums] + shares + [((ROWS, D), F32)],
        [((ROWS, D), BF)] * 2 + [((ROWS, D), F32)] * 2 + [stripes] + [((D, ff), BF), ((ff, D), BF)] * 2,
        10 * ROWS * D * ff, slot, (x2, vectors, inb, gy), in_w + out_w, in_shapes + out_shapes,
        ((ff // FF_BLOCK, len(in_plan)), len(out_plan), (ff // FF_BLOCK, len(in_targets)), len(out_targets)), name="mlp",
    )
    mixed, (g2, *mlp_grads) = results[:seq], results[seq:]
    in_grads, out_grads = mlp_grads[: len(in_shapes)], mlp_grads[len(in_shapes) :]

    if by_chip:
        (in_keep, in_send), (out_keep, out_send) = in_grads, out_grads
        in_got, out_got = over_core(in_send), over_core(out_send)
        in_pair, out_pair = pair_of(in_keep, in_got, 0), pair_of(out_keep, out_got, 0)
        g2, in_pair, out_pair = tie((g2, in_pair, out_pair))
        in_came, out_came = over_x(in_pair), over_y(out_pair)
    mixed = swap(mixed)
    *parts, time_sums, gproj1, gbr1 = call(
        functools.partial(time_backward_kernel, attn_plan, seq),
        shares + [sums], [state[1], state[0], state[1], state[2], ((ROWS, D), BF), stripes, weight], 2 * attn_flops,
        slot, (g2, x1, vectors), time_w + [proj1, soft1], [state[1], state[0]], (len(attn_plan), 4), name="time_backward",
    )
    if by_chip:
        parts, mixed = tie((parts, mixed))
    parts = swap(parts)
    time_grads = call(
        functools.partial(weight_grad_kernel, attn_targets), [], [weight], attn_flops,
        slot, (na1, gproj1, ctx1, gbr1), (), attn_shapes, (len(attn_targets),), name="time_weight_grad", cost=COVER,
    )
    if by_chip:
        time_keep, time_send = time_grads
        parts[1], time_send, in_came, out_came = tie((parts[1], time_send, in_came, out_came))
        time_got = over_core(time_send)
        in_rest, out_rest = rest_of(in_keep, in_got, 0, in_came), rest_of(out_keep, out_got, 0, out_came)
        in_last, out_last = over_y(in_rest), over_x(out_rest)
        time_pairs = pair_of(time_keep, time_got, 0), pair_of(time_keep, time_got, 4)
        parts, time_pairs = tie((parts, time_pairs))
        time_came = over_x(time_pairs[0]), over_y(time_pairs[1])
    peaks = jnp.concatenate([peak0[0, :H], peak1[0, :H]])
    devices = shards * seq
    peaks = jnp.where(jnp.arange(devices)[:, None] == me * seq + place, peaks[None], 0.0).reshape(-1, D)
    g_tok, small_grads, *space_grads = call(
        functools.partial(space_backward_kernel, attn_plan, attn_targets, seq),
        [((local_len, D), F32), ((24 + peaks.shape[0], D), F32)],
        [((ROWS, D), F32), ((ROWS, 3 * D), BF), ((ROWS, D), BF), ((ROWS, D), BF), weight, weight]
        + [state[1], state[2], state[0], state[3]], 2 * attn_flops,
        slot, [tok, vectors, mlp_sums, time_sums, peaks] + parts, space_w + [proj0, soft0, na0, ctx0], attn_shapes,
        (len(attn_plan), len(attn_targets), 4),
        name="space_backward",
    )
    if by_chip:
        space_keep, space_send = space_grads
        space_send, in_last, out_last, time_came = tie((space_send, in_last, out_last, time_came))
        space_got = over_core(space_send)
        mlp_keep, mlp_send = seq_halves(jnp.concatenate([
            own_of(in_keep, in_got, 0, in_came, in_last), pack_rows(own_of(out_keep, out_got, 0, out_came, out_last)),
        ]))
        space_got, mlp_send, small_grads = tie((space_got, mlp_send, small_grads))
        mlp_came = hop(mlp_send, "seq", 1)
        space_pairs = pair_of(space_keep, space_got, 0), pair_of(space_keep, space_got, 4)
        space_came = over_x(space_pairs[0]), over_y(space_pairs[1])
        small_came = over_core(small_grads)
        mlp_came, time_came, small_came = tie((mlp_came, time_came, small_came))
        small_grads = small_grads + small_came
        time_rests = rest_of(time_keep, time_got, 0, time_came[0]), rest_of(time_keep, time_got, 4, time_came[1])
        time_lasts = over_y(time_rests[0]), over_x(time_rests[1])
        mlp_part = (mlp_keep + mlp_came.astype(F32)).astype(BF)
        mlp_came = [hop(piece, "seq", 2) for piece in (mlp_part,)]
    if by_chip:
        space_came, small_grads, mixed, g_tok = tie((space_came, small_grads, mixed, g_tok))
        space_rests = rest_of(space_keep, space_got, 0, space_came[0]), rest_of(space_keep, space_got, 4, space_came[1])
        space_lasts = over_y(space_rests[0]), over_x(space_rests[1])
        time_keep, time_send = seq_halves(jnp.concatenate([
            own_of(time_keep, time_got, 0, time_came[0], time_lasts[0]), own_of(time_keep, time_got, 4, time_came[1], time_lasts[1]),
        ]))
        time_came = hop(time_send, "seq", 1)
        small_came = over_x(small_grads)
        space_lasts, small_came = tie((space_lasts, small_came))
        small_grads = small_grads + small_came
        space_keep, space_send = seq_halves(jnp.concatenate([
            own_of(space_keep, space_got, 0, space_came[0], space_lasts[0]),
            own_of(space_keep, space_got, 4, space_came[1], space_lasts[1]),
        ]))
        space_came = hop(space_send, "seq", 1)
        small_came = over_y(small_grads)
        time_part = (time_keep + time_came.astype(F32)).astype(BF)
        time_came = hop(time_part, "seq", 2)
        space_came, small_came, mlp_came = tie((space_came, small_came, mlp_came))
        small_grads = small_grads + small_came
        small_came = hop(small_grads, "seq", 1)
        mlp_part = (mlp_part.astype(F32) + jnp.concatenate(mlp_came).astype(F32)).astype(BF)
        space_part = (space_keep + space_came.astype(F32)).astype(BF)
        space_came = hop(space_part, "seq", 2)
        mlp_came = hop(mlp_part, "seq", 1)
        space_came, time_came, small_came = tie((space_came, time_came, small_came))
        small_grads = small_grads + small_came
        small_grads = small_grads + hop(small_grads, "seq", 2)
        mlp_total = seq_join(mlp_part, mlp_came)
        grad_in, grad_mout = mlp_total[:own_rows], unpack_rows(mlp_total[own_rows:])
        space_part = (space_part.astype(F32) + space_came.astype(F32)).astype(BF)
        time_part = (time_part.astype(F32) + time_came.astype(F32)).astype(BF)
        attn_totals = [seq_join(part, hop(part, "seq", 1)) for part in (space_part, time_part)]
    else:
        small_grads = lax.psum(small_grads, ("fsdp", "seq"))
        (in_grads,), (out_grads,) = in_grads, out_grads
        in_total, out_total, time_total, space_total = (
            reduce_plain(value) for value in (in_grads, out_grads, time_grads[0], space_grads[0])
        )
        grad_in, grad_mout = seq_total(in_total), seq_total(out_total)
        attn_totals = [seq_total(space_total), seq_total(time_total)]
    grad_qkv = jnp.stack([value[:, : 3 * D] for value in attn_totals])
    grad_out = jnp.stack([value[:, 3 * D :] for value in attn_totals])

    logit_max = jnp.max(small_grads[24:].reshape(devices, 2, H), axis=0)

    def share(rows, width):
        return lax.dynamic_slice_in_dim(rows.reshape(-1, shards * width), me * width, width, axis=1)

    pick = lambda *rows: jnp.concatenate([small_grads[row : row + 1] for row in rows])
    vector_grads = share(pick(16, 8, 0, 17, 9, 1, 18, 10, 2), own_rows)
    grad_gain, grad_shift, grad_outb, grad_moutb = vector_grads[0:3], vector_grads[3:6], vector_grads[6:8], vector_grads[8]
    grad_qv = share(pick(19, 20, 11, 12), 2 * own_rows)
    grad_inb = share(small_grads[3:7], ff // shards)[0]

    factor = threshold / jnp.maximum(logit_max, threshold)
    column_scale = jnp.repeat(jnp.sqrt(factor), HD, axis=1)
    clipped = attn_qkv[:, :, : 2 * D].astype(F32) * jnp.concatenate([column_scale, column_scale], axis=1)[:, None, :]
    mixed = jnp.swapaxes(by_distance(jnp.stack(mixed), place), 0, 1).reshape(tokens.shape)
    return (
        mixed, g_tok.reshape(tokens.shape), grad_gain, grad_shift, grad_qkv, grad_qv, grad_out, grad_outb,
        grad_in, grad_inb, grad_mout, grad_moutb, logit_max, clipped,
    )


def solution(mesh):
    placed = (
        P("fsdp", "seq", None), P(None, "fsdp"), P(None, "fsdp"), P(None, "fsdp", None), P(None, "fsdp"),
        P(None, "fsdp", None), P(None, "fsdp"), P("fsdp", None), P("fsdp"), P("fsdp", None), P("fsdp"), P(),
        P("fsdp", "seq", None),
    )
    return jax.shard_map(
        on_device,
        mesh=mesh,
        in_specs=placed,
        out_specs=(
            P("fsdp", "seq", None), P("fsdp", "seq", None), P(None, "fsdp"), P(None, "fsdp"), P(None, "fsdp", None),
            P(None, "fsdp"), P(None, "fsdp", None), P(None, "fsdp"), P("fsdp", None), P("fsdp"), P("fsdp", None),
            P("fsdp"), P(), P(None, "fsdp", None),
        ),
        check_vma=False,
    )
```
